32 devices in a mesh: dp: 8 (over y, x, core), fsdp: 4 (over z).
Axes of the slice: x: 2, y: 2, z: 4, core: 2. Of those that a mesh axis runs over, the one named last changes fastest.
Arguments:
- tokens: bfloat16 [16384, 768], P(('dp', 'fsdp')), may hold values from -6 to 6
- cotangent: float32 [16384, 768], P(('dp', 'fsdp')), may hold values from -6 to 6
- row_counts: int32 [32], P(('dp', 'fsdp')), may hold values from 128 to 512, as said below
- bucket_flags: int32 [32], P(('dp', 'fsdp')), may hold values from 0 to 1
- owner_slots: int32 [32], replicated, may hold values from 0 to 63, as said below
- master: float32 [64, 768, 768], P('dp', 'fsdp'), may hold values from -0.21875 to 0.21875
- first_moment: float32 [64, 768, 768], P('dp', 'fsdp'), may hold values from -320 to 320
- second_moment: float32 [64, 768, 768], P('dp', 'fsdp'), may hold values from 2621.44 to 10485.76
- gains: float32 [4, 768], replicated, may hold values from 0.5 to 1.5
- gain_first: float32 [4, 768], replicated, may hold values from -1024 to 1024
- gain_second: float32 [4, 768], replicated, may hold values from 32768 to 131072
Outputs:
- activations: bfloat16 [16384, 768], P(('dp', 'fsdp'))
- grad_input: float32 [16384, 768], P(('dp', 'fsdp'))
- new_first: float32 [64, 768, 768], P('dp', 'fsdp')
- new_second: float32 [64, 768, 768], P('dp', 'fsdp')
- new_master: float32 [64, 768, 768], P('dp', 'fsdp')
- gain_first_new: float32 [4, 768], replicated
- gain_second_new: float32 [4, 768], replicated
- gain_new: float32 [4, 768], replicated
The draws below stay inside these ranges and needn't reach their ends.
Inputs may be any that keep to these rules, and one draw needn't show every extreme that they name: `row_counts`: some device has all 512 rows live in every draw. `owner_slots`: the slots are distinct; one owner has all of its 8 slots taken in every draw.
All inputs are finite; a program needn't handle non-finite values.
Results may differ from the reference program's by a relative error of at most 0.02.
Values may be sent and summed in bfloat16 or wider, within the bound.
A program may use at most 384 MiB of HBM per device.

```python
import math
import jax
import jax.numpy as jnp
from jax import lax

D = 768
TOK_DEV = 512
LAYERS = 2
STEP = 5
SHORT = 128
BLOCKS = 32
GAINS = 4
CAP = 8
SHARDS = 32
TOKENS = 16384
N_DP = 8
N_FSDP = 4


def draw_row_counts(key, part):
    key = jax.random.fold_in(key, 11)
    key_counts, key_full = jax.random.split(key)
    counts = jax.random.randint(key_counts, (SHARDS,), TOK_DEV // 4, TOK_DEV + 1)
    full_at = jax.random.randint(key_full, (), 0, SHARDS)
    return jnp.where(jnp.arange(SHARDS) == full_at, TOK_DEV, counts).astype(jnp.int32)


def draw_owner_slots(key, part):
    key = jax.random.fold_in(key, 23)
    key_owner, key_others, key_blocks = jax.random.split(key, 3)
    full_owner = jax.random.randint(key_owner, (), 0, N_DP)
    others = jax.random.permutation(key_others, N_DP * CAP - CAP)
    others = jnp.where(others >= full_owner * CAP, others + CAP, others)
    chosen = jnp.concatenate([full_owner * CAP + jnp.arange(CAP), others[:BLOCKS - CAP]])
    ordering = jax.random.permutation(key_blocks, BLOCKS)
    return chosen[ordering].astype(jnp.int32)


def set_ends(values, key, least, high):
    longest = values.shape.index(max(values.shape))
    spots = []
    for shift in (0, 1):
        where = [jax.random.randint(jax.random.fold_in(key, axis), (), 0, length) for axis, length in enumerate(values.shape)]
        where[longest] = (where[longest] + shift) % values.shape[longest]
        spots.append(tuple(where))
    return values.at[spots[0]].set(least).at[spots[1]].set(high)


def shard_levels(own_key, dims, shards, smallest, top_value):
    gain, own = 1.0, jax.random.fold_in(own_key, 6)
    for dim, parts in shards:
        steps = jnp.exp(jax.random.uniform(jax.random.fold_in(own, dim), (parts,), jnp.float32, smallest / len(shards), top_value / len(shards)))
        gain = gain * jnp.repeat(steps, dims[dim] // parts).reshape([-1 if axis == dim else 1 for axis in range(len(dims))])
    return gain


def scatter_about(key, dims, spread, bound, cuts=(), kind=jnp.bfloat16):
    array = spread * jax.random.normal(key, dims, jnp.float32)
    if cuts:
        array = array * shard_levels(key, dims, cuts, -0.22, 0.18)
    return jnp.clip(array, -bound, bound).astype(kind)


def setup_inputs(seed: int = 0) -> dict:
    streams_of = jax.random.split(jax.random.key(seed), 12)
    return {
        "tokens": scatter_about(streams_of[0], (TOKENS, D), 1.0, 6.0, ((0, 32),)),
        "cotangent": scatter_about(streams_of[1], (TOKENS, D), 1.0, 6.0, ((0, 32),), jnp.float32),
        "row_counts": draw_row_counts(jax.random.fold_in(streams_of[11], 71), 0),
        "bucket_flags": set_ends(jax.random.randint(streams_of[3], (SHARDS,), 0, 2), jax.random.fold_in(streams_of[3], 1), 0, 1).astype(jnp.int32),
        "owner_slots": draw_owner_slots(jax.random.fold_in(streams_of[11], 71), 0),
        "master": scatter_about(streams_of[5], (N_DP * CAP, D, D), D ** -0.5, 0.21875, ((0, 8), (1, 4)), jnp.float32),
        "first_moment": scatter_about(streams_of[6], (N_DP * CAP, D, D), (0.4 * (TOK_DEV * N_DP * N_FSDP) ** 0.5), 320.0, ((0, 8), (1, 4)), jnp.float32),
        "second_moment": jnp.clip(jnp.exp(math.log(10485.76) - 1.3862944 * jax.random.uniform(streams_of[7], (N_DP * CAP, D, D), jnp.float32) ** shard_levels(streams_of[7], (N_DP * CAP, D, D), ((0, 8), (1, 4)), -0.2, 0.2)), 2621.44, 10485.76),
        "gains": jnp.clip(1.0 + 0.1 * jax.random.normal(streams_of[8], (GAINS, D), jnp.float32), 0.5, 1.5),
        "gain_first": scatter_about(streams_of[9], (GAINS, D), (1.5 * (TOK_DEV * N_DP * N_FSDP) ** 0.5), 1024.0, (), jnp.float32),
        "gain_second": jnp.clip(jnp.exp(jax.random.uniform(streams_of[10], (GAINS, D), jnp.float32, math.log(32768.0), math.log(131072.0))), 32768.0, 131072.0),
    }


@jax.custom_vjp
def low(v):
    return lax.optimization_barrier(v.astype(jnp.bfloat16)).astype(jnp.float32)

@jax.custom_vjp
def low_back(v):
    return v

def low_keep(v):
    return (low(v), None)

def low_pass(kept, grad):
    return (grad,)

def back_keep(v):
    return (v, None)

def back_low(kept, grad):
    return (low(grad),)
low.defvjp(low_keep, low_pass)
low_back.defvjp(back_keep, back_low)
highest = lax.Precision.HIGHEST
norm_eps = 1e-05
adam_eps = 1e-08

def normalize(inputs):
    centred = inputs - lax.optimization_barrier(jnp.mean(inputs, -1, keepdims=True))
    return centred * lax.rsqrt(lax.optimization_barrier(jnp.mean(centred * centred, -1, keepdims=True)) + norm_eps)

def causal_conv(filter_in, value_in, length):
    period = 2 * length
    filt_spec = jnp.fft.rfft(filter_in, n=period, axis=2)
    val_spec = jnp.fft.rfft(value_in, n=period, axis=2)
    return jnp.fft.irfft(filt_spec * val_spec, n=period, axis=2)[:, :, :length]

def forward(inputs, master, gains, owner_slots, valid, span_scale, long_mask):
    blocks = low(master[owner_slots])
    current = inputs
    for layer_idx in range(LAYERS):
        weights = blocks[16 * layer_idx:16 * layer_idx + 16]
        first_in = low(normalize(current) * gains[2 * layer_idx])
        projected = low_back(jnp.einsum('td,jde->jte', first_in, weights[0:3], precision=highest))
        values = projected[0] * valid
        gates_q = projected[1]
        key_rows = projected[2] * valid
        live_total = jnp.sum(valid)
        filter_norm = jnp.sqrt(lax.optimization_barrier(jnp.sum(key_rows * key_rows, 0)) / live_total + norm_eps)
        filter_rows = key_rows / filter_norm * span_scale
        filt_dev = filter_rows.reshape(SHARDS, TOK_DEV, D)
        val_dev = values.reshape(SHARDS, TOK_DEV, D)
        long_out = causal_conv(filt_dev[:, None], val_dev[:, None], TOK_DEV).reshape(SHARDS, TOK_DEV, D)
        short_out = causal_conv(filt_dev.reshape(SHARDS, 4, SHORT, D), val_dev.reshape(SHARDS, 4, SHORT, D), SHORT).reshape(SHARDS, TOK_DEV, D)
        conv_out = jnp.where(long_mask[:, None, None], long_out, short_out).reshape(TOKENS, D)
        mixed = low(conv_out * gates_q)
        current = current + low_back(jnp.dot(mixed, weights[3], precision=highest))
        second_in = low(normalize(current) * gains[2 * layer_idx + 1])
        gate_up = low_back(jnp.einsum('td,jde->jte', second_in, weights[4:12], precision=highest))
        hidden = low(jax.nn.silu(gate_up[:4]) * gate_up[4:])
        current = current + low_back(jnp.einsum('jte,jef->tf', hidden, weights[12:16], precision=highest))
    return current

def adam_step(grad_in, first_in, second_in, weight_in, rate, decay):
    first_out = 0.5 * first_in + 0.5 * grad_in
    second_out = 0.5 * second_in + 0.5 * grad_in * grad_in
    corr_one = 1.0 - 0.5 ** STEP
    corr_two = 1.0 - 0.5 ** STEP
    weight_out = weight_in - rate * (first_out / corr_one / (jnp.sqrt(second_out / corr_two) + adam_eps) + decay * weight_in)
    return (first_out, second_out, weight_out)

def reference(tokens, cotangent, row_counts, bucket_flags, owner_slots, master, first_moment, second_moment, gains, gain_first, gain_second):
    row_ids = jnp.arange(TOK_DEV, dtype=jnp.int32)
    valid = (row_ids[None, :] < row_counts[:, None]).astype(jnp.float32).reshape(TOKENS, 1)
    long_mask = bucket_flags == 1
    span_len = jnp.where(long_mask, jnp.float32(TOK_DEV), jnp.float32(SHORT))
    span_scale = jnp.repeat(lax.rsqrt(span_len), TOK_DEV)[:, None]

    def apply(inputs, weights_in, gains_in):
        return forward(inputs, weights_in, gains_in, owner_slots, valid, span_scale, long_mask)
    result, pullback = jax.vjp(apply, tokens.astype(jnp.float32), master, gains)
    grad_tokens, grad_master, grad_gains = pullback(cotangent * valid)
    slot_used = jnp.zeros((N_DP * CAP,), jnp.float32).at[owner_slots].set(1.0)[:, None, None] > 0.5
    first_out, second_out, weight_out = adam_step(grad_master, first_moment, second_moment, master, 0.03, 0.01)
    first_out = jnp.where(slot_used, first_out, first_moment)
    second_out = jnp.where(slot_used, second_out, second_moment)
    weight_out = jnp.where(slot_used, weight_out, master)
    gain_m, gain_v, gain_w = adam_step(grad_gains, gain_first, gain_second, gains, 0.2, 0.0)
    return (result.astype(jnp.bfloat16), grad_tokens, first_out, second_out, weight_out, gain_m, gain_v, gain_w)
```

```python
import functools
import math

import jax
import jax.numpy as jnp
import numpy as np
from jax import lax
from jax.experimental import pallas as pl
from jax.experimental.pallas import tpu as pltpu
from jax.sharding import PartitionSpec as P

STEP = 5
NORM_EPS = 1e-05
ADAM_EPS = 1e-08
LOW = jnp.bfloat16
F32 = jnp.float32
MESH = pl.DeviceIdType.MESH
VMEM_BYTES = 60 * 2**20


def span_tables(length):
    period = 2 * length
    freqs = np.arange(length)[:, None]
    places = np.arange(length)[None, :]
    angle = (freqs * places % period) * (2.0 * math.pi / period)
    cosine, sine = np.cos(angle), -np.sin(angle)
    sine[0] = np.cos(math.pi * np.arange(length))
    weight = np.where(np.arange(length) == 0, 1.0, 2.0)[None, :] / period
    return (cosine, sine, cosine.T * weight, sine.T * weight)


def transform_tables(rows):
    short = [np.kron(np.eye(4), table) for table in span_tables(rows // 4)]
    full = span_tables(rows)
    forward = np.stack([np.concatenate(t[:2], 0) for t in (short, full)])
    inverse = np.stack([np.concatenate(t[2:], 1) for t in (short, full)])
    return (jnp.asarray(forward, LOW), jnp.asarray(inverse, LOW))


class Place:
    def __init__(self, n_dp, n_fsdp):
        self.n_dp, self.depth = n_dp, n_fsdp
        self.up, self.across = 2, n_dp // 4
        self.d = lax.axis_index("dp")
        self.z = lax.axis_index("fsdp")
        self.core = lax.rem(self.d, 2)
        self.x = lax.rem(self.d // 2, self.across)
        self.y = self.d // (2 * self.across)

    def x_at(self, k):
        return lax.rem(self.x + k + self.across, self.across)

    def y_at(self, m):
        return lax.rem(self.y + m + self.up, self.up)

    def z_at(self, k):
        return lax.rem(self.z + k + self.depth, self.depth)

    def dp(self, y=None, x=None, core=None):
        y = self.y if y is None else y
        x = self.x if x is None else x
        core = self.core if core is None else core
        return (y * self.across + x) * 2 + core

    def greet(self):
        barrier = pltpu.get_barrier_semaphore()
        peers = [(self.dp(core=1 - self.core), self.z)]
        peers += [(self.dp(x=self.x_at(k)), self.z) for k in range(1, self.across)]
        peers += [(self.dp(y=self.y_at(m)), self.z) for m in range(1, self.up)]
        peers += [(self.d, self.z_at(k)) for k in range(1, self.depth)]
        for peer in peers:
            pl.semaphore_signal(barrier, inc=1, device_id=peer, device_id_type=MESH)
        pl.semaphore_wait(barrier, len(peers))


class Copies:
    def __init__(self, send, recv, local):
        self.send, self.recv, self.local = send, recv, local
        self.sent, self.moved = 0, 0

    def to(self, source, target, dp, z):
        index = self.sent
        self.sent += 1
        return pltpu.make_async_remote_copy(
            src_ref=source,
            dst_ref=target,
            send_sem=self.send.at[index],
            recv_sem=self.recv.at[index],
            device_id=(dp, z),
            device_id_type=MESH,
        )

    def here(self, source, target):
        index = self.moved
        self.moved += 1
        return pltpu.make_async_copy(source, target, self.local.at[index])


def add_into(total, terms, rows):
    step = 48 if rows % 48 == 0 else 16

    def piece(i, carry):
        at = pl.ds(pl.multiple_of(i * step, 16), step)
        value = total[at, :].astype(F32)
        for term in terms:
            value = value + term[at, :].astype(F32)
        total[at, :] = value.astype(LOW)
        return carry

    lax.fori_loop(0, rows // step, piece, 0)


class PlaneSum:
    def __init__(self, place, copies, s, acc, from_x, from_y, last_y, last_x):
        self.place, self.copies, self.s, self.acc = place, copies, s, acc
        self.from_x, self.from_y, self.last_y, self.last_x = from_x, from_y, last_y, last_x
        self.rows, cols = acc.shape[-2:]
        self.half = cols // 2
        self.first, self.second = pl.ds(0, self.half), pl.ds(self.half, self.half)

    def start(self):
        p, s = self.place, self.s
        self.one = []
        for k in range(1, p.across):
            source = self.acc.at[s, :, p.x_at(k), :, self.first]
            self.one.append(
                self.copies.to(source, self.from_x.at[s, k - 1], p.dp(x=p.x_at(k)), p.z)
            )
        for m in range(1, p.up):
            source = self.acc.at[s, p.y_at(m), :, :, self.second]
            self.one.append(
                self.copies.to(source, self.from_y.at[s, m - 1], p.dp(y=p.y_at(m)), p.z)
            )
        for copy in self.one:
            copy.start()

    def turn(self):
        p, s = self.place, self.s
        for copy in self.one:
            copy.wait_recv()
        for y in range(p.up):
            terms = [self.from_x.at[s, k - 1, y] for k in range(1, p.across)]
            add_into(self.acc.at[s, y, p.x, :, self.first], terms, self.rows)
        for x in range(p.across):
            terms = [self.from_y.at[s, m - 1, x] for m in range(1, p.up)]
            add_into(self.acc.at[s, p.y, x, :, self.second], terms, self.rows)
        self.two = []
        for m in range(1, p.up):
            source = self.acc.at[s, p.y_at(m), p.x, :, self.first]
            self.two.append(
                self.copies.to(source, self.last_y.at[s, m - 1], p.dp(y=p.y_at(m)), p.z)
            )
        for k in range(1, p.across):
            source = self.acc.at[s, p.y, p.x_at(k), :, self.second]
            self.two.append(
                self.copies.to(source, self.last_x.at[s, k - 1], p.dp(x=p.x_at(k)), p.z)
            )
        for copy in self.two:
            copy.start()

    def finish(self):
        p, s = self.place, self.s
        for copy in self.two:
            copy.wait_recv()
        terms = [self.last_y.at[s, m - 1] for m in range(1, p.up)]
        add_into(self.acc.at[s, p.y, p.x, :, self.first], terms, self.rows)
        terms = [self.last_x.at[s, k - 1] for k in range(1, p.across)]
        add_into(self.acc.at[s, p.y, p.x, :, self.second], terms, self.rows)

    def drain(self):
        for copy in self.one + self.two:
            copy.wait_send()


class PlaneSpread:
    def __init__(self, place, copies, base, array, halves):
        self.place, self.copies, self.base, self.array = place, copies, base, array
        self.halves = halves
        self.sends, self.arrive = [], []

    def block(self, **where):
        return self.array.at[self.base + self.place.dp(**where)]

    def fire(self, ref, dp):
        copy = self.copies.to(ref, ref, dp, self.place.z)
        copy.start()
        self.sends.append(copy)
        return copy

    def hand_over(self, **where):
        p = self.place
        self.arrive.append(self.fire(self.block(**where), p.dp(core=1 - p.core)))

    def start(self):
        p = self.place
        own = self.block()
        self.by_x = [self.fire(own, p.dp(x=p.x_at(k))) for k in range(1, p.across)]
        self.by_y = [self.fire(own, p.dp(y=p.y_at(m))) for m in range(1, p.up)]
        self.hand_over()

    def forward(self):
        p = self.place
        self.first, self.second = {}, {}
        for k in range(1, p.across):
            self.by_x[k - 1].wait_recv()
            block = self.block(x=p.x_at(-k)).at[self.halves[0]]
            for m in range(1, p.up):
                self.first[m, k] = self.fire(block, p.dp(y=p.y_at(m)))
        for m in range(1, p.up):
            self.by_y[m - 1].wait_recv()
            block = self.block(y=p.y_at(-m)).at[self.halves[1]]
            for k in range(1, p.across):
                self.second[m, k] = self.fire(block, p.dp(x=p.x_at(k)))
        for k in range(1, p.across):
            self.hand_over(x=p.x_at(-k))
        for m in range(1, p.up):
            self.hand_over(y=p.y_at(-m))

    def finish(self):
        p = self.place
        for m in range(1, p.up):
            for k in range(1, p.across):
                self.first[m, k].wait_recv()
                self.second[m, k].wait_recv()
                self.hand_over(y=p.y_at(-m), x=p.x_at(-k))

    def drain(self):
        for copy in self.arrive:
            copy.wait_recv()
        for copy in self.sends:
            copy.wait_send()


def plane_sum_shapes(n_dp, stages, rows, cols):
    up, across, half = 2, n_dp // 4, cols // 2
    return [
        pltpu.VMEM((stages, up, across, rows, cols), LOW),
        pltpu.VMEM((stages, max(1, across - 1), up, rows, half), LOW),
        pltpu.VMEM((stages, up - 1, across, rows, half), LOW),
        pltpu.VMEM((stages, up - 1, rows, half), LOW),
        pltpu.VMEM((stages, max(1, across - 1), rows, half), LOW),
    ]


def run_stages(stages, steps):
    for t in range(stages + len(steps) - 1):
        for i, step in enumerate(steps):
            if 0 <= t - i < stages:
                step(t - i)


def gather_kernel(
    n_dp, n_fsdp, slots_ref, master_ref, out_ref, held, acc, from_x, from_y, last_y, last_x, send, recv, local
):
    place = Place(n_dp, n_fsdp)
    copies = Copies(send, recv, local)
    slot_cap, rows, cols = master_ref.shape
    stages = acc.shape[0]
    place.greet()
    piece_rows = 48 if rows % 48 == 0 else 16

    def masked(s, y, x, core, at):
        slot = slots_ref[n_dp * s + place.dp(y, x, core)]
        low = slot - place.d * slot_cap
        mine = (low >= 0) & (low < slot_cap)
        index = jnp.clip(low, 0, slot_cap - 1)
        return jnp.where(mine, master_ref[index, at, :], 0.0).astype(LOW)

    def each_piece(s, body):
        pieces = rows // piece_rows

        def one(i, carry):
            spot, piece = i // pieces, lax.rem(i, pieces)
            y, x = spot // place.across, lax.rem(spot, place.across)
            body(y, x, pl.ds(pl.multiple_of(piece * piece_rows, 16), piece_rows))
            return carry

        lax.fori_loop(0, place.up * place.across * pieces, one, 0)

    across_core = []
    for s in range(stages):

        def fill(y, x, at, s=s):
            held[s, y, x, at, :] = masked(s, y, x, 1 - place.core, at)

        each_piece(s, fill)
        copy = copies.to(held.at[s], acc.at[s], place.dp(core=1 - place.core), place.z)
        copy.start()
        across_core.append(copy)

    sums = [PlaneSum(place, copies, s, acc, from_x, from_y, last_y, last_x) for s in range(stages)]
    half = cols // 2
    halves = (pl.ds(0, half), pl.ds(half, half))
    spreads = [PlaneSpread(place, copies, n_dp * s, out_ref, halves) for s in range(stages)]
    along_z, kept = [None] * stages, [None] * stages

    def enter(s):
        across_core[s].wait_recv()

        def join(y, x, at):
            acc[s, y, x, at, :] = acc[s, y, x, at, :] + masked(s, y, x, place.core, at)

        each_piece(s, join)
        sums[s].start()

    def turn(s):
        sums[s].turn()

    def send_z(s):
        sums[s].finish()
        source = acc.at[s, place.y, place.x]
        target = out_ref.at[n_dp * s + place.d, pl.ds(pl.multiple_of(place.z * rows, 16), rows)]
        kept[s] = copies.here(source, target)
        kept[s].start()
        along_z[s] = [
            copies.to(source, target, place.d, place.z_at(k)) for k in range(1, place.depth)
        ]
        for copy in along_z[s]:
            copy.start()

    def spread(s):
        kept[s].wait()
        for copy in along_z[s]:
            copy.wait_recv()
        spreads[s].start()

    run_stages(
        stages,
        [
            enter,
            turn,
            send_z,
            spread,
            lambda s: spreads[s].forward(),
            lambda s: spreads[s].finish(),
        ],
    )
    for s in range(stages):
        across_core[s].wait_send()
        sums[s].drain()
        for copy in along_z[s]:
            copy.wait_send()
        spreads[s].drain()


def copy_count(n_dp, n_fsdp, stages, blocks_in):
    up, across = 2, n_dp // 4
    near = up - 1 + across - 1
    diagonal = (up - 1) * (across - 1)
    return stages * (blocks_in + 2 * near + n_fsdp - 1 + near + 2 * diagonal + up * across)


def gather_blocks(n_dp, n_fsdp, owner_slots, master):
    blocks = owner_slots.shape[0]
    rows, cols = master.shape[1:]
    stages = blocks // n_dp
    count = copy_count(n_dp, n_fsdp, stages, 1)
    return pl.pallas_call(
        functools.partial(gather_kernel, n_dp, n_fsdp),
        name="gather_blocks",
        out_shape=jax.ShapeDtypeStruct((blocks, rows * n_fsdp, cols), LOW),
        in_specs=[
            pl.BlockSpec(memory_space=pltpu.SMEM),
            pl.BlockSpec(memory_space=pltpu.VMEM),
        ],
        out_specs=pl.BlockSpec(memory_space=pl.ANY),
        scratch_shapes=[pltpu.VMEM((stages, 2, n_dp // 4, rows, cols), LOW)]
        + plane_sum_shapes(n_dp, stages, rows, cols)
        + [
            pltpu.SemaphoreType.DMA((count,)),
            pltpu.SemaphoreType.DMA((count,)),
            pltpu.SemaphoreType.DMA((stages,)),
        ],
        compiler_params=pltpu.CompilerParams(
            collective_id=0, has_side_effects=True, vmem_limit_bytes=VMEM_BYTES
        ),
    )(owner_slots, master)


def scatter_kernel(n_dp, n_fsdp, n_arrays, *refs):
    grads, out_ref = refs[:n_arrays], refs[n_arrays]
    own, acc, from_x, from_y, last_y, last_x, from_z, send, recv, local = refs[n_arrays + 1 :]
    place = Place(n_dp, n_fsdp)
    copies = Copies(send, recv, local)
    stages = acc.shape[0]
    size = acc.shape[-2]
    rows = size // n_fsdp
    spots = place.up * place.across
    place.greet()

    def grad(s, spot, core):
        first = n_dp * s + 2 * spot
        return grads[first // 4].at[first % 4 + core]

    order = list(reversed(range(stages)))
    across_core = [None] * stages
    for s in order:
        across_core[s] = [
            copies.to(
                grad(s, spot, 1 - place.core),
                acc.at[s, spot // place.across, spot % place.across],
                place.dp(core=1 - place.core),
                place.z,
            )
            for spot in range(spots)
        ]
        for copy in across_core[s]:
            copy.start()

    fetched = [None] * stages

    def fetch(n):
        s = order[n]
        fetched[s] = [
            copies.here(grad(s, spot, place.core), own.at[n % 2, spot]) for spot in range(spots)
        ]
        for copy in fetched[s]:
            copy.start()

    fetch(0)
    sums = [PlaneSum(place, copies, s, acc, from_x, from_y, last_y, last_x) for s in range(stages)]
    half = acc.shape[-1] // 2
    halves = ((slice(None), pl.ds(0, half)), (slice(None), pl.ds(half, half)))
    spreads = [PlaneSpread(place, copies, n_dp * s, out_ref, halves) for s in range(stages)]
    along_z, kept = [None] * stages, [None] * stages

    def enter(n):
        s = order[n]
        if n + 1 < stages:
            fetch(n + 1)
        for spot in range(spots):
            fetched[s][spot].wait()
            across_core[s][spot].wait_recv()
            add_into(
                acc.at[s, spot // place.across, spot % place.across], [own.at[n % 2, spot]], size
            )
        sums[s].start()

    def turn(n):
        sums[order[n]].turn()

    def rows_of(z):
        return pl.ds(pl.multiple_of(z * rows, 16), rows)

    def send_z(n):
        s = order[n]
        sums[s].finish()
        along_z[s] = [
            copies.to(
                acc.at[s, place.y, place.x, rows_of(place.z_at(k)), :],
                from_z.at[s, k - 1],
                place.d,
                place.z_at(k),
            )
            for k in range(1, place.depth)
        ]
        for copy in along_z[s]:
            copy.start()

    def spread(n):
        s = order[n]
        for copy in along_z[s]:
            copy.wait_recv()
        total = acc.at[s, place.y, place.x, rows_of(place.z), :]
        add_into(total, [from_z.at[s, k - 1] for k in range(1, place.depth)], rows)
        kept[s] = copies.here(total, out_ref.at[n_dp * s + place.d])
        kept[s].start()
        kept[s].wait()
        spreads[s].start()

    run_stages(
        stages,
        [
            enter,
            turn,
            send_z,
            spread,
            lambda n: spreads[order[n]].forward(),
            lambda n: spreads[order[n]].finish(),
        ],
    )
    for s in order:
        for copy in across_core[s]:
            copy.wait_send()
        sums[s].drain()
        for copy in along_z[s]:
            copy.wait_send()
        spreads[s].drain()


def scatter_grads(n_dp, n_fsdp, grads):
    size = grads[0].shape[-1]
    blocks = 4 * len(grads)
    rows = size // n_fsdp
    stages = blocks // n_dp
    spots = n_dp // 2
    count = copy_count(n_dp, n_fsdp, stages, spots)
    return pl.pallas_call(
        functools.partial(scatter_kernel, n_dp, n_fsdp, len(grads)),
        name="scatter_grads",
        out_shape=jax.ShapeDtypeStruct((blocks, rows, size), LOW),
        in_specs=[pl.BlockSpec(memory_space=pl.ANY)] * len(grads),
        out_specs=pl.BlockSpec(memory_space=pl.ANY),
        scratch_shapes=[pltpu.VMEM((2, spots, size, size), LOW)]
        + plane_sum_shapes(n_dp, stages, size, size)
        + [
            pltpu.VMEM((stages, n_fsdp - 1, rows, size), LOW),
            pltpu.SemaphoreType.DMA((count,)),
            pltpu.SemaphoreType.DMA((count,)),
            pltpu.SemaphoreType.DMA((stages * (spots + 1),)),
        ],
        compiler_params=pltpu.CompilerParams(
            collective_id=1, has_side_effects=True, vmem_limit_bytes=VMEM_BYTES
        ),
    )(*grads)


def sum_kernel(n_dp, n_fsdp, part_ref, out_ref, by_z, by_d, mid, send, recv):
    d, z = lax.axis_index("dp"), lax.axis_index("fsdp")
    barrier = pltpu.get_barrier_semaphore()
    along = [(d, lax.rem(z + k, n_fsdp)) for k in range(1, n_fsdp)]
    about = [(lax.rem(d + k, n_dp), z) for k in range(1, n_dp)]
    for peer in along + about:
        pl.semaphore_signal(barrier, inc=1, device_id=peer, device_id_type=MESH)
    pl.semaphore_wait(barrier, len(along) + len(about))

    def exchange(source, slots, index, peers, first):
        sent = [
            pltpu.make_async_remote_copy(
                src_ref=source,
                dst_ref=slots.at[index],
                send_sem=send.at[first + i],
                recv_sem=recv.at[first + i],
                device_id=peer,
                device_id_type=MESH,
            )
            for i, peer in enumerate(peers)
        ]
        for copy in sent:
            copy.start()
        slots[index] = source[...]
        for copy in sent:
            copy.wait_recv()
        total = slots[0]
        for i in range(1, len(peers) + 1):
            total = total + slots[i]
        return (total, sent)

    total, sent_z = exchange(part_ref, by_z, z, along, 0)
    mid[...] = total
    total, sent_d = exchange(mid, by_d, d, about, len(along))
    out_ref[...] = total
    for copy in sent_z + sent_d:
        copy.wait_send()


def sum_rows(n_dp, n_fsdp, part):
    count = n_dp + n_fsdp - 2
    return pl.pallas_call(
        functools.partial(sum_kernel, n_dp, n_fsdp),
        name="sum_rows",
        out_shape=jax.ShapeDtypeStruct(part.shape, F32),
        in_specs=[pl.BlockSpec(memory_space=pltpu.VMEM)],
        out_specs=pl.BlockSpec(memory_space=pltpu.VMEM),
        scratch_shapes=[
            pltpu.VMEM((n_fsdp,) + part.shape, F32),
            pltpu.VMEM((n_dp,) + part.shape, F32),
            pltpu.VMEM(part.shape, F32),
            pltpu.SemaphoreType.DMA((count,)),
            pltpu.SemaphoreType.DMA((count,)),
        ],
        compiler_params=pltpu.CompilerParams(collective_id=2, has_side_effects=True),
    )(part)


def dot(left, right):
    return jnp.dot(left, right, preferred_element_type=F32)


def dot_nt(left, right):
    return lax.dot_general(left, right, (((1,), (1,)), ((), ())), preferred_element_type=F32)


def dot_tn(left, right):
    return lax.dot_general(left, right, (((0,), (0,)), ((), ())), preferred_element_type=F32)


def normalize(inputs):
    centred = inputs - jnp.mean(inputs, -1, keepdims=True)
    rstd = lax.rsqrt(jnp.mean(centred * centred, -1, keepdims=True) + NORM_EPS)
    return (centred * rstd, rstd)


def norm_back(grad, normed, rstd):
    return rstd * (
        grad
        - jnp.mean(grad, -1, keepdims=True)
        - normed * jnp.mean(grad * normed, -1, keepdims=True)
    )


def valid_rows(rows, count):
    return (lax.broadcasted_iota(jnp.int32, (rows, 1), 0) < count).astype(F32)


def lone_rows(rows, flag):
    span = jnp.where(flag == 1, rows, rows // 4)
    return lax.rem(lax.broadcasted_iota(jnp.int32, (rows, 1), 0), span) == 0


def span_scale(rows, flag):
    return jnp.where(flag == 1, rows**-0.5, (rows // 4) ** -0.5).astype(F32)


def filter_norm_of(total_ref):
    live = total_ref[1:2, :]
    return (jnp.sqrt(total_ref[0:1, :] / live + NORM_EPS), live)


def columns(width, body):
    step = 256

    def one(i, carry):
        body(pl.ds(pl.multiple_of(i * step, step), step))
        return carry

    lax.fori_loop(0, width // step, one, 0)


def front_kernel(
    flag, count, state_ref, gain_ref, w_ref, table_ref, back_ref, a_ref, q_ref, k_ref, kh_ref, vh_ref, y_ref, part_ref
):
    rows, width = state_ref.shape
    normed, _ = normalize(state_ref[...].astype(F32))
    a_ref[...] = (normed * gain_ref[...]).astype(LOW)
    valid = valid_rows(rows, count[0])
    lone = lone_rows(rows, flag[0])
    part_ref[...] = jnp.broadcast_to(jnp.sum(valid), part_ref.shape)

    def body(at):
        a = a_ref[...]
        keys = dot(a, w_ref[2, :, at]) * valid
        k_ref[:, at] = keys
        part_ref[0:1, at] = jnp.sum(keys * keys, 0, keepdims=True)
        q_ref[:, at] = dot(a, w_ref[1, :, at])
        values = dot(a, w_ref[0, :, at]) * valid
        kh = dot(table_ref[0], keys.astype(LOW))
        kh_ref[:, at] = kh.astype(LOW)
        vh = dot(table_ref[0], values.astype(LOW))
        vh_ref[:, at] = vh.astype(LOW)
        kr, ki, vr, vi = kh[:rows], kh[rows:], vh[:rows], vh[rows:]
        cross = ki * vi
        real = kr * vr - jnp.where(lone, 0.0, cross)
        imag = jnp.where(lone, cross, kr * vi + ki * vr)
        y_ref[:, at] = dot(back_ref[0, :, :rows], real.astype(LOW)) + dot(
            back_ref[0, :, rows:], imag.astype(LOW)
        )

    columns(width, body)


def whole(shape):
    return pl.BlockSpec(shape, lambda *_: (0,) * len(shape))


def table_specs(tables):
    return [
        pl.BlockSpec((1,) + t.shape[1:], lambda i, flag, count: (flag[0], 0, 0)) for t in tables
    ]


def block_spec(shape, first, each):
    return pl.BlockSpec((each,) + shape[1:], lambda i, *_: (first // each, 0, 0))


def step_spec(shape, first):
    return pl.BlockSpec((1,) + shape[1:], lambda i, *_: (first + i, 0, 0))


def call(kernel, name, grid, scalars, args, specs, outs, out_specs, scratch=()):
    return pl.pallas_call(
        kernel,
        name=name,
        out_shape=outs,
        grid_spec=pltpu.PrefetchScalarGridSpec(
            num_scalar_prefetch=len(scalars),
            grid=(grid,),
            in_specs=specs,
            out_specs=out_specs,
            scratch_shapes=scratch,
        ),
        compiler_params=pltpu.CompilerParams(vmem_limit_bytes=VMEM_BYTES),
    )(*scalars, *args)


def front(scalars, layer, state, gain, weights, tables):
    rows, width = state.shape
    shapes = [
        ((rows, width), LOW),
        ((rows, width), F32),
        ((rows, width), F32),
        ((2 * rows, width), LOW),
        ((2 * rows, width), LOW),
        ((rows, width), F32),
        ((8, width), F32),
    ]
    return call(
        front_kernel,
        f"front_{layer}",
        1,
        scalars,
        (state, gain, weights, *tables),
        [whole(state.shape), whole(gain.shape), block_spec(weights.shape, 16 * layer, 4)]
        + table_specs(tables),
        [jax.ShapeDtypeStruct(*s) for s in shapes],
        [whole(s[0]) for s in shapes],
    )


def mlp_kernel(
    flag, count, state_ref, y_ref, q_ref, total_ref, gain_ref, wo_ref, gate_ref, up_ref, down_ref,
    mixed_ref, mid_ref, b_ref, g_ref, u_ref, hidden_ref, out_ref, sum_ref,
):
    step = pl.program_id(0)
    rows, width = state_ref.shape

    @pl.when(step == 0)
    def _():
        norm, _ = filter_norm_of(total_ref)
        scale = span_scale(rows, flag[0]) / norm
        mixed_ref[...] = (y_ref[...] * scale * q_ref[...]).astype(LOW)
        mid = state_ref[...].astype(F32) + dot(mixed_ref[...], wo_ref[0])
        mid_ref[...] = mid
        sum_ref[...] = mid
        normed, _ = normalize(mid)
        b_ref[...] = (normed * gain_ref[...]).astype(LOW)

    def body(at):
        gate = dot(b_ref[...], gate_ref[0, :, at])
        up = dot(b_ref[...], up_ref[0, :, at])
        g_ref[0, :, at] = gate.astype(LOW)
        u_ref[0, :, at] = up.astype(LOW)
        hidden_ref[0, :, at] = (gate * jax.nn.sigmoid(gate) * up).astype(LOW)

    columns(width, body)
    sum_ref[...] += dot(hidden_ref[0], down_ref[0])

    @pl.when(step == pl.num_programs(0) - 1)
    def _():
        out_ref[...] = sum_ref[...].astype(out_ref.dtype)


def mlp(scalars, layer, state, y, q, total, gain, weights, out_type):
    rows, width = state.shape
    row = (rows, width)
    shapes = [(row, LOW), (row, F32), (row, LOW)] + [((4,) + row, LOW)] * 3 + [(row, out_type)]
    first = 16 * layer
    return call(
        mlp_kernel,
        f"mlp_{layer}",
        4,
        scalars,
        (state, y, q, total, gain, weights, weights, weights, weights),
        [whole(t.shape) for t in (state, y, q, total, gain)]
        + [block_spec(weights.shape, first + 3, 1)]
        + [step_spec(weights.shape, first + i) for i in (4, 8, 12)],
        [jax.ShapeDtypeStruct(*s) for s in shapes],
        [whole(row)] * 3 + [step_spec((4,) + row, 0)] * 3 + [whole(row)],
        [pltpu.VMEM(row, F32)],
    )


def mlp_back_kernel(
    flag, count, grad_ref, mid_ref, gain_ref, b_ref, g_ref, u_ref, hidden_ref, gate_ref, up_ref, down_ref, wo_ref, q_ref, y_ref,
    total_ref, kh_ref, vh_ref, table_ref, back_ref,
    dgate_ref, dup_ref, ddown_ref, dmid_ref, dfilter_ref, dv_ref, dq_ref, part_ref, low_ref, sum_ref,
):
    step = pl.program_id(0)
    rows, width = grad_ref.shape
    valid = valid_rows(rows, count[0])

    @pl.when(step == 0)
    def _():
        low_ref[...] = (grad_ref[...] * valid).astype(LOW)
        sum_ref[...] = jnp.zeros_like(sum_ref)

    def body(at):
        dhidden = dot_nt(low_ref[...], down_ref[0, at, :])
        gate = g_ref[0, :, at].astype(F32)
        up = u_ref[0, :, at].astype(F32)
        sig = jax.nn.sigmoid(gate)
        dup = (dhidden * gate * sig).astype(LOW)
        dgate = (dhidden * up * sig * (1.0 + gate * (1.0 - sig))).astype(LOW)
        ddown_ref[0, at, :] = dot_tn(hidden_ref[0, :, at], low_ref[...]).astype(LOW)
        dgate_ref[0, :, at] = dot_tn(b_ref[...], dgate).astype(LOW)
        dup_ref[0, :, at] = dot_tn(b_ref[...], dup).astype(LOW)
        sum_ref[...] += dot_nt(dgate, gate_ref[0, :, at]) + dot_nt(dup, up_ref[0, :, at])

    columns(width, body)

    @pl.when(step == pl.num_programs(0) - 1)
    def _():
        normed, rstd = normalize(mid_ref[...])
        db = sum_ref[...]
        part_ref[...] = jnp.zeros_like(part_ref)
        part_ref[1:2, :] = jnp.sum(db * normed, 0, keepdims=True)
        dmid = grad_ref[...] * valid + norm_back(db * gain_ref[...], normed, rstd)
        dmid_ref[...] = dmid
        low_ref[...] = dmid.astype(LOW)
        norm, _ = filter_norm_of(total_ref)
        spans = span_scale(rows, flag[0])
        sum_ref[0:1, :] = spans / norm
        lone = lone_rows(rows, flag[0])

        def mix(at):
            scale = sum_ref[0:1, at]
            dmixed = dot_nt(low_ref[...], wo_ref[0, at, :])
            y = y_ref[:, at]
            dq_ref[:, at] = (dmixed * y * scale).astype(LOW)
            dy = dmixed * q_ref[:, at]
            part_ref[0:1, at] = jnp.sum(dy * y, 0, keepdims=True) * spans
            dh = dot(table_ref[0], dy.astype(LOW))
            dr, di = dh[:rows], dh[rows:]

            def against(ref):
                orr, oi = ref[:rows, at].astype(F32), ref[rows:, at].astype(F32)
                cross = di * oi
                real = dr * orr + jnp.where(lone, 0.0, cross)
                imag = jnp.where(lone, cross, di * orr - dr * oi)
                return dot(back_ref[0, :, :rows], real.astype(LOW)) + dot(
                    back_ref[0, :, rows:], imag.astype(LOW)
                )

            dfilter_ref[:, at] = against(vh_ref)
            dv_ref[:, at] = (against(kh_ref) * scale * valid).astype(LOW)

        columns(width, mix)


def mlp_back(scalars, layer, grad, mid, gain, b, g, u, hidden, weights, q, y, total, kh, vh, tables):
    rows, width = grad.shape
    row = (rows, width)
    square = (4, width, width)
    first = 16 * layer
    shapes = [(square, LOW)] * 3 + [(row, F32), (row, F32), (row, LOW), (row, LOW), ((8, width), F32)]
    return call(
        mlp_back_kernel,
        f"mlp_back_{layer}",
        4,
        scalars,
        (grad, mid, gain, b, g, u, hidden, weights, weights, weights, weights, q, y, total, kh, vh, *tables),
        [whole(t.shape) for t in (grad, mid, gain, b)]
        + [step_spec(g.shape, 0)] * 3
        + [step_spec(weights.shape, first + i) for i in (4, 8, 12)]
        + [block_spec(weights.shape, first + 3, 1)]
        + [whole(t.shape) for t in (q, y, total, kh, vh)]
        + table_specs(tables),
        [jax.ShapeDtypeStruct(*s) for s in shapes],
        [step_spec(square, 0)] * 3 + [whole(s[0]) for s in shapes[3:]],
        [pltpu.VMEM(row, LOW), pltpu.VMEM(row, F32)],
    )


def front_back_kernel(
    flag, count, dfilter_ref, k_ref, dv_ref, dq_ref, dmid_ref, a_ref, mixed_ref, w_ref, total_ref, back_total_ref, gain_ref,
    state_ref, dw_ref, dstate_ref, part_ref, dk_ref, sum_ref,
):
    rows, width = dmid_ref.shape
    norm, live = filter_norm_of(total_ref)
    scale = span_scale(rows, flag[0]) / norm
    square = -back_total_ref[0:1, :] / (norm * norm) / (2.0 * norm * live)
    valid = valid_rows(rows, count[0])
    dk_ref[...] = ((dfilter_ref[...] * scale + 2.0 * k_ref[...] * square) * valid).astype(LOW)
    low = dmid_ref[...].astype(LOW)
    sum_ref[...] = (
        dot_nt(dv_ref[...], w_ref[0]) + dot_nt(dq_ref[...], w_ref[1]) + dot_nt(dk_ref[...], w_ref[2])
    )

    def body(at):
        a = a_ref[...]
        dw_ref[0, :, at] = dot_tn(a, dv_ref[:, at]).astype(LOW)
        dw_ref[1, :, at] = dot_tn(a, dq_ref[:, at]).astype(LOW)
        dw_ref[2, :, at] = dot_tn(a, dk_ref[:, at]).astype(LOW)
        dw_ref[3, at, :] = dot_tn(mixed_ref[:, at], low).astype(LOW)

    columns(width, body)
    da = sum_ref[...]
    normed, rstd = normalize(state_ref[...].astype(F32))
    part_ref[...] = jnp.broadcast_to(jnp.sum(da * normed, 0, keepdims=True), part_ref.shape)
    dstate_ref[...] = dmid_ref[...] + norm_back(da * gain_ref[...], normed, rstd)


def front_back(scalars, layer, dfilter, k, dv, dq, dmid, a, mixed, weights, total, back_total, gain, state):
    rows, width = dmid.shape
    row = (rows, width)
    square = (4, width, width)
    shapes = [(square, LOW), (row, F32), ((8, width), F32)]
    args = (dfilter, k, dv, dq, dmid, a, mixed, weights, total, back_total, gain, state)
    specs = [whole(t.shape) for t in args]
    specs[7] = block_spec(weights.shape, 16 * layer, 4)
    return call(
        front_back_kernel,
        f"front_back_{layer}",
        1,
        scalars,
        args,
        specs,
        [jax.ShapeDtypeStruct(*s) for s in shapes],
        [whole(s[0]) for s in shapes],
        [pltpu.VMEM(row, LOW), pltpu.VMEM(row, F32)],
    )


def adam_step(grad, first, second, weight, rate, decay):
    first_out = 0.5 * first + 0.5 * grad
    second_out = 0.5 * second + 0.5 * grad * grad
    corr = 1.0 - 0.5**STEP
    weight_out = weight - rate * (
        first_out / corr / (jnp.sqrt(second_out / corr) + ADAM_EPS) + decay * weight
    )
    return (first_out, second_out, weight_out)


def adam_kernel(
    block, used, grad_ref, master_ref, first_ref, second_ref, first_out, second_out, master_out
):
    taken = used[pl.program_id(0)] == 1
    first, second, master = first_ref[...], second_ref[...], master_ref[...]
    new = adam_step(grad_ref[...].astype(F32), first, second, master, 0.03, 0.01)
    first_out[...] = jnp.where(taken, new[0], first)
    second_out[...] = jnp.where(taken, new[1], second)
    master_out[...] = jnp.where(taken, new[2], master)


def adam_blocks(block, used, grads, master, first, second):
    shape = (1,) + master.shape[1:]
    own = pl.BlockSpec(shape, lambda i, block, used: (i, 0, 0))
    picked = pl.BlockSpec(shape, lambda i, block, used: (block[i], 0, 0))
    return call(
        adam_kernel,
        "adam",
        master.shape[0],
        (block, used),
        (grads, master, first, second),
        [picked, own, own, own],
        [jax.ShapeDtypeStruct(master.shape, F32)] * 3,
        [own] * 3,
    )


def on_device(
    n_dp,
    n_fsdp,
    tokens,
    cotangent,
    row_counts,
    bucket_flags,
    owner_slots,
    master,
    first_moment,
    second_moment,
    gains,
    gain_first,
    gain_second,
):
    rows = tokens.shape[0]
    slot_cap = master.shape[0]
    layers = owner_slots.shape[0] // 16
    tables = transform_tables(rows)
    scalars = (bucket_flags, row_counts)
    weights = gather_blocks(n_dp, n_fsdp, owner_slots, master)
    state = tokens
    kept = []
    for layer in range(layers):
        gain_one, gain_two = gains[2 * layer : 2 * layer + 1], gains[2 * layer + 1 : 2 * layer + 2]
        a, q, k, kh, vh, y, part = front(scalars, layer, state, gain_one, weights, tables)
        total = sum_rows(n_dp, n_fsdp, part)
        mixed, mid, b, g, u, hidden, after = mlp(
            scalars, layer, state, y, q, total, gain_two, weights, LOW if layer == layers - 1 else F32
        )
        kept.append((gain_one, gain_two, state, a, q, k, kh, vh, y, total, mixed, mid, b, g, u, hidden))
        state = after
    activations = state
    grad = cotangent
    gain_rows = [None] * (2 * layers)
    block_grads = [None] * (4 * layers)
    for layer in reversed(range(layers)):
        gain_one, gain_two, state, a, q, k, kh, vh, y, total, mixed, mid, b, g, u, hidden = kept[layer]
        dgate, dup, ddown, dmid, dfilter, dv, dq, part = mlp_back(
            scalars, layer, grad, mid, gain_two, b, g, u, hidden, weights, q, y, total, kh, vh, tables
        )
        gain_rows[2 * layer + 1] = part[1:2]
        back_total = sum_rows(n_dp, n_fsdp, part)
        dw, grad, part = front_back(
            scalars, layer, dfilter, k, dv, dq, dmid, a, mixed, weights, total, back_total, gain_one, state
        )
        gain_rows[2 * layer] = part[0:1]
        block_grads[4 * layer : 4 * layer + 4] = [dw, dgate, dup, ddown]
    summed = scatter_grads(n_dp, n_fsdp, block_grads)
    pad = [jnp.zeros((8 - 2 * layers, gains.shape[1]), F32)]
    gains_total = sum_rows(n_dp, n_fsdp, jnp.concatenate(gain_rows + pad, 0))[: 2 * layers]
    my_slots = lax.axis_index("dp") * slot_cap + jnp.arange(slot_cap, dtype=jnp.int32)
    hits = owner_slots[None, :] == my_slots[:, None]
    used = jnp.any(hits, 1).astype(jnp.int32)
    block = jnp.sum(jnp.where(hits, jnp.arange(owner_slots.shape[0], dtype=jnp.int32)[None, :], 0), 1)
    first_out, second_out, master_out = adam_blocks(
        block, used, summed, master, first_moment, second_moment
    )
    gain_m, gain_v, gain_w = adam_step(gains_total, gain_first, gain_second, gains, 0.2, 0.0)
    return (activations, grad, first_out, second_out, master_out, gain_m, gain_v, gain_w)


def solution(mesh):
    rows = P(("dp", "fsdp"), None)
    blocks = P("dp", "fsdp", None)
    flat = P(("dp", "fsdp"))
    return jax.shard_map(
        functools.partial(on_device, mesh.shape["dp"], mesh.shape["fsdp"]),
        mesh=mesh,
        in_specs=(rows, rows, flat, flat, P(), blocks, blocks, blocks, P(), P(), P()),
        out_specs=(rows, rows, blocks, blocks, blocks, P(), P(), P()),
        check_vma=False,
    )
```

```python
import functools
import math

import jax
import jax.numpy as jnp
import numpy as np
from jax import lax
from jax.experimental import pallas as pl
from jax.experimental.pallas import tpu as pltpu
from jax.sharding import PartitionSpec as P

STEP = 5
NORM_EPS = 1e-05
ADAM_EPS = 1e-08
LOW = jnp.bfloat16
F32 = jnp.float32
MESH = pl.DeviceIdType.MESH
VMEM_BYTES = 60 * 2**20


def span_tables(length):
    period = 2 * length
    freqs = np.arange(length)[:, None]
    places = np.arange(length)[None, :]
    angle = (freqs * places % period) * (2.0 * math.pi / period)
    cosine, sine = np.cos(angle), -np.sin(angle)
    sine[0] = np.cos(math.pi * np.arange(length))
    weight = np.where(np.arange(length) == 0, 1.0, 2.0)[None, :] / period
    return (cosine, sine, cosine.T * weight, sine.T * weight)


def transform_tables(rows):
    short = [np.kron(np.eye(4), table) for table in span_tables(rows // 4)]
    full = span_tables(rows)
    forward = np.stack([np.concatenate(t[:2], 0) for t in (short, full)])
    inverse = np.stack([np.concatenate(t[2:], 1) for t in (short, full)])
    return (jnp.asarray(forward, LOW), jnp.asarray(inverse, LOW))


class Place:
    def __init__(self, n_dp, n_fsdp):
        self.n_dp, self.depth = n_dp, n_fsdp
        self.up, self.across = 2, n_dp // 4
        self.d = lax.axis_index("dp")
        self.z = lax.axis_index("fsdp")
        self.core = lax.rem(self.d, 2)
        self.x = lax.rem(self.d // 2, self.across)
        self.y = self.d // (2 * self.across)

    def x_at(self, k):
        return lax.rem(self.x + k + self.across, self.across)

    def y_at(self, m):
        return lax.rem(self.y + m + self.up, self.up)

    def z_at(self, k):
        return lax.rem(self.z + k + self.depth, self.depth)

    def dp(self, y=None, x=None, core=None):
        y = self.y if y is None else y
        x = self.x if x is None else x
        core = self.core if core is None else core
        return (y * self.across + x) * 2 + core

    def greet(self):
        barrier = pltpu.get_barrier_semaphore()
        peers = [(self.dp(core=1 - self.core), self.z)]
        peers += [(self.dp(x=self.x_at(k)), self.z) for k in range(1, self.across)]
        peers += [(self.dp(y=self.y_at(m)), self.z) for m in range(1, self.up)]
        peers += [(self.d, self.z_at(k)) for k in range(1, self.depth)]
        for peer in peers:
            pl.semaphore_signal(barrier, inc=1, device_id=peer, device_id_type=MESH)
        pl.semaphore_wait(barrier, len(peers))

    def greet_all(self):
        barrier = pltpu.get_barrier_semaphore()
        peers = [(lax.rem(self.d + k, self.n_dp), self.z) for k in range(1, self.n_dp)]
        peers += [(self.d, self.z_at(k)) for k in range(1, self.depth)]
        for peer in peers:
            pl.semaphore_signal(barrier, inc=1, device_id=peer, device_id_type=MESH)
        pl.semaphore_wait(barrier, len(peers))


class Copies:
    def __init__(self, send, recv, local):
        self.send, self.recv, self.local = send, recv, local
        self.sent, self.moved = 0, 0

    def to(self, source, target, dp, z):
        index = self.sent
        self.sent += 1
        return pltpu.make_async_remote_copy(
            src_ref=source,
            dst_ref=target,
            send_sem=self.send.at[index],
            recv_sem=self.recv.at[index],
            device_id=(dp, z),
            device_id_type=MESH,
        )

    def here(self, source, target):
        index = self.moved
        self.moved += 1
        return pltpu.make_async_copy(source, target, self.local.at[index])


def add_into(total, terms, rows):
    step = 48 if rows % 48 == 0 else 16

    def piece(i, carry):
        at = pl.ds(pl.multiple_of(i * step, 16), step)
        value = total[at, :].astype(F32)
        for term in terms:
            value = value + term[at, :].astype(F32)
        total[at, :] = value.astype(LOW)
        return carry

    lax.fori_loop(0, rows // step, piece, 0)


class PlaneSum:
    def __init__(self, place, copies, s, acc, from_x, from_y, last_y, last_x):
        self.place, self.copies, self.s, self.acc = place, copies, s, acc
        self.from_x, self.from_y, self.last_y, self.last_x = from_x, from_y, last_y, last_x
        self.rows, cols = acc.shape[-2:]
        self.half = cols // 2
        self.first, self.second = pl.ds(0, self.half), pl.ds(self.half, self.half)

    def start(self):
        p, s = self.place, self.s
        self.one = []
        for k in range(1, p.across):
            source = self.acc.at[s, :, p.x_at(k), :, self.first]
            self.one.append(
                self.copies.to(source, self.from_x.at[s, k - 1], p.dp(x=p.x_at(k)), p.z)
            )
        for m in range(1, p.up):
            source = self.acc.at[s, p.y_at(m), :, :, self.second]
            self.one.append(
                self.copies.to(source, self.from_y.at[s, m - 1], p.dp(y=p.y_at(m)), p.z)
            )
        for copy in self.one:
            copy.start()

    def turn(self):
        p, s = self.place, self.s
        for copy in self.one:
            copy.wait_recv()
        for y in range(p.up):
            terms = [self.from_x.at[s, k - 1, y] for k in range(1, p.across)]
            add_into(self.acc.at[s, y, p.x, :, self.first], terms, self.rows)
        for x in range(p.across):
            terms = [self.from_y.at[s, m - 1, x] for m in range(1, p.up)]
            add_into(self.acc.at[s, p.y, x, :, self.second], terms, self.rows)
        self.two = []
        for m in range(1, p.up):
            source = self.acc.at[s, p.y_at(m), p.x, :, self.first]
            self.two.append(
                self.copies.to(source, self.last_y.at[s, m - 1], p.dp(y=p.y_at(m)), p.z)
            )
        for k in range(1, p.across):
            source = self.acc.at[s, p.y, p.x_at(k), :, self.second]
            self.two.append(
                self.copies.to(source, self.last_x.at[s, k - 1], p.dp(x=p.x_at(k)), p.z)
            )
        for copy in self.two:
            copy.start()

    def finish(self):
        p, s = self.place, self.s
        for copy in self.two:
            copy.wait_recv()
        terms = [self.last_y.at[s, m - 1] for m in range(1, p.up)]
        add_into(self.acc.at[s, p.y, p.x, :, self.first], terms, self.rows)
        terms = [self.last_x.at[s, k - 1] for k in range(1, p.across)]
        add_into(self.acc.at[s, p.y, p.x, :, self.second], terms, self.rows)

    def drain(self):
        for copy in self.one + self.two:
            copy.wait_send()


class PlaneSpread:
    def __init__(self, place, copies, base, array, halves):
        self.place, self.copies, self.base, self.array = place, copies, base, array
        self.halves = halves
        self.sends, self.arrive = [], []

    def block(self, **where):
        return self.array.at[self.base + self.place.dp(**where)]

    def fire(self, ref, dp):
        copy = self.copies.to(ref, ref, dp, self.place.z)
        copy.start()
        self.sends.append(copy)
        return copy

    def hand_over(self, **where):
        p = self.place
        self.arrive.append(self.fire(self.block(**where), p.dp(core=1 - p.core)))

    def start(self):
        p = self.place
        own = self.block()
        self.by_x = [self.fire(own, p.dp(x=p.x_at(k))) for k in range(1, p.across)]
        self.by_y = [self.fire(own, p.dp(y=p.y_at(m))) for m in range(1, p.up)]
        self.hand_over()

    def forward(self):
        p = self.place
        self.first, self.second = {}, {}
        for k in range(1, p.across):
            self.by_x[k - 1].wait_recv()
            block = self.block(x=p.x_at(-k)).at[self.halves[0]]
            for m in range(1, p.up):
                self.first[m, k] = self.fire(block, p.dp(y=p.y_at(m)))
        for m in range(1, p.up):
            self.by_y[m - 1].wait_recv()
            block = self.block(y=p.y_at(-m)).at[self.halves[1]]
            for k in range(1, p.across):
                self.second[m, k] = self.fire(block, p.dp(x=p.x_at(k)))
        for k in range(1, p.across):
            self.hand_over(x=p.x_at(-k))
        for m in range(1, p.up):
            self.hand_over(y=p.y_at(-m))

    def finish(self):
        p = self.place
        for m in range(1, p.up):
            for k in range(1, p.across):
                self.first[m, k].wait_recv()
                self.second[m, k].wait_recv()
                self.hand_over(y=p.y_at(-m), x=p.x_at(-k))

    def arrived(self):
        for copy in self.arrive:
            copy.wait_recv()

    def drain(self):
        for copy in self.sends:
            copy.wait_send()


def plane_sum_shapes(n_dp, stages, rows, cols):
    up, across, half = 2, n_dp // 4, cols // 2
    return [
        pltpu.VMEM((stages, up, across, rows, cols), LOW),
        pltpu.VMEM((stages, max(1, across - 1), up, rows, half), LOW),
        pltpu.VMEM((stages, up - 1, across, rows, half), LOW),
        pltpu.VMEM((stages, up - 1, rows, half), LOW),
        pltpu.VMEM((stages, max(1, across - 1), rows, half), LOW),
    ]


def run_stages(stages, steps):
    for t in range(stages + len(steps) - 1):
        for i, step in enumerate(steps):
            if 0 <= t - i < stages:
                step(t - i)


def copy_count(n_dp, n_fsdp, stages, blocks_in):
    up, across = 2, n_dp // 4
    near = up - 1 + across - 1
    diagonal = (up - 1) * (across - 1)
    return stages * (blocks_in + 2 * near + n_fsdp - 1 + near + 2 * diagonal + up * across)


def scatter_kernel(n_dp, n_fsdp, n_arrays, *refs):
    grads, out_ref = refs[:n_arrays], refs[n_arrays]
    own, acc, from_x, from_y, last_y, last_x, from_z, send, recv, local = refs[n_arrays + 1 :]
    place = Place(n_dp, n_fsdp)
    copies = Copies(send, recv, local)
    stages = acc.shape[0]
    size = acc.shape[-2]
    rows = size // n_fsdp
    spots = place.up * place.across
    place.greet()

    def grad(s, spot, core):
        first = n_dp * s + 2 * spot
        return grads[first // 4].at[first % 4 + core]

    order = list(reversed(range(stages)))
    across_core = [None] * stages
    for s in order:
        across_core[s] = [
            copies.to(
                grad(s, spot, 1 - place.core),
                acc.at[s, spot // place.across, spot % place.across],
                place.dp(core=1 - place.core),
                place.z,
            )
            for spot in range(spots)
        ]
        for copy in across_core[s]:
            copy.start()

    fetched = [None] * stages

    def fetch(n):
        s = order[n]
        fetched[s] = [
            copies.here(grad(s, spot, place.core), own.at[n % 2, spot]) for spot in range(spots)
        ]
        for copy in fetched[s]:
            copy.start()

    fetch(0)
    sums = [PlaneSum(place, copies, s, acc, from_x, from_y, last_y, last_x) for s in range(stages)]
    half = acc.shape[-1] // 2
    halves = ((slice(None), pl.ds(0, half)), (slice(None), pl.ds(half, half)))
    spreads = [PlaneSpread(place, copies, n_dp * s, out_ref, halves) for s in range(stages)]
    along_z, kept = [None] * stages, [None] * stages

    def enter(n):
        s = order[n]
        if n + 1 < stages:
            fetch(n + 1)
        for spot in range(spots):
            fetched[s][spot].wait()
            across_core[s][spot].wait_recv()
            add_into(
                acc.at[s, spot // place.across, spot % place.across], [own.at[n % 2, spot]], size
            )
        sums[s].start()

    def turn(n):
        sums[order[n]].turn()

    def rows_of(z):
        return pl.ds(pl.multiple_of(z * rows, 16), rows)

    def send_z(n):
        s = order[n]
        sums[s].finish()
        along_z[s] = [
            copies.to(
                acc.at[s, place.y, place.x, rows_of(place.z_at(k)), :],
                from_z.at[s, k - 1],
                place.d,
                place.z_at(k),
            )
            for k in range(1, place.depth)
        ]
        for copy in along_z[s]:
            copy.start()

    def spread(n):
        s = order[n]
        for copy in along_z[s]:
            copy.wait_recv()
        total = acc.at[s, place.y, place.x, rows_of(place.z), :]
        add_into(total, [from_z.at[s, k - 1] for k in range(1, place.depth)], rows)
        kept[s] = copies.here(total, out_ref.at[n_dp * s + place.d])
        kept[s].start()
        kept[s].wait()
        spreads[s].start()

    run_stages(
        stages,
        [
            enter,
            turn,
            send_z,
            spread,
            lambda n: spreads[order[n]].forward(),
            lambda n: spreads[order[n]].finish(),
        ],
    )
    for s in order:
        spreads[s].arrived()
        for copy in across_core[s]:
            copy.wait_send()
        sums[s].drain()
        for copy in along_z[s]:
            copy.wait_send()
        spreads[s].drain()


def scatter_grads(n_dp, n_fsdp, grads):
    size = grads[0].shape[-1]
    blocks = 4 * len(grads)
    rows = size // n_fsdp
    stages = blocks // n_dp
    spots = n_dp // 2
    count = copy_count(n_dp, n_fsdp, stages, spots)
    return pl.pallas_call(
        functools.partial(scatter_kernel, n_dp, n_fsdp, len(grads)),
        name="scatter_grads",
        out_shape=jax.ShapeDtypeStruct((blocks, rows, size), LOW),
        in_specs=[pl.BlockSpec(memory_space=pl.ANY)] * len(grads),
        out_specs=pl.BlockSpec(memory_space=pl.ANY),
        scratch_shapes=[pltpu.VMEM((2, spots, size, size), LOW)]
        + plane_sum_shapes(n_dp, stages, size, size)
        + [
            pltpu.VMEM((stages, n_fsdp - 1, rows, size), LOW),
            pltpu.SemaphoreType.DMA((count,)),
            pltpu.SemaphoreType.DMA((count,)),
            pltpu.SemaphoreType.DMA((stages * (spots + 1),)),
        ],
        compiler_params=pltpu.CompilerParams(
            collective_id=1, has_side_effects=True, vmem_limit_bytes=VMEM_BYTES
        ),
    )(*grads)


def sum_kernel(n_dp, n_fsdp, part_ref, out_ref, by_z, by_d, mid, send, recv):
    d, z = lax.axis_index("dp"), lax.axis_index("fsdp")
    barrier = pltpu.get_barrier_semaphore()
    along = [(d, lax.rem(z + k, n_fsdp)) for k in range(1, n_fsdp)]
    about = [(lax.rem(d + k, n_dp), z) for k in range(1, n_dp)]
    for peer in along + about:
        pl.semaphore_signal(barrier, inc=1, device_id=peer, device_id_type=MESH)
    pl.semaphore_wait(barrier, len(along) + len(about))

    def exchange(source, slots, index, peers, first):
        sent = [
            pltpu.make_async_remote_copy(
                src_ref=source,
                dst_ref=slots.at[index],
                send_sem=send.at[first + i],
                recv_sem=recv.at[first + i],
                device_id=peer,
                device_id_type=MESH,
            )
            for i, peer in enumerate(peers)
        ]
        for copy in sent:
            copy.start()
        slots[index] = source[...]
        for copy in sent:
            copy.wait_recv()
        total = slots[0]
        for i in range(1, len(peers) + 1):
            total = total + slots[i]
        return (total, sent)

    total, sent_z = exchange(part_ref, by_z, z, along, 0)
    mid[...] = total
    total, sent_d = exchange(mid, by_d, d, about, len(along))
    out_ref[...] = total
    for copy in sent_z + sent_d:
        copy.wait_send()


def sum_rows(n_dp, n_fsdp, part):
    count = n_dp + n_fsdp - 2
    return pl.pallas_call(
        functools.partial(sum_kernel, n_dp, n_fsdp),
        name="sum_rows",
        out_shape=jax.ShapeDtypeStruct(part.shape, F32),
        in_specs=[pl.BlockSpec(memory_space=pltpu.VMEM)],
        out_specs=pl.BlockSpec(memory_space=pltpu.VMEM),
        scratch_shapes=[
            pltpu.VMEM((n_fsdp,) + part.shape, F32),
            pltpu.VMEM((n_dp,) + part.shape, F32),
            pltpu.VMEM(part.shape, F32),
            pltpu.SemaphoreType.DMA((count,)),
            pltpu.SemaphoreType.DMA((count,)),
        ],
        compiler_params=pltpu.CompilerParams(collective_id=2, has_side_effects=True),
    )(part)


def dot(left, right):
    return jnp.dot(left, right, preferred_element_type=F32)


def dot_nt(left, right):
    return lax.dot_general(left, right, (((1,), (1,)), ((), ())), preferred_element_type=F32)


def dot_tn(left, right):
    return lax.dot_general(left, right, (((0,), (0,)), ((), ())), preferred_element_type=F32)


def normalize(inputs):
    centred = inputs - jnp.mean(inputs, -1, keepdims=True)
    rstd = lax.rsqrt(jnp.mean(centred * centred, -1, keepdims=True) + NORM_EPS)
    return (centred * rstd, rstd)


def norm_back(grad, normed, rstd):
    return rstd * (
        grad
        - jnp.mean(grad, -1, keepdims=True)
        - normed * jnp.mean(grad * normed, -1, keepdims=True)
    )


def valid_rows(rows, count):
    return (lax.broadcasted_iota(jnp.int32, (rows, 1), 0) < count).astype(F32)


def lone_rows(rows, flag):
    span = jnp.where(flag == 1, rows, rows // 4)
    return lax.rem(lax.broadcasted_iota(jnp.int32, (rows, 1), 0), span) == 0


def span_scale(rows, flag):
    return jnp.where(flag == 1, rows**-0.5, (rows // 4) ** -0.5).astype(F32)


def filter_norm_of(total_ref):
    live = total_ref[1:2, :]
    return (jnp.sqrt(total_ref[0:1, :] / live + NORM_EPS), live)


def columns(width, body):
    for at in range(0, width, 256):
        body(pl.ds(at, 256))


def front_kernel(
    flag, count, state_ref, gain_ref, w_ref, table_ref, back_ref, a_ref, q_ref, k_ref, kh_ref, vh_ref, y_ref, part_ref
):
    rows, width = state_ref.shape
    normed, _ = normalize(state_ref[...].astype(F32))
    a_ref[...] = (normed * gain_ref[...]).astype(LOW)
    valid = valid_rows(rows, count[0])
    lone = lone_rows(rows, flag[0])
    part_ref[...] = jnp.broadcast_to(jnp.sum(valid), part_ref.shape)

    def body(at):
        a = a_ref[...]
        keys = dot(a, w_ref[2, :, at]) * valid
        k_ref[:, at] = keys
        part_ref[0:1, at] = jnp.sum(keys * keys, 0, keepdims=True)
        q_ref[:, at] = dot(a, w_ref[1, :, at])
        values = dot(a, w_ref[0, :, at]) * valid
        kh = dot(table_ref[0], keys.astype(LOW))
        kh_ref[:, at] = kh.astype(LOW)
        vh = dot(table_ref[0], values.astype(LOW))
        vh_ref[:, at] = vh.astype(LOW)
        kr, ki, vr, vi = kh[:rows], kh[rows:], vh[:rows], vh[rows:]
        cross = ki * vi
        real = kr * vr - jnp.where(lone, 0.0, cross)
        imag = jnp.where(lone, cross, kr * vi + ki * vr)
        y_ref[:, at] = dot(back_ref[0, :, :rows], real.astype(LOW)) + dot(
            back_ref[0, :, rows:], imag.astype(LOW)
        )

    columns(width, body)


def whole(shape):
    return pl.BlockSpec(shape, lambda *_: (0,) * len(shape))


def table_specs(tables):
    return [
        pl.BlockSpec((1,) + t.shape[1:], lambda i, flag, count: (flag[0], 0, 0)) for t in tables
    ]


def block_spec(shape, first, each):
    return pl.BlockSpec((each,) + shape[1:], lambda i, *_: (first // each, 0, 0))


def step_spec(shape, first):
    return pl.BlockSpec((1,) + shape[1:], lambda i, *_: (first + i, 0, 0))


def call(kernel, name, grid, scalars, args, specs, outs, out_specs, scratch=()):
    return pl.pallas_call(
        kernel,
        name=name,
        out_shape=outs,
        grid_spec=pltpu.PrefetchScalarGridSpec(
            num_scalar_prefetch=len(scalars),
            grid=(grid,),
            in_specs=specs,
            out_specs=out_specs,
            scratch_shapes=scratch,
        ),
        compiler_params=pltpu.CompilerParams(vmem_limit_bytes=VMEM_BYTES),
    )(*scalars, *args)


def front(scalars, layer, state, gain, weights, tables):
    rows, width = state.shape
    shapes = [
        ((rows, width), LOW),
        ((rows, width), F32),
        ((rows, width), F32),
        ((2 * rows, width), LOW),
        ((2 * rows, width), LOW),
        ((rows, width), F32),
        ((8, width), F32),
    ]
    return call(
        front_kernel,
        f"front_{layer}",
        1,
        scalars,
        (state, gain, weights, *tables),
        [whole(state.shape), whole(gain.shape), block_spec(weights.shape, 16 * layer, 4)]
        + table_specs(tables),
        [jax.ShapeDtypeStruct(*s) for s in shapes],
        [whole(s[0]) for s in shapes],
    )


def mlp_kernel(
    flag, count, state_ref, y_ref, q_ref, total_ref, gain_ref, wo_ref, gate_ref, up_ref, down_ref,
    mixed_ref, mid_ref, b_ref, g_ref, u_ref, hidden_ref, out_ref, sum_ref,
):
    step = pl.program_id(0)
    rows, width = state_ref.shape

    @pl.when(step == 0)
    def _():
        norm, _ = filter_norm_of(total_ref)
        scale = span_scale(rows, flag[0]) / norm
        mixed_ref[...] = (y_ref[...] * scale * q_ref[...]).astype(LOW)
        mid = state_ref[...].astype(F32) + dot(mixed_ref[...], wo_ref[0])
        mid_ref[...] = mid
        sum_ref[...] = mid
        normed, _ = normalize(mid)
        b_ref[...] = (normed * gain_ref[...]).astype(LOW)

    def body(at):
        gate = dot(b_ref[...], gate_ref[0, :, at])
        up = dot(b_ref[...], up_ref[0, :, at])
        g_ref[0, :, at] = gate.astype(LOW)
        u_ref[0, :, at] = up.astype(LOW)
        hidden_ref[0, :, at] = (gate * jax.nn.sigmoid(gate) * up).astype(LOW)

    columns(width, body)
    sum_ref[...] += dot(hidden_ref[0], down_ref[0])

    @pl.when(step == pl.num_programs(0) - 1)
    def _():
        out_ref[...] = sum_ref[...].astype(out_ref.dtype)


def mlp(scalars, layer, state, y, q, total, gain, weights, out_type):
    rows, width = state.shape
    row = (rows, width)
    shapes = [(row, LOW), (row, F32), (row, LOW)] + [((4,) + row, LOW)] * 3 + [(row, out_type)]
    first = 16 * layer
    return call(
        mlp_kernel,
        f"mlp_{layer}",
        4,
        scalars,
        (state, y, q, total, gain, weights, weights, weights, weights),
        [whole(t.shape) for t in (state, y, q, total, gain)]
        + [block_spec(weights.shape, first + 3, 1)]
        + [step_spec(weights.shape, first + i) for i in (4, 8, 12)],
        [jax.ShapeDtypeStruct(*s) for s in shapes],
        [whole(row)] * 3 + [step_spec((4,) + row, 0)] * 3 + [whole(row)],
        [pltpu.VMEM(row, F32)],
    )


def mlp_back_kernel(
    flag, count, grad_ref, mid_ref, gain_ref, b_ref, g_ref, u_ref, hidden_ref, gate_ref, up_ref, down_ref, wo_ref, q_ref, y_ref,
    total_ref, kh_ref, vh_ref, table_ref, back_ref,
    dgate_ref, dup_ref, ddown_ref, dmid_ref, dfilter_ref, dv_ref, dq_ref, part_ref, low_ref, sum_ref,
):
    step = pl.program_id(0)
    rows, width = grad_ref.shape
    valid = valid_rows(rows, count[0])

    @pl.when(step == 0)
    def _():
        low_ref[...] = (grad_ref[...] * valid).astype(LOW)
        sum_ref[...] = jnp.zeros_like(sum_ref)

    def body(at):
        dhidden = dot_nt(low_ref[...], down_ref[0, at, :])
        gate = g_ref[0, :, at].astype(F32)
        up = u_ref[0, :, at].astype(F32)
        sig = jax.nn.sigmoid(gate)
        dup = (dhidden * gate * sig).astype(LOW)
        dgate = (dhidden * up * sig * (1.0 + gate * (1.0 - sig))).astype(LOW)
        ddown_ref[0, at, :] = dot_tn(hidden_ref[0, :, at], low_ref[...]).astype(LOW)
        dgate_ref[0, :, at] = dot_tn(b_ref[...], dgate).astype(LOW)
        dup_ref[0, :, at] = dot_tn(b_ref[...], dup).astype(LOW)
        sum_ref[...] += dot_nt(dgate, gate_ref[0, :, at]) + dot_nt(dup, up_ref[0, :, at])

    columns(width, body)

    @pl.when(step == pl.num_programs(0) - 1)
    def _():
        normed, rstd = normalize(mid_ref[...])
        db = sum_ref[...]
        part_ref[...] = jnp.zeros_like(part_ref)
        part_ref[1:2, :] = jnp.sum(db * normed, 0, keepdims=True)
        dmid = grad_ref[...] * valid + norm_back(db * gain_ref[...], normed, rstd)
        dmid_ref[...] = dmid
        low_ref[...] = dmid.astype(LOW)
        norm, _ = filter_norm_of(total_ref)
        spans = span_scale(rows, flag[0])
        sum_ref[0:1, :] = spans / norm
        lone = lone_rows(rows, flag[0])

        def mix(at):
            scale = sum_ref[0:1, at]
            dmixed = dot_nt(low_ref[...], wo_ref[0, at, :])
            y = y_ref[:, at]
            dq_ref[:, at] = (dmixed * y * scale).astype(LOW)
            dy = dmixed * q_ref[:, at]
            part_ref[0:1, at] = jnp.sum(dy * y, 0, keepdims=True) * spans
            dh = dot(table_ref[0], dy.astype(LOW))
            dr, di = dh[:rows], dh[rows:]

            def against(ref):
                orr, oi = ref[:rows, at].astype(F32), ref[rows:, at].astype(F32)
                cross = di * oi
                real = dr * orr + jnp.where(lone, 0.0, cross)
                imag = jnp.where(lone, cross, di * orr - dr * oi)
                return dot(back_ref[0, :, :rows], real.astype(LOW)) + dot(
                    back_ref[0, :, rows:], imag.astype(LOW)
                )

            dfilter_ref[:, at] = against(vh_ref)
            dv_ref[:, at] = (against(kh_ref) * scale * valid).astype(LOW)

        columns(width, mix)


def mlp_back(scalars, layer, grad, mid, gain, b, g, u, hidden, weights, q, y, total, kh, vh, tables):
    rows, width = grad.shape
    row = (rows, width)
    square = (4, width, width)
    first = 16 * layer
    shapes = [(square, LOW)] * 3 + [(row, F32), (row, F32), (row, LOW), (row, LOW), ((8, width), F32)]
    return call(
        mlp_back_kernel,
        f"mlp_back_{layer}",
        4,
        scalars,
        (grad, mid, gain, b, g, u, hidden, weights, weights, weights, weights, q, y, total, kh, vh, *tables),
        [whole(t.shape) for t in (grad, mid, gain, b)]
        + [step_spec(g.shape, 0)] * 3
        + [step_spec(weights.shape, first + i) for i in (4, 8, 12)]
        + [block_spec(weights.shape, first + 3, 1)]
        + [whole(t.shape) for t in (q, y, total, kh, vh)]
        + table_specs(tables),
        [jax.ShapeDtypeStruct(*s) for s in shapes],
        [step_spec(square, 0)] * 3 + [whole(s[0]) for s in shapes[3:]],
        [pltpu.VMEM(row, LOW), pltpu.VMEM(row, F32)],
    )


def front_back_kernel(
    flag, count, dfilter_ref, k_ref, dv_ref, dq_ref, dmid_ref, a_ref, mixed_ref, w_ref, total_ref, back_total_ref, gain_ref,
    state_ref, dw_ref, dstate_ref, part_ref, dk_ref, sum_ref,
):
    rows, width = dmid_ref.shape
    norm, live = filter_norm_of(total_ref)
    scale = span_scale(rows, flag[0]) / norm
    square = -back_total_ref[0:1, :] / (norm * norm) / (2.0 * norm * live)
    valid = valid_rows(rows, count[0])
    dk_ref[...] = ((dfilter_ref[...] * scale + 2.0 * k_ref[...] * square) * valid).astype(LOW)
    low = dmid_ref[...].astype(LOW)
    sum_ref[...] = (
        dot_nt(dv_ref[...], w_ref[0]) + dot_nt(dq_ref[...], w_ref[1]) + dot_nt(dk_ref[...], w_ref[2])
    )

    def body(at):
        a = a_ref[...]
        dw_ref[0, :, at] = dot_tn(a, dv_ref[:, at]).astype(LOW)
        dw_ref[1, :, at] = dot_tn(a, dq_ref[:, at]).astype(LOW)
        dw_ref[2, :, at] = dot_tn(a, dk_ref[:, at]).astype(LOW)
        dw_ref[3, at, :] = dot_tn(mixed_ref[:, at], low).astype(LOW)

    columns(width, body)
    da = sum_ref[...]
    normed, rstd = normalize(state_ref[...].astype(F32))
    part_ref[...] = jnp.broadcast_to(jnp.sum(da * normed, 0, keepdims=True), part_ref.shape)
    dstate_ref[...] = dmid_ref[...] + norm_back(da * gain_ref[...], normed, rstd)


def front_back(scalars, layer, dfilter, k, dv, dq, dmid, a, mixed, weights, total, back_total, gain, state):
    rows, width = dmid.shape
    row = (rows, width)
    square = (4, width, width)
    shapes = [(square, LOW), (row, F32), ((8, width), F32)]
    args = (dfilter, k, dv, dq, dmid, a, mixed, weights, total, back_total, gain, state)
    specs = [whole(t.shape) for t in args]
    specs[7] = block_spec(weights.shape, 16 * layer, 4)
    return call(
        front_back_kernel,
        f"front_back_{layer}",
        1,
        scalars,
        args,
        specs,
        [jax.ShapeDtypeStruct(*s) for s in shapes],
        [whole(s[0]) for s in shapes],
        [pltpu.VMEM(row, LOW), pltpu.VMEM(row, F32)],
    )


class RowSum:
    def __init__(self, place, copies, part, by_z, by_d, mid, total):
        self.place, self.copies = place, copies
        self.part, self.by_z, self.by_d, self.mid, self.total = part, by_z, by_d, mid, total

    def start(self):
        p = self.place
        self.one = [
            self.copies.to(self.part, self.by_z.at[p.z], p.d, p.z_at(k)) for k in range(1, p.depth)
        ]
        for copy in self.one:
            copy.start()
        self.by_z[p.z] = self.part[...]

    def turn(self):
        p = self.place
        for copy in self.one:
            copy.wait_recv()
        total = self.by_z[0]
        for i in range(1, p.depth):
            total = total + self.by_z[i]
        self.mid[...] = total
        self.two = [
            self.copies.to(self.mid, self.by_d.at[p.d], lax.rem(p.d + k, p.n_dp), p.z)
            for k in range(1, p.n_dp)
        ]
        for copy in self.two:
            copy.start()
        self.by_d[p.d] = total

    def finish(self):
        for copy in self.two:
            copy.wait_recv()
        total = self.by_d[0]
        for i in range(1, self.place.n_dp):
            total = total + self.by_d[i]
        self.total[...] = total

    def drain(self):
        for copy in self.one + self.two:
            copy.wait_send()


class Gather:
    def __init__(self, place, copies, slots_ref, master_ref, out_ref, held, acc, *sum_refs):
        self.place, self.copies, self.slots_ref, self.master_ref = place, copies, slots_ref, master_ref
        self.out_ref, self.held, self.acc = out_ref, held, acc
        self.stages = stages = acc.shape[0]
        self.slot_cap, self.rows, cols = master_ref.shape
        self.piece_rows = 48 if self.rows % 48 == 0 else 16
        half = cols // 2
        halves = (pl.ds(0, half), pl.ds(half, half))
        self.sums = [PlaneSum(place, copies, s, acc, *sum_refs) for s in range(stages)]
        self.spreads = [
            PlaneSpread(place, copies, place.n_dp * s, out_ref, halves) for s in range(stages)
        ]
        self.along_z, self.kept = [None] * stages, [None] * stages
        self.steps = [
            self.enter, self.turn, self.send_z, self.spread, self.forward, self.finish
        ]

    def masked(self, s, y, x, core, at):
        slot = self.slots_ref[self.place.n_dp * s + self.place.dp(y, x, core)]
        low = slot - self.place.d * self.slot_cap
        mine = (low >= 0) & (low < self.slot_cap)
        index = jnp.clip(low, 0, self.slot_cap - 1)
        return jnp.where(mine, self.master_ref[index, at, :], 0.0).astype(LOW)

    def each_piece(self, body):
        p, rows = self.place, self.piece_rows
        pieces = self.rows // rows

        def one(i, carry):
            spot, piece = i // pieces, lax.rem(i, pieces)
            y, x = spot // p.across, lax.rem(spot, p.across)
            body(y, x, pl.ds(pl.multiple_of(piece * rows, 16), rows))
            return carry

        lax.fori_loop(0, p.up * p.across * pieces, one, 0)

    def offer(self):
        p = self.place
        self.over = []
        for s in range(self.stages):

            def fill(y, x, at, s=s):
                self.held[s, y, x, at, :] = self.masked(s, y, x, 1 - p.core, at)

            self.each_piece(fill)
            copy = self.copies.to(self.held.at[s], self.acc.at[s], p.dp(core=1 - p.core), p.z)
            copy.start()
            self.over.append(copy)

    def enter(self, s):
        self.over[s].wait_recv()

        def join(y, x, at):
            mine = self.masked(s, y, x, self.place.core, at)
            self.acc[s, y, x, at, :] = self.acc[s, y, x, at, :] + mine

        self.each_piece(join)
        self.sums[s].start()

    def turn(self, s):
        self.sums[s].turn()

    def send_z(self, s):
        p = self.place
        self.sums[s].finish()
        source = self.acc.at[s, p.y, p.x]
        rows = pl.ds(pl.multiple_of(p.z * self.rows, 16), self.rows)
        target = self.out_ref.at[p.n_dp * s + p.d, rows]
        self.kept[s] = self.copies.here(source, target)
        self.kept[s].start()
        self.along_z[s] = [
            self.copies.to(source, target, p.d, p.z_at(k)) for k in range(1, p.depth)
        ]
        for copy in self.along_z[s]:
            copy.start()

    def spread(self, s):
        self.kept[s].wait()
        for copy in self.along_z[s]:
            copy.wait_recv()
        self.spreads[s].start()

    def forward(self, s):
        self.spreads[s].forward()

    def finish(self, s):
        self.spreads[s].finish()
        self.spreads[s].arrived()

    def drain(self):
        for s in range(self.stages):
            self.over[s].wait_send()
            self.sums[s].drain()
            for copy in self.along_z[s]:
                copy.wait_send()
            self.spreads[s].drain()


class Stores:
    def __init__(self, copies):
        self.copies, self.open = copies, {}

    def out(self, name, source, target):
        copy = self.copies.here(source, target)
        copy.start()
        self.open.setdefault(name, []).append(copy)

    def settle(self, *names):
        for name in names or list(self.open):
            for copy in self.open.pop(name, []):
                copy.wait()


def forward_kernel(n_dp, n_fsdp, layers, *refs):
    (
        slots_ref, flag_ref, count_ref, master_in, tokens_in, gains_ref, table_in, back_in,
        w_ref, a_out, q_out, k_out, kh_out, vh_out, y_out, mixed_out, mid_out, b_out, g_out, u_out, h_out,
        total_out, state_out, act_out,
        master, held, acc, from_x, from_y, last_y, last_x,
        tok, state, table, back, wfront, wmlp, a, q, k, kh, vh, y, mixed, mid, b, g, u, h,
        part, by_z, by_d, mid_sum, total, send, recv, local,
    ) = refs
    place = Place(n_dp, n_fsdp)
    copies = Copies(send, recv, local)
    stores = Stores(copies)
    rows, width = state.shape
    load_master = copies.here(master_in, master)
    load_master.start()
    loads = [copies.here(*pair) for pair in ((tokens_in, tok), (table_in, table), (back_in, back))]
    for copy in loads:
        copy.start()
    place.greet_all()
    load_master.wait()
    gather = Gather(place, copies, slots_ref, master, w_ref, held, acc, from_x, from_y, last_y, last_x)
    sums = [
        RowSum(place, copies, *(ref.at[layer] for ref in (part, by_z, by_d, mid_sum, total)))
        for layer in range(layers)
    ]
    valid = valid_rows(rows, count_ref[0])
    lone = lone_rows(rows, flag_ref[0])
    spans = span_scale(rows, flag_ref[0])
    waiting = {}

    def fetch(name, blocks, targets):
        waiting[name] = [copies.here(w_ref.at[j], t) for j, t in zip(blocks, targets)]
        for copy in waiting[name]:
            copy.start()

    def fetched(name):
        for copy in waiting.pop(name):
            copy.wait()

    def front_of(layer):
        fetch("front", [16 * layer + i for i in range(4)], [wfront.at[i] for i in range(4)])
        if layer == 0:
            for copy in loads:
                copy.wait()
            state[...] = tok[...].astype(F32)
        stores.settle("a", "k", "q", "kh", "vh", "y")
        stores.out("state", state, state_out.at[layer])
        normed, _ = normalize(state[...])
        a[...] = (normed * gains_ref[2 * layer : 2 * layer + 1, :]).astype(LOW)
        stores.out("a", a, a_out.at[layer])
        part[layer] = jnp.broadcast_to(jnp.sum(valid), part.shape[1:])
        fetched("front")

        def keys(at):
            value = dot(a[...], wfront[2, :, at]) * valid
            k[:, at] = value
            part[layer, 0:1, at] = jnp.sum(value * value, 0, keepdims=True)

        columns(width, keys)
        sums[layer].start()
        stores.out("k", k, k_out.at[layer])

        def spectra(at):
            q[:, at] = dot(a[...], wfront[1, :, at])
            values = (dot(a[...], wfront[0, :, at]) * valid).astype(LOW)
            kh[:, at] = dot(table[...], k[:, at].astype(LOW)).astype(LOW)
            vh[:, at] = dot(table[...], values).astype(LOW)

        columns(width, spectra)
        stores.out("q", q, q_out.at[layer])
        stores.out("kh", kh, kh_out.at[layer])
        stores.out("vh", vh, vh_out.at[layer])
        sums[layer].turn()

        def product(at):
            kr, ki = kh[:rows, at].astype(F32), kh[rows:, at].astype(F32)
            vr, vi = vh[:rows, at].astype(F32), vh[rows:, at].astype(F32)
            cross = ki * vi
            real = kr * vr - jnp.where(lone, 0.0, cross)
            imag = jnp.where(lone, cross, kr * vi + ki * vr)
            y[:, at] = dot(back[:, :rows], real.astype(LOW)) + dot(
                back[:, rows:], imag.astype(LOW)
            )

        columns(width, product)
        stores.out("y", y, y_out.at[layer])

    def fetch_mlp(layer, i):
        first = 16 * layer + i
        fetch(("mlp", i), [first + 4, first + 8, first + 12], [wmlp.at[i % 2, j] for j in range(3)])

    def mlp_of(layer):
        fetch_mlp(layer, 0)
        stores.settle("mixed", "mid", "b", "state")
        sums[layer].finish()
        stores.out("total", total.at[layer], total_out.at[layer])
        norm, _ = filter_norm_of(total.at[layer])
        mixed[...] = (y[...] * (spans / norm) * q[...]).astype(LOW)
        stores.out("mixed", mixed, mixed_out.at[layer])
        state[...] += dot(mixed[...], wfront[3])
        mid[...] = state[...]
        stores.out("mid", mid, mid_out.at[layer])
        normed, _ = normalize(state[...])
        b[...] = (normed * gains_ref[2 * layer + 1 : 2 * layer + 2, :]).astype(LOW)
        stores.out("b", b, b_out.at[layer])
        for i in range(4):
            turn = i % 2
            fetched(("mlp", i))
            if i < 3:
                fetch_mlp(layer, i + 1)
            stores.settle(("g", turn))

            def body(at, turn=turn):
                gate = dot(b[...], wmlp[turn, 0, :, at])
                up = dot(b[...], wmlp[turn, 1, :, at])
                g[turn, :, at] = gate.astype(LOW)
                u[turn, :, at] = up.astype(LOW)
                h[turn, :, at] = (gate * jax.nn.sigmoid(gate) * up).astype(LOW)

            columns(width, body)
            for held_ref, out in ((g, g_out), (u, u_out), (h, h_out)):
                stores.out(("g", turn), held_ref.at[turn], out.at[layer, i])
            state[...] += dot(h[turn], wmlp[turn, 2])
        if layer == layers - 1:
            tok[...] = state[...].astype(LOW)
            stores.out("act", tok, act_out)

    gather.offer()
    last = len(gather.steps) - 1
    for t in range(gather.stages + last):
        for i, step in enumerate(gather.steps):
            if 0 <= t - i < gather.stages:
                step(t - i)
        for layer in range(layers):
            if t == 16 * layer // n_dp + last:
                front_of(layer)
            if t == (16 * layer + 15) // n_dp + last:
                mlp_of(layer)
    gather.drain()
    for one in sums:
        one.drain()
    stores.settle()


def forward(n_dp, n_fsdp, scalars, owner_slots, master, tokens, gains, tables):
    blocks = owner_slots.shape[0]
    layers = blocks // 16
    part_rows, cols = master.shape[1:]
    rows, width = tokens.shape
    stages = blocks // n_dp
    row = (rows, width)
    spectrum = (2 * rows, width)
    saved = [
        (row, LOW), (row, F32), (row, F32), (spectrum, LOW), (spectrum, LOW), (row, F32), (row, LOW), (row, F32), (row, LOW),
        ((4,) + row, LOW), ((4,) + row, LOW), ((4,) + row, LOW), ((8, width), F32), (row, F32),
    ]
    count = copy_count(n_dp, n_fsdp, stages, 1) + layers * (n_dp + n_fsdp - 2)
    any_space = pl.BlockSpec(memory_space=pl.ANY)
    scalar = pl.BlockSpec(memory_space=pltpu.SMEM)
    vmem = pl.BlockSpec(memory_space=pltpu.VMEM)
    return pl.pallas_call(
        functools.partial(forward_kernel, n_dp, n_fsdp, layers),
        name="forward",
        out_shape=[jax.ShapeDtypeStruct((blocks, width, width), LOW)]
        + [jax.ShapeDtypeStruct((layers,) + shape, kind) for shape, kind in saved]
        + [jax.ShapeDtypeStruct(row, LOW)],
        in_specs=[scalar] * 3 + [any_space, any_space, vmem, any_space, any_space],
        out_specs=[any_space] * (2 + len(saved)),
        scratch_shapes=[
            pltpu.VMEM(master.shape, F32),
            pltpu.VMEM((stages, 2, n_dp // 4, part_rows, cols), LOW),
        ]
        + plane_sum_shapes(n_dp, stages, part_rows, cols)
        + [
            pltpu.VMEM(row, LOW),
            pltpu.VMEM(row, F32),
            pltpu.VMEM(tables[0].shape, LOW),
            pltpu.VMEM(tables[1].shape, LOW),
            pltpu.VMEM((4, width, width), LOW),
            pltpu.VMEM((2, 3, width, width), LOW),
        ]
        + [pltpu.VMEM(shape, kind) for shape, kind in saved[:9]]
        + [pltpu.VMEM((2,) + row, LOW)] * 3
        + [
            pltpu.VMEM((layers, 8, width), F32),
            pltpu.VMEM((layers, n_fsdp, 8, width), F32),
            pltpu.VMEM((layers, n_dp, 8, width), F32),
            pltpu.VMEM((layers, 8, width), F32),
            pltpu.VMEM((layers, 8, width), F32),
            pltpu.SemaphoreType.DMA((count,)),
            pltpu.SemaphoreType.DMA((count,)),
            pltpu.SemaphoreType.DMA((stages + 8 + layers * 48,)),
        ],
        compiler_params=pltpu.CompilerParams(
            collective_id=0, has_side_effects=True, vmem_limit_bytes=VMEM_BYTES
        ),
    )(owner_slots, *scalars, master, tokens, gains, *tables)


def adam_step(grad, first, second, weight, rate, decay):
    first_out = 0.5 * first + 0.5 * grad
    second_out = 0.5 * second + 0.5 * grad * grad
    corr = 1.0 - 0.5**STEP
    weight_out = weight - rate * (
        first_out / corr / (jnp.sqrt(second_out / corr) + ADAM_EPS) + decay * weight
    )
    return (first_out, second_out, weight_out)


def adam_kernel(
    block, used, grad_ref, master_ref, first_ref, second_ref, first_out, second_out, master_out
):
    taken = used[pl.program_id(0)] == 1
    first, second, master = first_ref[...], second_ref[...], master_ref[...]
    new = adam_step(grad_ref[...].astype(F32), first, second, master, 0.03, 0.01)
    first_out[...] = jnp.where(taken, new[0], first)
    second_out[...] = jnp.where(taken, new[1], second)
    master_out[...] = jnp.where(taken, new[2], master)


def adam_blocks(block, used, grads, master, first, second):
    shape = (1,) + master.shape[1:]
    own = pl.BlockSpec(shape, lambda i, block, used: (i, 0, 0))
    picked = pl.BlockSpec(shape, lambda i, block, used: (block[i], 0, 0))
    return call(
        adam_kernel,
        "adam",
        master.shape[0],
        (block, used),
        (grads, master, first, second),
        [picked, own, own, own],
        [jax.ShapeDtypeStruct(master.shape, F32)] * 3,
        [own] * 3,
    )


def on_device(
    n_dp,
    n_fsdp,
    tokens,
    cotangent,
    row_counts,
    bucket_flags,
    owner_slots,
    master,
    first_moment,
    second_moment,
    gains,
    gain_first,
    gain_second,
):
    rows = tokens.shape[0]
    slot_cap = master.shape[0]
    layers = owner_slots.shape[0] // 16
    tables = transform_tables(rows)
    scalars = (bucket_flags, row_counts)
    picked = [lax.dynamic_index_in_dim(t, bucket_flags[0], 0, keepdims=False) for t in tables]
    weights, *saved, activations = forward(
        n_dp, n_fsdp, scalars, owner_slots, master, tokens, gains, picked
    )
    grad = cotangent
    gain_rows = [None] * (2 * layers)
    block_grads = [None] * (4 * layers)
    for layer in reversed(range(layers)):
        gain_one, gain_two = gains[2 * layer : 2 * layer + 1], gains[2 * layer + 1 : 2 * layer + 2]
        a, q, k, kh, vh, y, mixed, mid, b, g, u, hidden, total, state = (t[layer] for t in saved)
        dgate, dup, ddown, dmid, dfilter, dv, dq, part = mlp_back(
            scalars, layer, grad, mid, gain_two, b, g, u, hidden, weights, q, y, total, kh, vh, tables
        )
        gain_rows[2 * layer + 1] = part[1:2]
        back_total = sum_rows(n_dp, n_fsdp, part)
        dw, grad, part = front_back(
            scalars, layer, dfilter, k, dv, dq, dmid, a, mixed, weights, total, back_total, gain_one, state
        )
        gain_rows[2 * layer] = part[0:1]
        block_grads[4 * layer : 4 * layer + 4] = [dw, dgate, dup, ddown]
    summed = scatter_grads(n_dp, n_fsdp, block_grads)
    pad = [jnp.zeros((8 - 2 * layers, gains.shape[1]), F32)]
    gains_total = sum_rows(n_dp, n_fsdp, jnp.concatenate(gain_rows + pad, 0))[: 2 * layers]
    my_slots = lax.axis_index("dp") * slot_cap + jnp.arange(slot_cap, dtype=jnp.int32)
    hits = owner_slots[None, :] == my_slots[:, None]
    used = jnp.any(hits, 1).astype(jnp.int32)
    block = jnp.sum(jnp.where(hits, jnp.arange(owner_slots.shape[0], dtype=jnp.int32)[None, :], 0), 1)
    first_out, second_out, master_out = adam_blocks(
        block, used, summed, master, first_moment, second_moment
    )
    gain_m, gain_v, gain_w = adam_step(gains_total, gain_first, gain_second, gains, 0.2, 0.0)
    return (activations, grad, first_out, second_out, master_out, gain_m, gain_v, gain_w)


def solution(mesh):
    rows = P(("dp", "fsdp"), None)
    blocks = P("dp", "fsdp", None)
    flat = P(("dp", "fsdp"))
    return jax.shard_map(
        functools.partial(on_device, mesh.shape["dp"], mesh.shape["fsdp"]),
        mesh=mesh,
        in_specs=(rows, rows, flat, flat, P(), blocks, blocks, blocks, P(), P(), P()),
        out_specs=(rows, rows, blocks, blocks, blocks, P(), P(), P()),
        check_vma=False,
    )
```

```python
import functools
import math
import types

import jax
import jax.numpy as jnp
import numpy as np
from jax import lax
from jax.experimental import pallas as pl
from jax.experimental.pallas import tpu as pltpu
from jax.sharding import PartitionSpec as P

STEP = 5
NORM_EPS = 1e-05
ADAM_EPS = 1e-08
LOW = jnp.bfloat16
F32 = jnp.float32
MESH = pl.DeviceIdType.MESH
VMEM_BYTES = 60 * 2**20


FORWARD_PLAN = [
    "gather.fill:0", "gather.fill:1", "gather.fill:2", "gather.fill:3", "gather.enter:0", "gather.enter:1",
    "gather.enter:2", "gather.turn:0", "gather.enter:3", "gather.turn:1", "gather.home:0", "gather.column:0",
    "gather.turn:2", "gather.home:1", "gather.turn:3", "gather.home:2", "gather.column:1", "gather.passing:0,0",
    "gather.cell:0,1", "gather.cell:0,3", "gather.close:0,0", "gather.cell:0,2", "gather.column:2",
    "gather.passing:0,1", "gather.passing:1,0", "gather.passing:0,3", "gather.cell:1,1", "gather.close:0,1",
    "gather.cell:1,3", "gather.close:1,0", "gather.close:0,3", "gather.passing:0,2", "gather.cell:1,2",
    "gather.passing:1,1", "gather.cell:2,1", "gather.close:0,2", "gather.done:0", "compute.front_a:0",
    "gather.close:1,1", "gather.passing:1,3", "gather.cell:2,2", "compute.front_b:0", "gather.passing:1,2",
    "compute.front_c:0", "gather.close:1,3", "gather.cell:2,3", "gather.home:3", "gather.close:1,2",
    "gather.column:3", "gather.done:1", "compute.mix:0", "gather.passing:2,0", "compute.mlp:0,0",
    "gather.passing:2,1", "compute.mlp:0,1", "gather.passing:2,2", "compute.mlp:0,2", "compute.mlp:0,3",
    "gather.passing:2,3", "gather.passing:3,0", "gather.close:2,0", "gather.close:2,1", "gather.cell:3,1",
    "gather.close:2,2", "gather.cell:3,2", "gather.close:2,3", "gather.close:3,0", "gather.done:2",
    "compute.front_a:1", "gather.cell:3,3", "compute.front_b:1", "gather.passing:3,1", "gather.passing:3,2",
    "compute.front_c:1", "gather.passing:3,3", "gather.close:3,1", "gather.close:3,2", "gather.close:3,3",
    "gather.done:3", "compute.mix:1", "compute.mlp:1,0", "compute.mlp:1,1", "compute.mlp:1,2", "compute.mlp:1,3",
]
BACKWARD_PLAN = [
    "compute.mlp:1,0", "compute.mlp:1,1", "compute.mlp:1,2", "compute.mlp:1,3", "scatter.offer:0", "compute.mix_a:1",
    "compute.mix_b:1", "compute.front_a:1", "scatter.enter:0", "scatter.push:0,1", "scatter.push:0,2",
    "compute.front_b:1", "scatter.offer:1", "scatter.push:0,3", "compute.mlp:0,0", "compute.mlp:0,1",
    "scatter.turn:0,1", "scatter.turn:0,2", "scatter.enter:1", "scatter.turn:0,3", "scatter.home:0,1",
    "scatter.home:0,2", "scatter.push:0,0", "scatter.push:1,1", "compute.mlp:0,2", "scatter.push:1,2",
    "scatter.home:0,3", "compute.mlp:0,3", "scatter.offer:2", "scatter.push:1,3", "compute.mix_a:0",
    "compute.mix_b:0", "scatter.turn:0,0", "scatter.turn:1,1", "compute.front_a:0", "scatter.turn:1,2",
    "compute.front_b:0", "scatter.offer:3", "scatter.turn:1,3", "scatter.home:1,1", "scatter.home:0,0",
    "scatter.total:0", "scatter.enter:2", "scatter.home:1,2", "scatter.push:2,1", "scatter.push:2,2",
    "scatter.push:1,0", "scatter.home:1,3", "scatter.passing:0", "scatter.push:2,3", "scatter.turn:2,1",
    "scatter.turn:2,2", "scatter.close:0", "scatter.done:0", "scatter.turn:1,0", "scatter.home:2,1",
    "scatter.home:2,2", "scatter.turn:2,3", "scatter.home:1,0", "scatter.total:1", "scatter.enter:3",
    "scatter.home:2,3", "scatter.push:2,0", "scatter.push:3,1", "scatter.passing:1", "scatter.push:3,2",
    "scatter.push:3,3", "scatter.turn:3,1", "scatter.close:1", "scatter.turn:2,0", "scatter.done:1",
    "scatter.push:3,0", "scatter.turn:3,2", "scatter.home:3,1", "scatter.turn:3,3", "scatter.home:2,0",
    "scatter.total:2", "scatter.home:3,2", "scatter.home:3,3", "scatter.turn:3,0", "scatter.passing:2",
    "scatter.home:3,0", "scatter.close:2", "scatter.total:3", "scatter.done:2", "scatter.passing:3",
    "scatter.close:3", "scatter.done:3",
]


def span_tables(length):
    period = 2 * length
    freqs = np.arange(length)[:, None]
    places = np.arange(length)[None, :]
    angle = (freqs * places % period) * (2.0 * math.pi / period)
    cosine, sine = np.cos(angle), -np.sin(angle)
    sine[0] = np.cos(math.pi * np.arange(length))
    weight = np.where(np.arange(length) == 0, 1.0, 2.0)[None, :] / period
    return (cosine, sine, cosine.T * weight, sine.T * weight)


def transform_tables(rows):
    short = [np.kron(np.eye(4), table) for table in span_tables(rows // 4)]
    full = span_tables(rows)
    forward = np.stack([np.concatenate(t[:2], 0) for t in (short, full)])
    inverse = np.stack([np.concatenate(t[2:], 1) for t in (short, full)])
    return (jnp.asarray(forward, LOW), jnp.asarray(inverse, LOW))


class Place:
    def __init__(self, n_dp, n_fsdp):
        self.n_dp, self.depth = n_dp, n_fsdp
        self.up, self.across = 2, n_dp // 4
        self.d = lax.axis_index("dp")
        self.z = lax.axis_index("fsdp")
        self.core = lax.rem(self.d, 2)
        self.x = lax.rem(self.d // 2, self.across)
        self.y = self.d // (2 * self.across)

    def x_at(self, k):
        return lax.rem(self.x + k + self.across, self.across)

    def y_at(self, m):
        return lax.rem(self.y + m + self.up, self.up)

    def z_at(self, k):
        return lax.rem(self.z + k + self.depth, self.depth)

    def dp(self, y=None, x=None, core=None):
        y = self.y if y is None else y
        x = self.x if x is None else x
        core = self.core if core is None else core
        return (y * self.across + x) * 2 + core

    def greet(self):
        barrier = pltpu.get_barrier_semaphore()
        peers = [(self.dp(core=1 - self.core), self.z)]
        peers += [(self.dp(x=self.x_at(k)), self.z) for k in range(1, self.across)]
        peers += [(self.dp(y=self.y_at(m)), self.z) for m in range(1, self.up)]
        peers += [(self.d, self.z_at(k)) for k in range(1, self.depth)]
        for peer in peers:
            pl.semaphore_signal(barrier, inc=1, device_id=peer, device_id_type=MESH)
        pl.semaphore_wait(barrier, len(peers))

    def greet_all(self):
        barrier = pltpu.get_barrier_semaphore()
        peers = [(lax.rem(self.d + k, self.n_dp), self.z) for k in range(1, self.n_dp)]
        peers += [(self.d, self.z_at(k)) for k in range(1, self.depth)]
        for peer in peers:
            pl.semaphore_signal(barrier, inc=1, device_id=peer, device_id_type=MESH)
        pl.semaphore_wait(barrier, len(peers))


class Copies:
    def __init__(self, send, recv, local):
        self.send, self.recv, self.local = send, recv, local
        self.sent, self.moved = 0, 0

    def to(self, source, target, dp, z):
        index = self.sent
        self.sent += 1
        return pltpu.make_async_remote_copy(
            src_ref=source,
            dst_ref=target,
            send_sem=self.send.at[index],
            recv_sem=self.recv.at[index],
            device_id=(dp, z),
            device_id_type=MESH,
        )

    def here(self, source, target):
        index = self.moved
        self.moved += 1
        return pltpu.make_async_copy(source, target, self.local.at[index])


def add_into(total, terms, rows):
    step = next(size for size in (48, 32, 16) if rows % size == 0)

    def piece(i, carry):
        at = pl.ds(pl.multiple_of(i * step, 16), step)
        value = total[at, :].astype(F32)
        for term in terms:
            value = value + term[at, :].astype(F32)
        total[at, :] = value.astype(LOW)
        return carry

    lax.fori_loop(0, rows // step, piece, 0)


class PlaneSum:
    def __init__(self, place, copies, acc, window, count, from_x, from_y, last_y, last_x):
        self.place, self.copies, self.acc, self.window, self.count = place, copies, acc, window, count
        self.from_x, self.from_y, self.last_y, self.last_x = from_x, from_y, last_y, last_x
        half = acc.shape[-1] // 2
        self.first, self.second = pl.ds(0, half), pl.ds(half, half)
        self.rows = pl.ds(0, count)

    def start(self):
        p, rows = self.place, self.rows
        self.one = []
        for k in range(1, p.across):
            source = self.acc.at[:, p.x_at(k), self.window, self.first]
            target = self.from_x.at[k - 1, :, rows]
            self.one.append(self.copies.to(source, target, p.dp(x=p.x_at(k)), p.z))
        for m in range(1, p.up):
            source = self.acc.at[p.y_at(m), :, self.window, self.second]
            target = self.from_y.at[m - 1, :, rows]
            self.one.append(self.copies.to(source, target, p.dp(y=p.y_at(m)), p.z))
        for copy in self.one:
            copy.start()

    def turn(self):
        p, rows = self.place, self.rows
        for copy in self.one:
            copy.wait_recv()
        for y in range(p.up):
            terms = [self.from_x.at[k - 1, y, rows] for k in range(1, p.across)]
            add_into(self.acc.at[y, p.x, self.window, self.first], terms, self.count)
        for x in range(p.across):
            terms = [self.from_y.at[m - 1, x, rows] for m in range(1, p.up)]
            add_into(self.acc.at[p.y, x, self.window, self.second], terms, self.count)
        self.two = []
        for m in range(1, p.up):
            source = self.acc.at[p.y_at(m), p.x, self.window, self.first]
            target = self.last_y.at[m - 1, rows]
            self.two.append(self.copies.to(source, target, p.dp(y=p.y_at(m)), p.z))
        for k in range(1, p.across):
            source = self.acc.at[p.y, p.x_at(k), self.window, self.second]
            target = self.last_x.at[k - 1, rows]
            self.two.append(self.copies.to(source, target, p.dp(x=p.x_at(k)), p.z))
        for copy in self.two:
            copy.start()

    def finish(self):
        p, rows = self.place, self.rows
        for copy in self.two:
            copy.wait_recv()
        terms = [self.last_y.at[m - 1, rows] for m in range(1, p.up)]
        add_into(self.acc.at[p.y, p.x, self.window, self.first], terms, self.count)
        terms = [self.last_x.at[k - 1, rows] for k in range(1, p.across)]
        add_into(self.acc.at[p.y, p.x, self.window, self.second], terms, self.count)

    def drain(self):
        for copy in self.one + self.two:
            copy.wait_send()


class PlaneSpread:
    def __init__(self, place, copies, base, array, window, source=None):
        self.place, self.copies, self.base, self.array = place, copies, base, array
        self.window, self.source = window, source
        half = array.shape[-1] // 2
        self.halves = (pl.ds(0, half), pl.ds(half, half))
        self.sends, self.arrive = [], []

    def block(self, half=None, **where):
        index = self.base + self.place.dp(**where)
        if half is None:
            return self.array.at[index, self.window]
        return self.array.at[index, self.window, self.halves[half]]

    def fire(self, ref, dp, source=None):
        copy = self.copies.to(ref if source is None else source, ref, dp, self.place.z)
        copy.start()
        self.sends.append(copy)
        return copy

    def hand_over(self, source=None, **where):
        p = self.place
        self.arrive.append(self.fire(self.block(**where), p.dp(core=1 - p.core), source))

    def start(self):
        p, own = self.place, self.block()
        self.by_x = [self.fire(own, p.dp(x=p.x_at(k)), self.source) for k in range(1, p.across)]
        self.by_y = [self.fire(own, p.dp(y=p.y_at(m)), self.source) for m in range(1, p.up)]
        self.hand_over(self.source)

    def forward(self):
        p = self.place
        self.first, self.second = {}, {}
        for k in range(1, p.across):
            self.by_x[k - 1].wait_recv()
            for m in range(1, p.up):
                block = self.block(0, x=p.x_at(-k))
                self.first[m, k] = self.fire(block, p.dp(y=p.y_at(m)))
        for m in range(1, p.up):
            self.by_y[m - 1].wait_recv()
            for k in range(1, p.across):
                block = self.block(1, y=p.y_at(-m))
                self.second[m, k] = self.fire(block, p.dp(x=p.x_at(k)))
        for k in range(1, p.across):
            self.hand_over(x=p.x_at(-k))
        for m in range(1, p.up):
            self.hand_over(y=p.y_at(-m))

    def finish(self):
        p = self.place
        for m in range(1, p.up):
            for k in range(1, p.across):
                self.first[m, k].wait_recv()
                self.second[m, k].wait_recv()
                self.hand_over(y=p.y_at(-m), x=p.x_at(-k))

    def arrived(self):
        for copy in self.arrive:
            copy.wait_recv()

    def drain(self):
        for copy in self.sends:
            copy.wait_send()


def plane_sum_shapes(n_dp, lead, rows, cols):
    up, across, half = 2, n_dp // 4, cols // 2
    return [
        pltpu.VMEM(lead + (across - 1, up, rows, half), LOW),
        pltpu.VMEM(lead + (up - 1, across, rows, half), LOW),
        pltpu.VMEM(lead + (up - 1, rows, half), LOW),
        pltpu.VMEM(lead + (across - 1, rows, half), LOW),
    ]


def copy_count(n_dp, n_fsdp, stages, sums, spreads, others):
    up, across = 2, n_dp // 4
    near = up - 1 + across - 1
    diagonal = (up - 1) * (across - 1)
    each_spread = near + 2 * diagonal + up * across
    return stages * (sums * 2 * near + spreads * each_spread + others)


def run_plan(plan, **actors):
    for step in plan:
        name, _, where = step.partition(":")
        actor, _, method = name.partition(".")
        getattr(actors[actor], method)(*(int(i) for i in where.split(",")))


def dot(left, right):
    return jnp.dot(left, right, preferred_element_type=F32)


def dot_nt(left, right):
    return lax.dot_general(left, right, (((1,), (1,)), ((), ())), preferred_element_type=F32)


def dot_tn(left, right):
    return lax.dot_general(left, right, (((0,), (0,)), ((), ())), preferred_element_type=F32)


def normalize(inputs):
    centred = inputs - jnp.mean(inputs, -1, keepdims=True)
    rstd = lax.rsqrt(jnp.mean(centred * centred, -1, keepdims=True) + NORM_EPS)
    return (centred * rstd, rstd)


def norm_back(grad, normed, rstd):
    return rstd * (
        grad
        - jnp.mean(grad, -1, keepdims=True)
        - normed * jnp.mean(grad * normed, -1, keepdims=True)
    )


def valid_rows(rows, count):
    return (lax.broadcasted_iota(jnp.int32, (rows, 1), 0) < count).astype(F32)


def lone_rows(rows, flag):
    span = jnp.where(flag == 1, rows, rows // 4)
    return lax.rem(lax.broadcasted_iota(jnp.int32, (rows, 1), 0), span) == 0


def span_scale(rows, flag):
    return jnp.where(flag == 1, rows**-0.5, (rows // 4) ** -0.5).astype(F32)


def filter_norm_of(total_ref):
    live = total_ref[1:2, :]
    return (jnp.sqrt(total_ref[0:1, :] / live + NORM_EPS), live)


def columns(width, body):
    for at in range(0, width, 256):
        body(pl.ds(at, 256))


class RowSum:
    def __init__(self, place, copies, part, by_z, by_d, mid, total):
        self.place, self.copies = place, copies
        self.part, self.by_z, self.by_d, self.mid, self.total = part, by_z, by_d, mid, total

    def start(self):
        p = self.place
        self.one = [
            self.copies.to(self.part, self.by_z.at[p.z], p.d, p.z_at(k)) for k in range(1, p.depth)
        ]
        for copy in self.one:
            copy.start()
        self.by_z[p.z] = self.part[...]

    def turn(self):
        p = self.place
        for copy in self.one:
            copy.wait_recv()
        total = self.by_z[0]
        for i in range(1, p.depth):
            total = total + self.by_z[i]
        self.mid[...] = total
        self.two = [
            self.copies.to(self.mid, self.by_d.at[p.d], lax.rem(p.d + k, p.n_dp), p.z)
            for k in range(1, p.n_dp)
        ]
        for copy in self.two:
            copy.start()
        self.by_d[p.d] = total

    def finish(self):
        for copy in self.two:
            copy.wait_recv()
        total = self.by_d[0]
        for i in range(1, self.place.n_dp):
            total = total + self.by_d[i]
        self.total[...] = total

    def drain(self):
        for copy in self.one + self.two:
            copy.wait_send()


class Gather:
    def __init__(self, place, copies, slots_ref, master_ref, out_ref, held, acc, *sum_refs):
        self.place, self.copies, self.slots_ref, self.master_ref = place, copies, slots_ref, master_ref
        self.out_ref, self.held, self.acc = out_ref, held, acc
        self.stages = stages = acc.shape[0]
        self.slot_cap, self.rows, _ = master_ref.shape
        self.piece_rows = 48 if self.rows % 48 == 0 else 16
        whole = pl.ds(0, self.rows)
        self.sums = [
            PlaneSum(place, copies, acc.at[s], whole, self.rows, *(ref.at[s] for ref in sum_refs))
            for s in range(stages)
        ]
        self.cells = [
            [
                PlaneSpread(
                    place, copies, place.n_dp * s, out_ref, self.rows_of(place.z_at(-k)),
                    acc.at[s, place.y, place.x] if k == 0 else None,
                )
                for k in range(place.depth)
            ]
            for s in range(stages)
        ]
        self.over, self.along_z, self.kept = [None] * stages, [None] * stages, [None] * stages

    def rows_of(self, z):
        return pl.ds(pl.multiple_of(z * self.rows, 16), self.rows)

    def masked(self, s, y, x, core, at):
        slot = self.slots_ref[self.place.n_dp * s + self.place.dp(y, x, core)]
        low = slot - self.place.d * self.slot_cap
        mine = (low >= 0) & (low < self.slot_cap)
        index = jnp.clip(low, 0, self.slot_cap - 1)
        return jnp.where(mine, self.master_ref[index, at, :], 0.0).astype(LOW)

    def each_piece(self, body):
        p, rows = self.place, self.piece_rows
        pieces = self.rows // rows

        def one(i, carry):
            spot, piece = i // pieces, lax.rem(i, pieces)
            y, x = spot // p.across, lax.rem(spot, p.across)
            body(y, x, pl.ds(pl.multiple_of(piece * rows, 16), rows))
            return carry

        lax.fori_loop(0, p.up * p.across * pieces, one, 0)

    def fill(self, s):
        p = self.place

        def body(y, x, at):
            self.held[s, y, x, at, :] = self.masked(s, y, x, 1 - p.core, at)

        self.each_piece(body)
        self.over[s] = self.copies.to(
            self.held.at[s], self.acc.at[s], p.dp(core=1 - p.core), p.z
        )
        self.over[s].start()

    def enter(self, s):
        self.over[s].wait_recv()

        def join(y, x, at):
            mine = self.masked(s, y, x, self.place.core, at)
            self.acc[s, y, x, at, :] = self.acc[s, y, x, at, :] + mine

        self.each_piece(join)
        self.sums[s].start()

    def turn(self, s):
        self.sums[s].turn()

    def home(self, s):
        p = self.place
        self.sums[s].finish()
        target = self.out_ref.at[p.n_dp * s + p.d, self.rows_of(p.z)]
        self.kept[s] = self.copies.here(self.acc.at[s, p.y, p.x], target)
        self.kept[s].start()
        self.cells[s][0].start()

    def column(self, s):
        p = self.place
        source = self.acc.at[s, p.y, p.x]
        target = self.out_ref.at[p.n_dp * s + p.d, self.rows_of(p.z)]
        self.along_z[s] = [
            self.copies.to(source, target, p.d, p.z_at(k)) for k in range(1, p.depth)
        ]
        for copy in self.along_z[s]:
            copy.start()

    def cell(self, s, k):
        self.along_z[s][k - 1].wait_recv()
        self.cells[s][k].start()

    def passing(self, s, k):
        self.cells[s][k].forward()

    def close(self, s, k):
        self.cells[s][k].finish()

    def done(self, s):
        self.kept[s].wait()
        for cell in self.cells[s]:
            cell.arrived()

    def drain(self):
        for s in range(self.stages):
            self.over[s].wait_send()
            self.sums[s].drain()
            for copy in self.along_z[s]:
                copy.wait_send()
            for cell in self.cells[s]:
                cell.drain()


class Stores:
    def __init__(self, copies):
        self.copies, self.open = copies, {}

    def out(self, name, source, target):
        copy = self.copies.here(source, target)
        copy.start()
        self.open.setdefault(name, []).append(copy)

    def settle(self, *names):
        for name in names or list(self.open):
            for copy in self.open.pop(name, []):
                copy.wait()


def forward_plan(layers, stages, depth):
    if (layers, stages, depth) == (2, 4, 4):
        return FORWARD_PLAN
    plan = []
    for s in range(stages):
        plan += [f"gather.{step}:{s}" for step in ("fill", "enter", "turn", "home", "column")]
        for k in range(depth):
            plan += [f"gather.cell:{s},{k}"] if k else []
            plan += [f"gather.passing:{s},{k}", f"gather.close:{s},{k}"]
        plan += [f"gather.done:{s}"]
        for layer in range(layers):
            if s == (layer + 1) * stages // layers - 1:
                plan += [f"compute.{step}:{layer}" for step in ("front_a", "front_b", "front_c", "mix")]
                plan += [f"compute.mlp:{layer},{i}" for i in range(4)]
    return plan


def forward_kernel(n_dp, n_fsdp, layers, *refs):
    (
        slots_ref, flag_ref, count_ref, master_in, tokens_in, gains_ref, table_in, back_in,
        w_ref, a_out, q_out, k_out, kh_out, vh_out, y_out, mixed_out, mid_out, b_out, g_out, u_out, h_out,
        total_out, state_out, act_out,
        master, held, acc, from_x, from_y, last_y, last_x,
        tok, state, table, back, wfront, wmlp, a, q, k, kh, vh, y, mixed, mid, b, g, u, h,
        part, by_z, by_d, mid_sum, total, send, recv, local,
    ) = refs
    place = Place(n_dp, n_fsdp)
    copies = Copies(send, recv, local)
    stores = Stores(copies)
    rows, width = state.shape
    load_master = copies.here(master_in, master)
    load_master.start()
    loads = [copies.here(*pair) for pair in ((tokens_in, tok), (table_in, table), (back_in, back))]
    for copy in loads:
        copy.start()
    place.greet_all()
    load_master.wait()
    gather = Gather(place, copies, slots_ref, master, w_ref, held, acc, from_x, from_y, last_y, last_x)
    sums = [
        RowSum(place, copies, *(ref.at[layer] for ref in (part, by_z, by_d, mid_sum, total)))
        for layer in range(layers)
    ]
    valid = valid_rows(rows, count_ref[0])
    lone = lone_rows(rows, flag_ref[0])
    spans = span_scale(rows, flag_ref[0])
    waiting = {}

    def fetch(name, blocks, targets):
        waiting[name] = [copies.here(w_ref.at[j], t) for j, t in zip(blocks, targets)]
        for copy in waiting[name]:
            copy.start()

    def fetched(name):
        for copy in waiting.pop(name):
            copy.wait()

    def front_a(layer):
        fetch("front", [16 * layer + i for i in range(4)], [wfront.at[i] for i in range(4)])
        if layer == 0:
            for copy in loads:
                copy.wait()
            state[...] = tok[...].astype(F32)
        stores.settle("a", "k", "q", "kh", "vh", "y")
        stores.out("state", state, state_out.at[layer])
        normed, _ = normalize(state[...])
        a[...] = (normed * gains_ref[2 * layer : 2 * layer + 1, :]).astype(LOW)
        stores.out("a", a, a_out.at[layer])
        part[layer] = jnp.broadcast_to(jnp.sum(valid), part.shape[1:])
        fetched("front")

        def keys(at):
            value = dot(a[...], wfront[2, :, at]) * valid
            k[:, at] = value
            part[layer, 0:1, at] = jnp.sum(value * value, 0, keepdims=True)

        columns(width, keys)
        sums[layer].start()
        stores.out("k", k, k_out.at[layer])

    def front_b(layer):
        def spectra(at):
            q[:, at] = dot(a[...], wfront[1, :, at])
            values = (dot(a[...], wfront[0, :, at]) * valid).astype(LOW)
            kh[:, at] = dot(table[...], k[:, at].astype(LOW)).astype(LOW)
            vh[:, at] = dot(table[...], values).astype(LOW)

        columns(width, spectra)
        stores.out("q", q, q_out.at[layer])
        stores.out("kh", kh, kh_out.at[layer])
        stores.out("vh", vh, vh_out.at[layer])
        sums[layer].turn()

    def front_c(layer):
        def product(at):
            kr, ki = kh[:rows, at].astype(F32), kh[rows:, at].astype(F32)
            vr, vi = vh[:rows, at].astype(F32), vh[rows:, at].astype(F32)
            cross = ki * vi
            real = kr * vr - jnp.where(lone, 0.0, cross)
            imag = jnp.where(lone, cross, kr * vi + ki * vr)
            y[:, at] = dot(back[:, :rows], real.astype(LOW)) + dot(
                back[:, rows:], imag.astype(LOW)
            )

        columns(width, product)
        stores.out("y", y, y_out.at[layer])

    def fetch_mlp(layer, i):
        first = 16 * layer + i
        fetch(("mlp", i), [first + 4, first + 8, first + 12], [wmlp.at[i % 2, j] for j in range(3)])

    def mix(layer):
        fetch_mlp(layer, 0)
        stores.settle("mixed", "mid", "b", "state")
        sums[layer].finish()
        stores.out("total", total.at[layer], total_out.at[layer])
        norm, _ = filter_norm_of(total.at[layer])
        mixed[...] = (y[...] * (spans / norm) * q[...]).astype(LOW)
        stores.out("mixed", mixed, mixed_out.at[layer])
        state[...] += dot(mixed[...], wfront[3])
        mid[...] = state[...]
        stores.out("mid", mid, mid_out.at[layer])
        normed, _ = normalize(state[...])
        b[...] = (normed * gains_ref[2 * layer + 1 : 2 * layer + 2, :]).astype(LOW)
        stores.out("b", b, b_out.at[layer])

    def mlp(layer, i):
        turn = i % 2
        fetched(("mlp", i))
        if i < 3:
            fetch_mlp(layer, i + 1)
        stores.settle(("g", turn))

        def body(at, turn=turn):
            gate = dot(b[...], wmlp[turn, 0, :, at])
            up = dot(b[...], wmlp[turn, 1, :, at])
            g[turn, :, at] = gate.astype(LOW)
            u[turn, :, at] = up.astype(LOW)
            h[turn, :, at] = (gate * jax.nn.sigmoid(gate) * up).astype(LOW)

        columns(width, body)
        for held_ref, out in ((g, g_out), (u, u_out), (h, h_out)):
            stores.out(("g", turn), held_ref.at[turn], out.at[layer, i])
        state[...] += dot(h[turn], wmlp[turn, 2])
        if i == 3 and layer == layers - 1:
            tok[...] = state[...].astype(LOW)
            stores.out("act", tok, act_out)

    compute = types.SimpleNamespace(
        front_a=front_a, front_b=front_b, front_c=front_c, mix=mix, mlp=mlp
    )
    run_plan(forward_plan(layers, gather.stages, n_fsdp), gather=gather, compute=compute)
    gather.drain()
    for one in sums:
        one.drain()
    stores.settle()


def forward(n_dp, n_fsdp, scalars, owner_slots, master, tokens, gains, tables):
    blocks = owner_slots.shape[0]
    layers = blocks // 16
    part_rows, cols = master.shape[1:]
    rows, width = tokens.shape
    stages = blocks // n_dp
    row = (rows, width)
    spectrum = (2 * rows, width)
    saved = [
        (row, LOW), (row, F32), (row, F32), (spectrum, LOW), (spectrum, LOW), (row, F32), (row, LOW), (row, F32), (row, LOW),
        ((4,) + row, LOW), ((4,) + row, LOW), ((4,) + row, LOW), ((8, width), F32), (row, F32),
    ]
    count = copy_count(n_dp, n_fsdp, stages, 1, n_fsdp, n_fsdp) + layers * (n_dp + n_fsdp - 2)
    any_space = pl.BlockSpec(memory_space=pl.ANY)
    scalar = pl.BlockSpec(memory_space=pltpu.SMEM)
    vmem = pl.BlockSpec(memory_space=pltpu.VMEM)
    return pl.pallas_call(
        functools.partial(forward_kernel, n_dp, n_fsdp, layers),
        name="forward",
        out_shape=[jax.ShapeDtypeStruct((blocks, width, width), LOW)]
        + [jax.ShapeDtypeStruct((layers,) + shape, kind) for shape, kind in saved]
        + [jax.ShapeDtypeStruct(row, LOW)],
        in_specs=[scalar] * 3 + [any_space, any_space, vmem, any_space, any_space],
        out_specs=[any_space] * (2 + len(saved)),
        scratch_shapes=[
            pltpu.VMEM(master.shape, F32),
            pltpu.VMEM((stages, 2, n_dp // 4, part_rows, cols), LOW),
            pltpu.VMEM((stages, 2, n_dp // 4, part_rows, cols), LOW),
        ]
        + plane_sum_shapes(n_dp, (stages,), part_rows, cols)
        + [
            pltpu.VMEM(row, LOW),
            pltpu.VMEM(row, F32),
            pltpu.VMEM(tables[0].shape, LOW),
            pltpu.VMEM(tables[1].shape, LOW),
            pltpu.VMEM((4, width, width), LOW),
            pltpu.VMEM((2, 3, width, width), LOW),
        ]
        + [pltpu.VMEM(shape, kind) for shape, kind in saved[:9]]
        + [pltpu.VMEM((2,) + row, LOW)] * 3
        + [
            pltpu.VMEM((layers, 8, width), F32),
            pltpu.VMEM((layers, n_fsdp, 8, width), F32),
            pltpu.VMEM((layers, n_dp, 8, width), F32),
            pltpu.VMEM((layers, 8, width), F32),
            pltpu.VMEM((layers, 8, width), F32),
            pltpu.SemaphoreType.DMA((count,)),
            pltpu.SemaphoreType.DMA((count,)),
            pltpu.SemaphoreType.DMA((stages + 8 + layers * 48,)),
        ],
        compiler_params=pltpu.CompilerParams(
            collective_id=0, has_side_effects=True, vmem_limit_bytes=VMEM_BYTES
        ),
    )(owner_slots, *scalars, master, tokens, gains, *tables)


class Scatter:
    def __init__(self, place, copies, stores, order, grads, landed, out_ref, acc, aside, from_a, from_b, credits, *sum_refs):
        self.place, self.copies, self.stores, self.order = place, copies, stores, order
        self.grads, self.landed, self.out_ref = grads, landed, out_ref
        self.acc, self.aside, self.from_a, self.from_b = acc, aside, from_a, from_b
        self.credits = credits
        self.slots, self.size = acc.shape[0], acc.shape[-2]
        self.rows = self.size // place.depth
        self.late = from_b.shape[-2]
        self.early = self.rows - self.late
        self.spots = place.up * place.across
        self.stages = len(order)
        self.sums = [
            [
                PlaneSum(
                    place, copies, acc.at[n % self.slots],
                    self.window(place.z_at(k), 0, self.early if k else self.rows),
                    self.early if k else self.rows,
                    *(ref.at[n % self.slots, k] for ref in sum_refs),
                )
                for k in range(place.depth)
            ]
            for n in range(self.stages)
        ]
        whole = pl.ds(0, self.rows)
        self.spreads = [PlaneSpread(place, copies, place.n_dp * s, out_ref, whole) for s in order]
        self.over = [None] * self.stages
        self.along_a = [{} for _ in order]
        self.along_b = [[] for _ in order]

    def window(self, z, first, count):
        return pl.ds(pl.multiple_of(z * self.rows + first, 16), count)

    def near(self):
        p = self.place
        peers = [(p.dp(x=p.x_at(k)), p.z) for k in range(1, p.across)]
        return peers + [(p.dp(y=p.y_at(m)), p.z) for m in range(1, p.up)]

    def column(self):
        p = self.place
        return [(p.d, p.z_at(k)) for k in range(1, p.depth)]

    def free(self, n, kind, peers):
        if n + self.slots < self.stages:
            for peer in peers:
                pl.semaphore_signal(
                    self.credits.at[kind, n], inc=1, device_id=peer, device_id_type=MESH
                )

    def claim(self, n, kind, peers):
        if n >= self.slots:
            pl.semaphore_wait(self.credits.at[kind, n - self.slots], len(peers))

    def grad(self, n, spot, core):
        return self.grads.at[self.place.n_dp * self.order[n] + 2 * spot + core]

    def offer(self, n):
        p = self.place
        self.stores.settle("outs")
        self.over[n] = [
            self.copies.to(
                self.grad(n, spot, 1 - p.core),
                self.landed.at[n * self.spots + spot],
                p.dp(core=1 - p.core),
                p.z,
            )
            for spot in range(self.spots)
        ]
        for copy in self.over[n]:
            copy.start()

    def sent(self, n):
        for one in self.sums[n]:
            one.drain()
        for copy in list(self.along_a[n].values()) + self.along_b[n]:
            copy.wait_send()

    def enter(self, n):
        p, slot = self.place, n % self.slots
        if n >= self.slots:
            self.sent(n - self.slots)
        targets = [self.acc.at[slot, i // p.across, i % p.across] for i in range(self.spots)]
        own = [self.copies.here(self.grad(n, i, p.core), targets[i]) for i in range(self.spots)]
        other = [
            self.copies.here(self.landed.at[n * self.spots + i], self.aside.at[i % 2])
            for i in range(self.spots)
        ]
        for copy in own:
            copy.start()
        for i in range(min(2, self.spots)):
            self.over[n][i].wait_recv()
            other[i].start()
        for i in range(self.spots):
            own[i].wait()
            other[i].wait()
            add_into(targets[i], [self.aside.at[i % 2]], self.size)
            if i + 2 < self.spots:
                self.over[n][i + 2].wait_recv()
                other[i + 2].start()
        self.claim(n, 0, self.near())
        self.claim(n, 1, self.column())
        for k in range(1, p.depth):
            source = self.acc.at[slot, :, :, self.window(p.z_at(k), self.early, self.late), :]
            self.along_b[n].append(
                self.copies.to(source, self.from_b.at[slot, k - 1], p.d, p.z_at(k))
            )
        for copy in self.along_b[n]:
            copy.start()

    def push(self, n, k):
        p, slot = self.place, n % self.slots
        if k == 0:
            for copy in self.along_b[n]:
                copy.wait_recv()
            window = self.window(p.z, self.early, self.late)
            for y in range(p.up):
                for x in range(p.across):
                    terms = [self.from_b.at[slot, i, y, x] for i in range(p.depth - 1)]
                    add_into(self.acc.at[slot, y, x, window, :], terms, self.late)
        self.sums[n][k].start()

    def turn(self, n, k):
        self.sums[n][k].turn()

    def home(self, n, k):
        p, slot = self.place, n % self.slots
        self.sums[n][k].finish()
        if k > 0:
            source = self.acc.at[slot, p.y, p.x, self.window(p.z_at(k), 0, self.early), :]
            self.along_a[n][k] = self.copies.to(
                source, self.from_a.at[slot, k - 1], p.d, p.z_at(k)
            )
            self.along_a[n][k].start()

    def total(self, n):
        p, slot = self.place, n % self.slots
        self.free(n, 0, self.near())
        for copy in self.along_a[n].values():
            copy.wait_recv()
        terms = [self.from_a.at[slot, k - 1] for k in range(1, p.depth)]
        add_into(self.acc.at[slot, p.y, p.x, self.window(p.z, 0, self.early), :], terms, self.early)
        self.free(n, 1, self.column())
        total = self.acc.at[slot, p.y, p.x, self.window(p.z, 0, self.rows), :]
        kept = self.copies.here(total, self.out_ref.at[p.n_dp * self.order[n] + p.d])
        kept.start()
        kept.wait()
        self.spreads[n].start()

    def passing(self, n):
        self.spreads[n].forward()

    def close(self, n):
        self.spreads[n].finish()

    def done(self, n):
        self.spreads[n].arrived()

    def drain(self):
        for n in range(self.stages):
            for copy in self.over[n]:
                copy.wait_send()
            if n + self.slots >= self.stages:
                self.sent(n)
            self.spreads[n].drain()


def backward_plan(layers, stages, depth):
    if (layers, stages, depth) == (2, 4, 4):
        return BACKWARD_PLAN
    plan = []
    for layer in reversed(range(layers)):
        plan += [f"compute.mlp:{layer},{i}" for i in range(4)]
        plan += [f"compute.{step}:{layer}" for step in ("mix_a", "mix_b", "front_a", "front_b")]
    plan += [f"scatter.offer:{n}" for n in range(stages)]
    for n in range(stages):
        plan += [f"scatter.enter:{n}"]
        for k in list(range(1, depth)) + [0]:
            plan += [f"scatter.{step}:{n},{k}" for step in ("push", "turn", "home")]
        plan += [f"scatter.{step}:{n}" for step in ("total", "passing", "close", "done")]
    return plan


def backward_kernel(n_dp, n_fsdp, layers, *refs):
    (
        flag_ref, count_ref, cotangent, w_ref, gains_ref, table_in, back_in,
        a_in, q_in, k_in, kh_in, vh_in, y_in, mixed_in, mid_in, b_in, g_in, u_in, h_in, total_in, state_in,
        red_ref, grad_out, gain_total, grads_ref, landed_ref,
        acc, from_x, from_y, last_y, last_x, from_a, from_b, aside,
        table, back, weights, tiles, outs, grad, sums, mid, q, y, low, b, mixed, dv, dq, dk,
        totals, part, by_z, by_d, mid_sum, total, send, recv, local, credits,
    ) = refs
    place = Place(n_dp, n_fsdp)
    copies = Copies(send, recv, local)
    stores = Stores(copies)
    rows, width = grad.shape
    valid = valid_rows(rows, count_ref[0])
    lone = lone_rows(rows, flag_ref[0])
    spans = span_scale(rows, flag_ref[0])
    waiting = {}

    def fetch(name, *pairs):
        waiting[name] = [copies.here(*pair) for pair in pairs]
        for copy in waiting[name]:
            copy.start()

    def fetched(*names):
        for name in names:
            for copy in waiting.pop(name):
                copy.wait()

    def fetch_mlp(layer, i):
        first, turn = 16 * layer + i, i % 2
        fetch(
            ("mlp", i),
            *[(w_ref.at[first + 4 * (j + 1)], weights.at[3 * turn + j]) for j in range(3)],
            *[(ref.at[layer, i], tiles.at[turn, j]) for j, ref in enumerate((g_in, u_in, h_in))],
        )

    fetch("cotangent", (cotangent, grad))
    fetch("b", (b_in.at[layers - 1], b))
    fetch_mlp(layers - 1, 0)
    fetch("tables", (table_in, table), (back_in, back))
    fetch("totals", (total_in, totals))
    place.greet_all()
    order = list(reversed(range(layers * 16 // n_dp)))
    scatter = Scatter(
        place, copies, stores, order, grads_ref, landed_ref, red_ref, acc, aside, from_a, from_b, credits, from_x, from_y, last_y, last_x
    )
    row_sums = [
        RowSum(place, copies, *(ref.at[i] for ref in (part, by_z, by_d, mid_sum, total)))
        for i in range(layers + 1)
    ]
    part[layers] = jnp.zeros(part.shape[1:], F32)

    def begin(layer):
        if layer == layers - 1:
            fetched("cotangent")
            grad[...] = grad[...] * valid
        low[...] = grad[...].astype(LOW)
        sums[...] = jnp.zeros_like(sums)
        fetch("mid", (mid_in.at[layer], mid))
        fetch("mix", (q_in.at[layer], q), (y_in.at[layer], y), (mixed_in.at[layer], mixed))
        fetched("b")

    def mlp(layer, i):
        turn, first = i % 2, 16 * layer + i
        if i == 0:
            begin(layer)
        fetched(("mlp", i))
        if i < 3:
            fetch_mlp(layer, i + 1)
        else:
            first_two = [(16 * layer + 3, 0), (16 * layer, 1), (16 * layer + 1, 2)]
            fetch("front", *[(w_ref.at[j], weights.at[to]) for j, to in first_two])
            fetch("kh", *[(kh_in.at[layer, pl.ds(rows * j, rows)], tiles.at[0, j]) for j in range(2)])
        stores.settle("outs")
        gate_w, up_w, down_w = (weights.at[3 * turn + j] for j in range(3))

        def body(at):
            dhidden = dot_nt(low[...], down_w[at, :])
            gate = tiles[turn, 0, :, at].astype(F32)
            up = tiles[turn, 1, :, at].astype(F32)
            sig = jax.nn.sigmoid(gate)
            dup = (dhidden * gate * sig).astype(LOW)
            dgate = (dhidden * up * sig * (1.0 + gate * (1.0 - sig))).astype(LOW)
            outs[2, at, :] = dot_tn(tiles[turn, 2, :, at], low[...]).astype(LOW)
            outs[0, :, at] = dot_tn(b[...], dgate).astype(LOW)
            outs[1, :, at] = dot_tn(b[...], dup).astype(LOW)
            sums[...] += dot_nt(dgate, gate_w[:, at]) + dot_nt(dup, up_w[:, at])

        columns(width, body)
        for j in range(3):
            block = first + 4 * (j + 1)
            stores.out("outs", outs.at[j], grads_ref.at[block])
        if i == 3:
            fetch("key", (w_ref.at[16 * layer + 2], weights.at[3]))
            fetch("vh", *[(vh_in.at[layer, pl.ds(rows * j, rows)], tiles.at[1, j]) for j in range(2)])
            fetch("a", (a_in.at[layer], b))

    def mix_a(layer):
        if layer == layers - 1:
            fetched("tables", "totals")
        fetched("mid")
        normed, rstd = normalize(mid[...])
        db = sums[...]
        part[layers, 2 * layer + 1 : 2 * layer + 2, :] = jnp.sum(db * normed, 0, keepdims=True)
        gain = gains_ref[2 * layer + 1 : 2 * layer + 2, :]
        grad[...] += norm_back(db * gain, normed, rstd)
        low[...] = grad[...].astype(LOW)
        fetch("k", (k_in.at[layer], mid))
        norm, _ = filter_norm_of(totals.at[layer])
        scale_row = spans / norm
        sums[0:1, :] = scale_row
        part[layer] = jnp.zeros(part.shape[1:], F32)
        fetched("mix", "front", "kh", "vh")

        def through(at):
            dmixed = dot_nt(low[...], weights[0, at, :])
            dq[:, at] = (dmixed * y[:, at] * sums[0:1, at]).astype(LOW)
            dy = dmixed * q[:, at]
            part[layer, 0:1, at] = jnp.sum(dy * y[:, at], 0, keepdims=True) * spans
            q[:, at] = dy

        columns(width, through)
        row_sums[layer].start()

    def mix_b(layer):
        def body(at):
            dh = dot(table[...], q[:, at].astype(LOW))
            dr, di = dh[:rows], dh[rows:]

            def against(turn):
                other_r = tiles[turn, 0, :, at].astype(F32)
                other_i = tiles[turn, 1, :, at].astype(F32)
                cross = di * other_i
                real = dr * other_r + jnp.where(lone, 0.0, cross)
                imag = jnp.where(lone, cross, di * other_r - dr * other_i)
                return dot(back[:, :rows], real.astype(LOW)) + dot(
                    back[:, rows:], imag.astype(LOW)
                )

            y[:, at] = against(1)
            dv[:, at] = (against(0) * sums[0:1, at] * valid).astype(LOW)

        columns(width, body)
        fetch("state", (state_in.at[layer], q))
        row_sums[layer].turn()

    def front_a(layer):
        fetched("a", "key")
        if layer > 0:
            fetch_mlp_tiles(layer - 1)
        stores.settle("outs")

        def body(at):
            outs[3, at, :] = dot_tn(mixed[:, at], low[...]).astype(LOW)
            outs[0, :, at] = dot_tn(b[...], dv[:, at]).astype(LOW)
            outs[1, :, at] = dot_tn(b[...], dq[:, at]).astype(LOW)

        columns(width, body)
        sums[...] = dot_nt(dv[...], weights[1]) + dot_nt(dq[...], weights[2])

    def front_b(layer):
        fetched("k")
        row_sums[layer].finish()
        norm, live = filter_norm_of(totals.at[layer])
        square = -total[layer, 0:1, :] / (norm * norm) / (2.0 * norm * live)
        dk[...] = ((y[...] * (spans / norm) + 2.0 * mid[...] * square) * valid).astype(LOW)

        def keys(at):
            outs[2, :, at] = dot_tn(b[...], dk[:, at]).astype(LOW)

        columns(width, keys)
        for j in range(4):
            stores.out("outs", outs.at[j], grads_ref.at[16 * layer + j])
        sums[...] += dot_nt(dk[...], weights[3])
        if layer > 0:
            fetch("b", (b_in.at[layer - 1], b))
            fetch_mlp_weights(layer - 1)
        fetched("state")
        da = sums[...]
        normed, rstd = normalize(q[...])
        part[layers, 2 * layer : 2 * layer + 1, :] = jnp.sum(da * normed, 0, keepdims=True)
        gain = gains_ref[2 * layer : 2 * layer + 1, :]
        grad[...] += norm_back(da * gain, normed, rstd)
        if layer == 0:
            stores.out("grad", grad, grad_out)
            row_sums[layers].start()

    def fetch_mlp_tiles(layer):
        fetch(
            "tiles", *[(ref.at[layer, 0], tiles.at[0, j]) for j, ref in enumerate((g_in, u_in, h_in))]
        )

    def fetch_mlp_weights(layer):
        fetch("weights", *[(w_ref.at[16 * layer + 4 * (j + 1)], weights.at[j]) for j in range(3)])
        waiting[("mlp", 0)] = waiting.pop("tiles") + waiting.pop("weights")

    compute = types.SimpleNamespace(
        mlp=mlp, mix_a=mix_a, mix_b=mix_b, front_a=front_a, front_b=front_b
    )
    run_plan(backward_plan(layers, scatter.stages, n_fsdp), scatter=scatter, compute=compute)
    row_sums[layers].turn()
    row_sums[layers].finish()
    gain_total[...] = total[layers]
    scatter.drain()
    for one in row_sums:
        one.drain()
    stores.settle()


def backward(n_dp, n_fsdp, scalars, cotangent, weights, gains, tables, saved):
    blocks, width, _ = weights.shape
    layers = blocks // 16
    rows = cotangent.shape[0]
    stages = blocks // n_dp
    spots = n_dp // 2
    slots = 2 if n_dp == 8 else 1
    part_rows = width // n_fsdp
    row = (rows, width)
    late = max(16, part_rows // 6 // 16 * 16)
    spread_count = spots + 2 * (n_fsdp - 1)
    count = copy_count(n_dp, n_fsdp, stages, n_fsdp, 1, spread_count)
    count += (layers + 1) * (n_dp + n_fsdp - 2)
    any_space = pl.BlockSpec(memory_space=pl.ANY)
    scalar = pl.BlockSpec(memory_space=pltpu.SMEM)
    vmem = pl.BlockSpec(memory_space=pltpu.VMEM)
    return pl.pallas_call(
        functools.partial(backward_kernel, n_dp, n_fsdp, layers),
        name="backward",
        out_shape=[
            jax.ShapeDtypeStruct((blocks, part_rows, width), LOW),
            jax.ShapeDtypeStruct(row, F32),
            jax.ShapeDtypeStruct((8, width), F32),
            jax.ShapeDtypeStruct((blocks, width, width), LOW),
            jax.ShapeDtypeStruct((blocks // 2, width, width), LOW),
        ],
        in_specs=[scalar, scalar, any_space, any_space, vmem] + [any_space] * (2 + len(saved)),
        out_specs=[any_space, any_space, vmem, any_space, any_space],
        scratch_shapes=[pltpu.VMEM((slots, 2, n_dp // 4, width, width), LOW)]
        + plane_sum_shapes(n_dp, (slots, n_fsdp), part_rows, width)
        + [
            pltpu.VMEM((slots, n_fsdp - 1, part_rows - late, width), LOW),
            pltpu.VMEM((slots, n_fsdp - 1, 2, n_dp // 4, late, width), LOW),
            pltpu.VMEM((2, width, width), LOW),
            pltpu.VMEM(tables[0].shape, LOW),
            pltpu.VMEM(tables[1].shape, LOW),
            pltpu.VMEM((6, width, width), LOW),
            pltpu.VMEM((2, 3) + row, LOW),
            pltpu.VMEM((4, width, width), LOW),
        ]
        + [pltpu.VMEM(row, F32)] * 5
        + [pltpu.VMEM(row, LOW)] * 6
        + [
            pltpu.VMEM((layers, 8, width), F32),
            pltpu.VMEM((layers + 1, 8, width), F32),
            pltpu.VMEM((layers + 1, n_fsdp, 8, width), F32),
            pltpu.VMEM((layers + 1, n_dp, 8, width), F32),
            pltpu.VMEM((layers + 1, 8, width), F32),
            pltpu.VMEM((layers + 1, 8, width), F32),
            pltpu.SemaphoreType.DMA((count,)),
            pltpu.SemaphoreType.DMA((count,)),
            pltpu.SemaphoreType.DMA((stages * (2 * spots + 1) + layers * 64 + 16,)),
            pltpu.SemaphoreType.REGULAR((2, stages)),
        ],
        compiler_params=pltpu.CompilerParams(
            collective_id=1, has_side_effects=True, vmem_limit_bytes=VMEM_BYTES
        ),
    )(*scalars, cotangent, weights, gains, *tables, *saved)


def call(kernel, name, grid, scalars, args, specs, outs, out_specs, scratch=()):
    return pl.pallas_call(
        kernel,
        name=name,
        out_shape=outs,
        grid_spec=pltpu.PrefetchScalarGridSpec(
            num_scalar_prefetch=len(scalars),
            grid=(grid,),
            in_specs=specs,
            out_specs=out_specs,
            scratch_shapes=scratch,
        ),
        compiler_params=pltpu.CompilerParams(vmem_limit_bytes=VMEM_BYTES),
    )(*scalars, *args)


def adam_step(grad, first, second, weight, rate, decay):
    first_out = 0.5 * first + 0.5 * grad
    second_out = 0.5 * second + 0.5 * grad * grad
    corr = 1.0 - 0.5**STEP
    weight_out = weight - rate * (
        first_out / corr / (jnp.sqrt(second_out / corr) + ADAM_EPS) + decay * weight
    )
    return (first_out, second_out, weight_out)


def adam_kernel(
    block, used, grad_ref, master_ref, first_ref, second_ref, first_out, second_out, master_out
):
    taken = used[pl.program_id(0)] == 1
    first, second, master = first_ref[...], second_ref[...], master_ref[...]
    new = adam_step(grad_ref[...].astype(F32), first, second, master, 0.03, 0.01)
    first_out[...] = jnp.where(taken, new[0], first)
    second_out[...] = jnp.where(taken, new[1], second)
    master_out[...] = jnp.where(taken, new[2], master)


def adam_blocks(block, used, grads, master, first, second):
    shape = (1,) + master.shape[1:]
    own = pl.BlockSpec(shape, lambda i, block, used: (i, 0, 0))
    picked = pl.BlockSpec(shape, lambda i, block, used: (block[i], 0, 0))
    return call(
        adam_kernel,
        "adam",
        master.shape[0],
        (block, used),
        (grads, master, first, second),
        [picked, own, own, own],
        [jax.ShapeDtypeStruct(master.shape, F32)] * 3,
        [own] * 3,
    )


def on_device(
    n_dp,
    n_fsdp,
    tokens,
    cotangent,
    row_counts,
    bucket_flags,
    owner_slots,
    master,
    first_moment,
    second_moment,
    gains,
    gain_first,
    gain_second,
):
    rows = tokens.shape[0]
    slot_cap = master.shape[0]
    layers = owner_slots.shape[0] // 16
    tables = transform_tables(rows)
    scalars = (bucket_flags, row_counts)
    picked = [lax.dynamic_index_in_dim(t, bucket_flags[0], 0, keepdims=False) for t in tables]
    weights, *saved, activations = forward(
        n_dp, n_fsdp, scalars, owner_slots, master, tokens, gains, picked
    )
    summed, grad, gain_sums, _, _ = backward(
        n_dp, n_fsdp, scalars, cotangent, weights, gains, picked, saved
    )
    gains_total = gain_sums[: 2 * layers]
    my_slots = lax.axis_index("dp") * slot_cap + jnp.arange(slot_cap, dtype=jnp.int32)
    hits = owner_slots[None, :] == my_slots[:, None]
    used = jnp.any(hits, 1).astype(jnp.int32)
    block = jnp.sum(jnp.where(hits, jnp.arange(owner_slots.shape[0], dtype=jnp.int32)[None, :], 0), 1)
    first_out, second_out, master_out = adam_blocks(
        block, used, summed, master, first_moment, second_moment
    )
    gain_m, gain_v, gain_w = adam_step(gains_total, gain_first, gain_second, gains, 0.2, 0.0)
    return (activations, grad, first_out, second_out, master_out, gain_m, gain_v, gain_w)


def solution(mesh):
    rows = P(("dp", "fsdp"), None)
    blocks = P("dp", "fsdp", None)
    flat = P(("dp", "fsdp"))
    return jax.shard_map(
        functools.partial(on_device, mesh.shape["dp"], mesh.shape["fsdp"]),
        mesh=mesh,
        in_specs=(rows, rows, flat, flat, P(), blocks, blocks, blocks, P(), P(), P()),
        out_specs=(rows, rows, blocks, blocks, blocks, P(), P(), P()),
        check_vma=False,
    )
```

```python
import functools
import math
import types

import jax
import jax.numpy as jnp
import numpy as np
from jax import lax
from jax.experimental import pallas as pl
from jax.experimental.pallas import tpu as pltpu
from jax.sharding import PartitionSpec as P

STEP = 5
NORM_EPS = 1e-05
ADAM_EPS = 1e-08
LOW = jnp.bfloat16
F32 = jnp.float32
MESH = pl.DeviceIdType.MESH
VMEM_BYTES = 60 * 2**20


FORWARD_STEPS = (
    ("fill", 1), ("enter", 1), ("turn", 1), ("home", 1), ("column", 1), ("cell", 2), ("passing", 2),
    ("close", 2), ("late", 1), ("share", 1), ("done", 1), ("front_a", 1), ("front_b", 1), ("sum_turn", 1),
    ("front_c", 1), ("mix", 1), ("load", 1), ("mlp", 2),
)
FORWARD_ORDER = (
    0, 10, 100, 20, 110, 200, 120, 300, 400, 501, 600, 210, 700, 800, 601, 30, 503, 310, 701, 410, 502, 603,
    900, 602, 220, 610, 130, 703, 710, 512, 702, 810, 320, 230, 1000, 420, 612, 620, 513, 330, 720, 521, 511,
    1100, 522, 1200, 820, 430, 1300, 611, 712, 613, 1400, 630, 523, 622, 621, 1500, 711, 920, 910, 623, 713,
    730, 531, 721, 1010, 1600, 723, 1700, 830, 532, 722, 1701, 1702, 631, 1703, 533, 1020, 1110, 632, 731,
    1210, 633, 1410, 732, 1310, 930, 733, 1510, 1030, 1610, 1710, 1711, 1712, 1713,
)
BACKWARD_STEPS = (
    ("mlp", 2), ("mix_a", 1), ("mix_b", 1), ("sum_turn", 1), ("front_a", 1), ("front_b", 1), ("gain_turn", 1),
    ("offer", 1), ("enter", 1), ("push", 2), ("turn", 2), ("home", 2), ("total", 1), ("passing", 1),
    ("close", 1), ("done", 1),
)
BACKWARD_ORDER = (
    10, 11, 12, 13, 700, 110, 210, 310, 410, 800, 902, 901, 510, 710, 0, 1002, 903, 1, 1001, 810, 911, 2, 912,
    1003, 3, 1012, 100, 913, 1101, 1103, 900, 200, 720, 1011, 300, 1013, 1102, 1000, 910, 400, 1113, 1100,
    1111, 1112, 1200, 820, 922, 500, 921, 1010, 1021, 923, 1300, 730, 1110, 1210, 1121, 1022, 1023, 830, 1400,
    931, 933, 1031, 932, 1123, 1122, 1131, 920, 1032, 1020, 930, 1132, 1033, 1310, 1120, 1030, 1220, 1133,
    1130, 1230, 1320, 1410, 1330, 1420, 600, 1430, 1500, 1510, 1520, 1530,
)


def span_tables(length):
    period = 2 * length
    freqs = np.arange(length)[:, None]
    places = np.arange(length)[None, :]
    angle = (freqs * places % period) * (2.0 * math.pi / period)
    cosine, sine = np.cos(angle), -np.sin(angle)
    sine[0] = np.cos(math.pi * np.arange(length))
    weight = np.where(np.arange(length) == 0, 1.0, 2.0)[None, :] / period
    return (cosine, sine, cosine.T * weight, sine.T * weight)


def transform_tables(rows):
    short = [np.kron(np.eye(4), table) for table in span_tables(rows // 4)]
    full = span_tables(rows)
    forward = np.stack([np.concatenate(t[:2], 0) for t in (short, full)])
    inverse = np.stack([np.concatenate(t[2:], 1) for t in (short, full)])
    return (jnp.asarray(forward, LOW), jnp.asarray(inverse, LOW))


class Place:
    def __init__(self, n_dp, n_fsdp):
        self.n_dp, self.depth = n_dp, n_fsdp
        self.up, self.across = 2, n_dp // 4
        self.d = lax.axis_index("dp")
        self.z = lax.axis_index("fsdp")
        self.core = lax.rem(self.d, 2)
        self.x = lax.rem(self.d // 2, self.across)
        self.y = self.d // (2 * self.across)

    def x_at(self, k):
        return lax.rem(self.x + k + self.across, self.across)

    def y_at(self, m):
        return lax.rem(self.y + m + self.up, self.up)

    def z_at(self, k):
        return lax.rem(self.z + k + self.depth, self.depth)

    def dp(self, y=None, x=None, core=None):
        y = self.y if y is None else y
        x = self.x if x is None else x
        core = self.core if core is None else core
        return (y * self.across + x) * 2 + core

    def greet(self):
        barrier = pltpu.get_barrier_semaphore()
        peers = [(self.dp(core=1 - self.core), self.z)]
        peers += [(self.dp(x=self.x_at(k)), self.z) for k in range(1, self.across)]
        peers += [(self.dp(y=self.y_at(m)), self.z) for m in range(1, self.up)]
        peers += [(self.d, self.z_at(k)) for k in range(1, self.depth)]
        for peer in peers:
            pl.semaphore_signal(barrier, inc=1, device_id=peer, device_id_type=MESH)
        pl.semaphore_wait(barrier, len(peers))

    def greet_all(self):
        barrier = pltpu.get_barrier_semaphore()
        peers = [(lax.rem(self.d + k, self.n_dp), self.z) for k in range(1, self.n_dp)]
        peers += [(self.d, self.z_at(k)) for k in range(1, self.depth)]
        for peer in peers:
            pl.semaphore_signal(barrier, inc=1, device_id=peer, device_id_type=MESH)
        pl.semaphore_wait(barrier, len(peers))


class Copies:
    def __init__(self, send, recv, local):
        self.send, self.recv, self.local = send, recv, local
        self.sent, self.moved = 0, 0

    def to(self, source, target, dp, z):
        index = self.sent
        self.sent += 1
        return pltpu.make_async_remote_copy(
            src_ref=source,
            dst_ref=target,
            send_sem=self.send.at[index],
            recv_sem=self.recv.at[index],
            device_id=(dp, z),
            device_id_type=MESH,
        )

    def here(self, source, target):
        index = self.moved
        self.moved += 1
        return pltpu.make_async_copy(source, target, self.local.at[index])


def add_into(total, terms, rows):
    step = next(size for size in (48, 32, 16) if rows % size == 0)

    def piece(i, carry):
        at = pl.ds(pl.multiple_of(i * step, 16), step)
        value = total[at, :].astype(F32)
        for term in terms:
            value = value + term[at, :].astype(F32)
        total[at, :] = value.astype(LOW)
        return carry

    lax.fori_loop(0, rows // step, piece, 0)


class PlaneSum:
    def __init__(self, place, copies, acc, window, count, from_x, from_y, last_y, last_x):
        self.place, self.copies, self.acc, self.window, self.count = place, copies, acc, window, count
        self.from_x, self.from_y, self.last_y, self.last_x = from_x, from_y, last_y, last_x
        half = acc.shape[-1] // 2
        self.first, self.second = pl.ds(0, half), pl.ds(half, half)
        self.rows = pl.ds(0, count)

    def start(self):
        p, rows = self.place, self.rows
        self.one = []
        for k in range(1, p.across):
            source = self.acc.at[:, p.x_at(k), self.window, self.first]
            target = self.from_x.at[k - 1, :, rows]
            self.one.append(self.copies.to(source, target, p.dp(x=p.x_at(k)), p.z))
        for m in range(1, p.up):
            source = self.acc.at[p.y_at(m), :, self.window, self.second]
            target = self.from_y.at[m - 1, :, rows]
            self.one.append(self.copies.to(source, target, p.dp(y=p.y_at(m)), p.z))
        for copy in self.one:
            copy.start()

    def turn(self):
        p, rows = self.place, self.rows
        for copy in self.one:
            copy.wait_recv()
        for y in range(p.up):
            terms = [self.from_x.at[k - 1, y, rows] for k in range(1, p.across)]
            add_into(self.acc.at[y, p.x, self.window, self.first], terms, self.count)
        for x in range(p.across):
            terms = [self.from_y.at[m - 1, x, rows] for m in range(1, p.up)]
            add_into(self.acc.at[p.y, x, self.window, self.second], terms, self.count)
        self.two = []
        for m in range(1, p.up):
            source = self.acc.at[p.y_at(m), p.x, self.window, self.first]
            target = self.last_y.at[m - 1, rows]
            self.two.append(self.copies.to(source, target, p.dp(y=p.y_at(m)), p.z))
        for k in range(1, p.across):
            source = self.acc.at[p.y, p.x_at(k), self.window, self.second]
            target = self.last_x.at[k - 1, rows]
            self.two.append(self.copies.to(source, target, p.dp(x=p.x_at(k)), p.z))
        for copy in self.two:
            copy.start()

    def finish(self):
        p, rows = self.place, self.rows
        for copy in self.two:
            copy.wait_recv()
        terms = [self.last_y.at[m - 1, rows] for m in range(1, p.up)]
        add_into(self.acc.at[p.y, p.x, self.window, self.first], terms, self.count)
        terms = [self.last_x.at[k - 1, rows] for k in range(1, p.across)]
        add_into(self.acc.at[p.y, p.x, self.window, self.second], terms, self.count)

    def drain(self):
        for copy in self.one + self.two:
            copy.wait_send()


class PlaneSpread:
    def __init__(self, place, copies, array, window, source=None):
        self.place, self.copies, self.array = place, copies, array
        self.window, self.source = window, source
        half = array.shape[-1] // 2
        self.halves = (pl.ds(0, half), pl.ds(half, half))
        self.sends = []

    def block(self, half=None, y=None, x=None):
        p = self.place
        y, x = p.y if y is None else y, p.x if x is None else x
        view = self.array.at[y * p.across + x, p.core, self.window]
        return view if half is None else view.at[:, self.halves[half]]

    def fire(self, ref, dp, source=None):
        copy = self.copies.to(ref if source is None else source, ref, dp, self.place.z)
        copy.start()
        self.sends.append(copy)
        return copy

    def start(self):
        p, own = self.place, self.block()
        self.by_x = [self.fire(own, p.dp(x=p.x_at(k)), self.source) for k in range(1, p.across)]
        self.by_y = [self.fire(own, p.dp(y=p.y_at(m)), self.source) for m in range(1, p.up)]

    def forward(self):
        p = self.place
        self.last = []
        for k in range(1, p.across):
            self.by_x[k - 1].wait_recv()
            for m in range(1, p.up):
                self.last.append(self.fire(self.block(0, x=p.x_at(-k)), p.dp(y=p.y_at(m))))
        for m in range(1, p.up):
            self.by_y[m - 1].wait_recv()
            for k in range(1, p.across):
                self.last.append(self.fire(self.block(1, y=p.y_at(-m)), p.dp(x=p.x_at(k))))

    def finish(self):
        for copy in self.last:
            copy.wait_recv()
        self.hand_over(self.window)

    def hand_over(self, window):
        p = self.place
        self.over = self.fire(self.array.at[:, p.core, window], p.dp(core=1 - p.core))

    def arrived(self):
        self.over.wait_recv()

    def drain(self):
        for copy in self.sends:
            copy.wait_send()


def plane_sum_shapes(n_dp, lead, rows, cols):
    up, across, half = 2, n_dp // 4, cols // 2
    return [
        pltpu.VMEM(lead + (across - 1, up, rows, half), LOW),
        pltpu.VMEM(lead + (up - 1, across, rows, half), LOW),
        pltpu.VMEM(lead + (up - 1, rows, half), LOW),
        pltpu.VMEM(lead + (across - 1, rows, half), LOW),
    ]


def copy_count(n_dp, n_fsdp, stages, sums, spreads, others):
    up, across = 2, n_dp // 4
    near = up - 1 + across - 1
    diagonal = (up - 1) * (across - 1)
    each_spread = near + 2 * diagonal + 1
    return stages * (sums * 2 * near + spreads * each_spread + others)


def run_plan(plan, *actors):
    for name, *where in plan:
        actor = next(a for a in actors if hasattr(a, name))
        getattr(actor, name)(*where)


def decode(steps, codes):
    plan = []
    for code in codes:
        name, count = steps[code // 100]
        plan.append((name, code // 10 % 10, code % 10)[: count + 1])
    return plan


def dot(left, right):
    return jnp.dot(left, right, preferred_element_type=F32)


def dot_nt(left, right):
    return lax.dot_general(left, right, (((1,), (1,)), ((), ())), preferred_element_type=F32)


def dot_tn(left, right):
    return lax.dot_general(left, right, (((0,), (0,)), ((), ())), preferred_element_type=F32)


def normalize(inputs):
    centred = inputs - jnp.mean(inputs, -1, keepdims=True)
    rstd = lax.rsqrt(jnp.mean(centred * centred, -1, keepdims=True) + NORM_EPS)
    return (centred * rstd, rstd)


def norm_back(grad, normed, rstd):
    return rstd * (
        grad
        - jnp.mean(grad, -1, keepdims=True)
        - normed * jnp.mean(grad * normed, -1, keepdims=True)
    )


def valid_rows(rows, count):
    return (lax.broadcasted_iota(jnp.int32, (rows, 1), 0) < count).astype(F32)


def lone_rows(rows, flag):
    span = jnp.where(flag == 1, rows, rows // 4)
    return lax.rem(lax.broadcasted_iota(jnp.int32, (rows, 1), 0), span) == 0


def span_scale(rows, flag):
    return jnp.where(flag == 1, rows**-0.5, (rows // 4) ** -0.5).astype(F32)


def filter_norm_of(total_ref):
    live = total_ref[1:2, :]
    return (jnp.sqrt(total_ref[0:1, :] / live + NORM_EPS), live)


def columns(width, body):
    for at in range(0, width, 256):
        body(pl.ds(at, 256))


class RowSum:
    def __init__(self, place, copies, part, by_z, by_d, mid, total):
        self.place, self.copies = place, copies
        self.part, self.by_z, self.by_d, self.mid, self.total = part, by_z, by_d, mid, total

    def start(self):
        p = self.place
        self.one = [
            self.copies.to(self.part, self.by_z.at[p.z], p.d, p.z_at(k)) for k in range(1, p.depth)
        ]
        for copy in self.one:
            copy.start()
        self.by_z[p.z] = self.part[...]

    def turn(self):
        p = self.place
        for copy in self.one:
            copy.wait_recv()
        total = self.by_z[0]
        for i in range(1, p.depth):
            total = total + self.by_z[i]
        self.mid[...] = total
        self.two = [
            self.copies.to(self.mid, self.by_d.at[p.d], lax.rem(p.d + k, p.n_dp), p.z)
            for k in range(1, p.n_dp)
        ]
        for copy in self.two:
            copy.start()
        self.by_d[p.d] = total

    def finish(self):
        for copy in self.two:
            copy.wait_recv()
        total = self.by_d[0]
        for i in range(1, self.place.n_dp):
            total = total + self.by_d[i]
        self.total[...] = total

    def drain(self):
        for copy in self.one + self.two:
            copy.wait_send()


class Gather:
    def __init__(self, place, copies, slots_ref, master_ref, out_ref, held, acc, *sum_refs):
        self.place, self.copies, self.slots_ref, self.master_ref = place, copies, slots_ref, master_ref
        self.out_ref, self.held, self.acc = out_ref, held, acc
        self.stages = stages = acc.shape[0]
        self.slot_cap, self.rows, _ = master_ref.shape
        self.piece_rows = 48 if self.rows % 48 == 0 else 16
        self.late_rows = max(16, self.rows // 6 // 16 * 16)
        early = self.early = self.rows - self.late_rows
        whole = pl.ds(0, self.rows)
        self.sums = [
            PlaneSum(place, copies, acc.at[s], whole, self.rows, *(ref.at[s] for ref in sum_refs))
            for s in range(stages)
        ]
        self.cells = [
            [
                PlaneSpread(
                    place, copies, out_ref.at[s], self.rows_of(place.z_at(-k), early if k else self.rows),
                    acc.at[s, place.y, place.x] if k == 0 else None,
                )
                for k in range(place.depth)
            ]
            for s in range(stages)
        ]
        self.over, self.along_z, self.kept = [None] * stages, [None] * stages, [None] * stages
        self.lates = [None] * stages
        self.shares = [[] for _ in range(stages)]

    def rows_of(self, z, count, first=0):
        return pl.ds(pl.multiple_of(z * self.rows + first, 16), count)

    def own(self, s, window):
        p = self.place
        return self.out_ref.at[s, p.y * p.across + p.x, p.core, window]

    def masked(self, s, y, x, core, at):
        slot = self.slots_ref[self.place.n_dp * s + self.place.dp(y, x, core)]
        low = slot - self.place.d * self.slot_cap
        mine = (low >= 0) & (low < self.slot_cap)
        index = jnp.clip(low, 0, self.slot_cap - 1)
        return jnp.where(mine, self.master_ref[index, at, :], 0.0).astype(LOW)

    def each_piece(self, body):
        p, rows = self.place, self.piece_rows
        pieces = self.rows // rows

        def one(i, carry):
            spot, piece = i // pieces, lax.rem(i, pieces)
            y, x = spot // p.across, lax.rem(spot, p.across)
            body(y, x, pl.ds(pl.multiple_of(piece * rows, 16), rows))
            return carry

        lax.fori_loop(0, p.up * p.across * pieces, one, 0)

    def fill(self, s):
        p = self.place

        def body(y, x, at):
            self.held[s, y, x, at, :] = self.masked(s, y, x, 1 - p.core, at)

        self.each_piece(body)
        self.over[s] = self.copies.to(
            self.held.at[s], self.acc.at[s], p.dp(core=1 - p.core), p.z
        )
        self.over[s].start()

    def enter(self, s):
        self.over[s].wait_recv()

        def join(y, x, at):
            mine = self.masked(s, y, x, self.place.core, at)
            self.acc[s, y, x, at, :] = self.acc[s, y, x, at, :] + mine

        self.each_piece(join)
        self.sums[s].start()

    def turn(self, s):
        self.sums[s].turn()

    def home(self, s):
        p = self.place
        self.sums[s].finish()
        target = self.own(s, self.rows_of(p.z, self.rows))
        self.kept[s] = self.copies.here(self.acc.at[s, p.y, p.x], target)
        self.kept[s].start()
        self.cells[s][0].start()

    def column(self, s):
        p = self.place
        source = self.acc.at[s, p.y, p.x, pl.ds(0, self.early), :]
        target = self.own(s, self.rows_of(p.z, self.early))
        self.along_z[s] = [
            self.copies.to(source, target, p.d, p.z_at(k)) for k in range(1, p.depth)
        ]
        for copy in self.along_z[s]:
            copy.start()

    def cell(self, s, k):
        self.along_z[s][k - 1].wait_recv()
        self.cells[s][k].start()

    def passing(self, s, k):
        self.cells[s][k].forward()

    def close(self, s, k):
        if k == 0:
            self.kept[s].wait()
        self.cells[s][k].finish()

    def late(self, s):
        p = self.place
        view = self.out_ref.at[s, :, p.core, self.rows_of(p.z, self.late_rows, self.early)]
        self.lates[s] = [self.copies.to(view, view, p.d, p.z_at(k)) for k in range(1, p.depth)]
        for copy in self.lates[s]:
            copy.start()

    def share(self, s):
        p = self.place
        for k in range(1, p.depth):
            self.lates[s][k - 1].wait_recv()
            rows = self.rows_of(p.z_at(-k), self.late_rows, self.early)
            view = self.out_ref.at[s, :, p.core, rows]
            self.shares[s].append(self.copies.to(view, view, p.dp(core=1 - p.core), p.z))
            self.shares[s][-1].start()

    def done(self, s):
        for cell in self.cells[s]:
            cell.arrived()
        for copy in self.shares[s]:
            copy.wait_recv()

    def drain(self):
        for s in range(self.stages):
            self.over[s].wait_send()
            self.sums[s].drain()
            for copy in self.along_z[s] + self.lates[s] + self.shares[s]:
                copy.wait_send()
            for cell in self.cells[s]:
                cell.drain()


class Stores:
    def __init__(self, copies):
        self.copies, self.open = copies, {}

    def out(self, name, source, target):
        copy = self.copies.here(source, target)
        copy.start()
        self.open.setdefault(name, []).append(copy)

    def settle(self, *names):
        for name in names or list(self.open):
            for copy in self.open.pop(name, []):
                copy.wait()


def forward_plan(layers, stages, depth):
    if (layers, stages, depth) == (2, 4, 4):
        return decode(FORWARD_STEPS, FORWARD_ORDER)
    plan = []
    for s in range(stages):
        plan += [(step, s) for step in ("fill", "enter", "turn", "home", "column")]
        for k in range(depth):
            plan += [("cell", s, k)] if k else []
            plan += [("passing", s, k), ("close", s, k)]
        plan += [(step, s) for step in ("late", "share", "done")]
        for layer in range(layers):
            if s == (layer + 1) * stages // layers - 1:
                steps = ("front_a", "front_b", "sum_turn", "front_c", "mix", "load")
                plan += [(step, layer) for step in steps]
                plan += [("mlp", layer, i) for i in range(4)]
    return plan


def forward_kernel(n_dp, n_fsdp, layers, *refs):
    (
        slots_ref, flag_ref, count_ref, master_in, tokens_in, gains_ref, table_in, back_in,
        w_ref, a_out, q_out, k_out, kh_out, vh_out, y_out, mixed_out, mid_out, b_out, g_out, u_out, h_out,
        total_out, state_out, act_out,
        master, held, acc, from_x, from_y, last_y, last_x,
        tok, state, table, back, wfront, wmlp, a, q, k, kh, vh, y, mixed, mid, b, g, u, h,
        part, by_z, by_d, mid_sum, total, send, recv, local,
    ) = refs
    place = Place(n_dp, n_fsdp)
    copies = Copies(send, recv, local)
    stores = Stores(copies)
    rows, width = state.shape
    load_master = copies.here(master_in, master)
    load_master.start()
    loads = [copies.here(*pair) for pair in ((tokens_in, tok), (table_in, table), (back_in, back))]
    for copy in loads:
        copy.start()
    place.greet_all()
    load_master.wait()
    gather = Gather(place, copies, slots_ref, master, w_ref, held, acc, from_x, from_y, last_y, last_x)
    sums = [
        RowSum(place, copies, *(ref.at[layer] for ref in (part, by_z, by_d, mid_sum, total)))
        for layer in range(layers)
    ]
    valid = valid_rows(rows, count_ref[0])
    long = flag_ref[0]
    lone = lone_rows(rows, long)
    spans = span_scale(rows, flag_ref[0])
    waiting = {}

    def fetch(name, blocks, targets):
        waiting[name] = [
            copies.here(w_ref.at[j // n_dp, j % n_dp // 2, j % 2], t)
            for j, t in zip(blocks, targets)
        ]
        for copy in waiting[name]:
            copy.start()

    def fetched(name):
        for copy in waiting.pop(name):
            copy.wait()

    def front_a(layer):
        fetch("front", [16 * layer + i for i in range(4)], [wfront.at[i] for i in range(4)])
        if layer == 0:
            for copy in loads:
                copy.wait()
            state[...] = tok[...].astype(F32)
        stores.settle("a", "k", "q", "kh", "vh", "y")
        stores.out("state", state, state_out.at[layer])
        normed, _ = normalize(state[...])
        a[...] = (normed * gains_ref[2 * layer : 2 * layer + 1, :]).astype(LOW)
        stores.out("a", a, a_out.at[layer])
        part[layer] = jnp.broadcast_to(jnp.sum(valid), part.shape[1:])
        fetched("front")

        def keys(at):
            value = dot(a[...], wfront[2, :, at]) * valid
            k[:, at] = value
            part[layer, 0:1, at] = jnp.sum(value * value, 0, keepdims=True)

        columns(width, keys)
        sums[layer].start()
        stores.out("k", k, k_out.at[layer])

    def front_b(layer):
        def spectra(at):
            q[:, at] = dot(a[...], wfront[1, :, at])
            values = (dot(a[...], wfront[0, :, at]) * valid).astype(LOW)
            kh[:, at] = dot(table[long], k[:, at].astype(LOW)).astype(LOW)
            vh[:, at] = dot(table[long], values).astype(LOW)

        columns(width, spectra)
        stores.out("q", q, q_out.at[layer])
        stores.out("kh", kh, kh_out.at[layer])
        stores.out("vh", vh, vh_out.at[layer])

    def sum_turn(layer):
        sums[layer].turn()

    def front_c(layer):
        def product(at):
            kr, ki = kh[:rows, at].astype(F32), kh[rows:, at].astype(F32)
            vr, vi = vh[:rows, at].astype(F32), vh[rows:, at].astype(F32)
            cross = ki * vi
            real = kr * vr - jnp.where(lone, 0.0, cross)
            imag = jnp.where(lone, cross, kr * vi + ki * vr)
            y[:, at] = dot(back[long, :, :rows], real.astype(LOW)) + dot(
                back[long, :, rows:], imag.astype(LOW)
            )

        columns(width, product)
        stores.out("y", y, y_out.at[layer])

    def fetch_mlp(layer, i):
        first = 16 * layer + i
        fetch(("mlp", i), [first + 4, first + 8, first + 12], [wmlp.at[i % 2, j] for j in range(3)])

    def load(layer):
        fetch_mlp(layer, 0)

    def mix(layer):
        stores.settle("mixed", "mid", "b", "state")
        sums[layer].finish()
        stores.out("total", total.at[layer], total_out.at[layer])
        norm, _ = filter_norm_of(total.at[layer])
        mixed[...] = (y[...] * (spans / norm) * q[...]).astype(LOW)
        stores.out("mixed", mixed, mixed_out.at[layer])
        state[...] += dot(mixed[...], wfront[3])
        mid[...] = state[...]
        stores.out("mid", mid, mid_out.at[layer])
        normed, _ = normalize(state[...])
        b[...] = (normed * gains_ref[2 * layer + 1 : 2 * layer + 2, :]).astype(LOW)
        stores.out("b", b, b_out.at[layer])

    def mlp(layer, i):
        turn = i % 2
        fetched(("mlp", i))
        if i < 3:
            fetch_mlp(layer, i + 1)
        stores.settle(("g", turn))

        def body(at, turn=turn):
            gate = dot(b[...], wmlp[turn, 0, :, at])
            up = dot(b[...], wmlp[turn, 1, :, at])
            g[turn, :, at] = gate.astype(LOW)
            u[turn, :, at] = up.astype(LOW)
            h[turn, :, at] = (gate * jax.nn.sigmoid(gate) * up).astype(LOW)

        columns(width, body)
        for held_ref, out in ((g, g_out), (u, u_out), (h, h_out)):
            stores.out(("g", turn), held_ref.at[turn], out.at[layer, i])
        state[...] += dot(h[turn], wmlp[turn, 2])
        if i == 3 and layer == layers - 1:
            tok[...] = state[...].astype(LOW)
            stores.out("act", tok, act_out)

    compute = types.SimpleNamespace(
        front_a=front_a, front_b=front_b, front_c=front_c, sum_turn=sum_turn, mix=mix, load=load, mlp=mlp
    )
    run_plan(forward_plan(layers, gather.stages, n_fsdp), gather, compute)
    gather.drain()
    for one in sums:
        one.drain()
    stores.settle()


def forward(n_dp, n_fsdp, scalars, owner_slots, master, tokens, gains, tables):
    blocks = owner_slots.shape[0]
    layers = blocks // 16
    part_rows, cols = master.shape[1:]
    rows, width = tokens.shape
    stages = blocks // n_dp
    row = (rows, width)
    spectrum = (2 * rows, width)
    saved = [
        (row, LOW), (row, F32), (row, F32), (spectrum, LOW), (spectrum, LOW), (row, F32), (row, LOW), (row, F32), (row, LOW),
        ((4,) + row, LOW), ((4,) + row, LOW), ((4,) + row, LOW), ((8, width), F32), (row, F32),
    ]
    count = copy_count(n_dp, n_fsdp, stages, 1, n_fsdp, 3 * n_fsdp) + layers * (n_dp + n_fsdp - 2)
    any_space = pl.BlockSpec(memory_space=pl.ANY)
    scalar = pl.BlockSpec(memory_space=pltpu.SMEM)
    vmem = pl.BlockSpec(memory_space=pltpu.VMEM)
    return pl.pallas_call(
        functools.partial(forward_kernel, n_dp, n_fsdp, layers),
        name="forward",
        out_shape=[jax.ShapeDtypeStruct((stages, n_dp // 2, 2, width, width), LOW)]
        + [jax.ShapeDtypeStruct((layers,) + shape, kind) for shape, kind in saved]
        + [jax.ShapeDtypeStruct(row, LOW)],
        in_specs=[scalar] * 3 + [any_space, any_space, vmem, any_space, any_space],
        out_specs=[any_space] * (2 + len(saved)),
        scratch_shapes=[
            pltpu.VMEM(master.shape, F32),
            pltpu.VMEM((stages, 2, n_dp // 4, part_rows, cols), LOW),
            pltpu.VMEM((stages, 2, n_dp // 4, part_rows, cols), LOW),
        ]
        + plane_sum_shapes(n_dp, (stages,), part_rows, cols)
        + [
            pltpu.VMEM(row, LOW),
            pltpu.VMEM(row, F32),
            pltpu.VMEM(tables[0].shape, LOW),
            pltpu.VMEM(tables[1].shape, LOW),
            pltpu.VMEM((4, width, width), LOW),
            pltpu.VMEM((2, 3, width, width), LOW),
        ]
        + [pltpu.VMEM(shape, kind) for shape, kind in saved[:9]]
        + [pltpu.VMEM((2,) + row, LOW)] * 3
        + [
            pltpu.VMEM((layers, 8, width), F32),
            pltpu.VMEM((layers, n_fsdp, 8, width), F32),
            pltpu.VMEM((layers, n_dp, 8, width), F32),
            pltpu.VMEM((layers, 8, width), F32),
            pltpu.VMEM((layers, 8, width), F32),
            pltpu.SemaphoreType.DMA((count,)),
            pltpu.SemaphoreType.DMA((count,)),
            pltpu.SemaphoreType.DMA((stages + 8 + layers * 48,)),
        ],
        compiler_params=pltpu.CompilerParams(
            collective_id=0, has_side_effects=True, vmem_limit_bytes=VMEM_BYTES
        ),
    )(owner_slots, *scalars, master, tokens, gains, *tables)


class Scatter:
    def __init__(self, place, copies, stores, order, grads, landed, out_ref, acc, aside, from_a, from_b, credits, *sum_refs):
        self.place, self.copies, self.stores, self.order = place, copies, stores, order
        self.grads, self.landed, self.out_ref = grads, landed, out_ref
        self.acc, self.aside, self.from_a, self.from_b = acc, aside, from_a, from_b
        self.credits = credits
        self.slots, self.size = acc.shape[0], acc.shape[-2]
        self.rows = self.size // place.depth
        self.late = from_b.shape[-2]
        self.early = self.rows - self.late
        self.spots = place.up * place.across
        self.stages = len(order)
        self.sums = [
            [
                PlaneSum(
                    place, copies, acc.at[n % self.slots],
                    self.window(place.z_at(k), 0, self.early if k else self.rows),
                    self.early if k else self.rows,
                    *(ref.at[n % self.slots, k] for ref in sum_refs),
                )
                for k in range(place.depth)
            ]
            for n in range(self.stages)
        ]
        whole = pl.ds(0, self.rows)
        self.spreads = [PlaneSpread(place, copies, out_ref.at[s], whole) for s in order]
        self.over = [None] * self.stages
        self.along_a = [{} for _ in order]
        self.along_b = [[] for _ in order]

    def window(self, z, first, count):
        return pl.ds(pl.multiple_of(z * self.rows + first, 16), count)

    def near(self):
        p = self.place
        peers = [(p.dp(x=p.x_at(k)), p.z) for k in range(1, p.across)]
        return peers + [(p.dp(y=p.y_at(m)), p.z) for m in range(1, p.up)]

    def column(self):
        p = self.place
        return [(p.d, p.z_at(k)) for k in range(1, p.depth)]

    def free(self, n, kind, peers):
        if n + self.slots < self.stages:
            for peer in peers:
                pl.semaphore_signal(
                    self.credits.at[kind, n], inc=1, device_id=peer, device_id_type=MESH
                )

    def claim(self, n, kind, peers):
        if n >= self.slots:
            pl.semaphore_wait(self.credits.at[kind, n - self.slots], len(peers))

    def grad(self, n, spot, core):
        return self.grads.at[self.place.n_dp * self.order[n] + 2 * spot + core]

    def offer(self, n):
        p = self.place
        self.stores.settle("outs")
        self.over[n] = [
            self.copies.to(
                self.grad(n, spot, 1 - p.core),
                self.landed.at[n * self.spots + spot],
                p.dp(core=1 - p.core),
                p.z,
            )
            for spot in range(self.spots)
        ]
        for copy in self.over[n]:
            copy.start()

    def sent(self, n):
        for one in self.sums[n]:
            one.drain()
        for copy in list(self.along_a[n].values()) + self.along_b[n]:
            copy.wait_send()

    def enter(self, n):
        p, slot = self.place, n % self.slots
        if n >= self.slots:
            self.sent(n - self.slots)
        targets = [self.acc.at[slot, i // p.across, i % p.across] for i in range(self.spots)]
        own = [self.copies.here(self.grad(n, i, p.core), targets[i]) for i in range(self.spots)]
        other = [
            self.copies.here(self.landed.at[n * self.spots + i], self.aside.at[i % 2])
            for i in range(self.spots)
        ]
        for copy in own:
            copy.start()
        for i in range(min(2, self.spots)):
            self.over[n][i].wait_recv()
            other[i].start()
        for i in range(self.spots):
            own[i].wait()
            other[i].wait()
            add_into(targets[i], [self.aside.at[i % 2]], self.size)
            if i + 2 < self.spots:
                self.over[n][i + 2].wait_recv()
                other[i + 2].start()
        self.claim(n, 0, self.near())
        self.claim(n, 1, self.column())
        for k in range(1, p.depth):
            source = self.acc.at[slot, :, :, self.window(p.z_at(k), self.early, self.late), :]
            self.along_b[n].append(
                self.copies.to(source, self.from_b.at[slot, k - 1], p.d, p.z_at(k))
            )
        for copy in self.along_b[n]:
            copy.start()

    def push(self, n, k):
        p, slot = self.place, n % self.slots
        if k == 0:
            for copy in self.along_b[n]:
                copy.wait_recv()
            window = self.window(p.z, self.early, self.late)
            for y in range(p.up):
                for x in range(p.across):
                    terms = [self.from_b.at[slot, i, y, x] for i in range(p.depth - 1)]
                    add_into(self.acc.at[slot, y, x, window, :], terms, self.late)
        self.sums[n][k].start()

    def turn(self, n, k):
        self.sums[n][k].turn()

    def home(self, n, k):
        p, slot = self.place, n % self.slots
        self.sums[n][k].finish()
        if k > 0:
            source = self.acc.at[slot, p.y, p.x, self.window(p.z_at(k), 0, self.early), :]
            self.along_a[n][k] = self.copies.to(
                source, self.from_a.at[slot, k - 1], p.d, p.z_at(k)
            )
            self.along_a[n][k].start()

    def total(self, n):
        p, slot = self.place, n % self.slots
        self.free(n, 0, self.near())
        for copy in self.along_a[n].values():
            copy.wait_recv()
        terms = [self.from_a.at[slot, k - 1] for k in range(1, p.depth)]
        add_into(self.acc.at[slot, p.y, p.x, self.window(p.z, 0, self.early), :], terms, self.early)
        self.free(n, 1, self.column())
        total = self.acc.at[slot, p.y, p.x, self.window(p.z, 0, self.rows), :]
        own = self.out_ref.at[self.order[n], p.y * p.across + p.x, p.core]
        kept = self.copies.here(total, own)
        kept.start()
        kept.wait()
        self.spreads[n].start()

    def passing(self, n):
        self.spreads[n].forward()

    def close(self, n):
        self.spreads[n].finish()

    def done(self, n):
        self.spreads[n].arrived()

    def drain(self):
        for n in range(self.stages):
            for copy in self.over[n]:
                copy.wait_send()
            if n + self.slots >= self.stages:
                self.sent(n)
            self.spreads[n].drain()


def backward_plan(layers, stages, depth):
    if (layers, stages, depth) == (2, 4, 4):
        return decode(BACKWARD_STEPS, BACKWARD_ORDER)
    plan = []
    for layer in reversed(range(layers)):
        plan += [("mlp", layer, i) for i in range(4)]
        plan += [(step, layer) for step in ("mix_a", "mix_b", "sum_turn", "front_a", "front_b")]
    plan += [("gain_turn", 0)] + [("offer", n) for n in range(stages)]
    for n in range(stages):
        plan += [("enter", n)]
        for k in list(range(1, depth)) + [0]:
            plan += [(step, n, k) for step in ("push", "turn", "home")]
        plan += [(step, n) for step in ("total", "passing", "close", "done")]
    return plan


def backward_kernel(n_dp, n_fsdp, layers, *refs):
    (
        flag_ref, count_ref, cotangent, w_ref, gains_ref, table_in, back_in,
        a_in, q_in, k_in, kh_in, vh_in, y_in, mixed_in, mid_in, b_in, g_in, u_in, h_in, total_in, state_in,
        red_ref, grad_out, gain_total, grads_ref, landed_ref,
        acc, from_x, from_y, last_y, last_x, from_a, from_b, aside,
        table, back, weights, tiles, outs, grad, sums, mid, q, y, low, b, mixed, dv, dq, dk,
        totals, part, by_z, by_d, mid_sum, total, send, recv, local, credits,
    ) = refs
    place = Place(n_dp, n_fsdp)
    copies = Copies(send, recv, local)
    stores = Stores(copies)
    rows, width = grad.shape
    valid = valid_rows(rows, count_ref[0])
    long = flag_ref[0]
    lone = lone_rows(rows, long)
    spans = span_scale(rows, flag_ref[0])
    waiting = {}

    def fetch(name, *pairs):
        waiting[name] = [copies.here(*pair) for pair in pairs]
        for copy in waiting[name]:
            copy.start()

    def fetched(*names):
        for name in names:
            for copy in waiting.pop(name):
                copy.wait()

    def fetch_mlp(layer, i):
        first, turn = 16 * layer + i, i % 2
        fetch(
            ("mlp", i),
            *[(w_ref.at[first + 4 * (j + 1)], weights.at[3 * turn + j]) for j in range(3)],
            *[(ref.at[layer, i], tiles.at[turn, j]) for j, ref in enumerate((g_in, u_in, h_in))],
        )

    fetch("cotangent", (cotangent, grad))
    fetch("b", (b_in.at[layers - 1], b))
    fetch_mlp(layers - 1, 0)
    fetch("tables", (table_in, table), (back_in, back))
    fetch("totals", (total_in, totals))
    place.greet_all()
    order = list(reversed(range(layers * 16 // n_dp)))
    scatter = Scatter(
        place, copies, stores, order, grads_ref, landed_ref, red_ref, acc, aside, from_a, from_b, credits, from_x, from_y, last_y, last_x
    )
    row_sums = [
        RowSum(place, copies, *(ref.at[i] for ref in (part, by_z, by_d, mid_sum, total)))
        for i in range(layers + 1)
    ]
    part[layers] = jnp.zeros(part.shape[1:], F32)

    def begin(layer):
        if layer == layers - 1:
            fetched("cotangent")
            grad[...] = grad[...] * valid
        low[...] = grad[...].astype(LOW)
        sums[...] = jnp.zeros_like(sums)
        fetch("mid", (mid_in.at[layer], mid))
        fetch("mix", (q_in.at[layer], q), (y_in.at[layer], y), (mixed_in.at[layer], mixed))
        fetched("b")

    def mlp(layer, i):
        turn, first = i % 2, 16 * layer + i
        if i == 0:
            begin(layer)
        fetched(("mlp", i))
        if i < 3:
            fetch_mlp(layer, i + 1)
        else:
            first_two = [(16 * layer + 3, 0), (16 * layer, 1), (16 * layer + 1, 2)]
            fetch("front", *[(w_ref.at[j], weights.at[to]) for j, to in first_two])
            fetch("kh", *[(kh_in.at[layer, pl.ds(rows * j, rows)], tiles.at[0, j]) for j in range(2)])
        stores.settle("outs")
        gate_w, up_w, down_w = (weights.at[3 * turn + j] for j in range(3))

        def body(at):
            dhidden = dot_nt(low[...], down_w[at, :])
            gate = tiles[turn, 0, :, at].astype(F32)
            up = tiles[turn, 1, :, at].astype(F32)
            sig = jax.nn.sigmoid(gate)
            dup = (dhidden * gate * sig).astype(LOW)
            dgate = (dhidden * up * sig * (1.0 + gate * (1.0 - sig))).astype(LOW)
            outs[2, at, :] = dot_tn(tiles[turn, 2, :, at], low[...]).astype(LOW)
            outs[0, :, at] = dot_tn(b[...], dgate).astype(LOW)
            outs[1, :, at] = dot_tn(b[...], dup).astype(LOW)
            sums[...] += dot_nt(dgate, gate_w[:, at]) + dot_nt(dup, up_w[:, at])

        columns(width, body)
        for j in range(3):
            block = first + 4 * (j + 1)
            stores.out("outs", outs.at[j], grads_ref.at[block])
        if i == 3:
            fetch("key", (w_ref.at[16 * layer + 2], weights.at[3]))
            fetch("vh", *[(vh_in.at[layer, pl.ds(rows * j, rows)], tiles.at[1, j]) for j in range(2)])
            fetch("a", (a_in.at[layer], b))

    def mix_a(layer):
        if layer == layers - 1:
            fetched("tables", "totals")
        fetched("mid")
        normed, rstd = normalize(mid[...])
        db = sums[...]
        part[layers, 2 * layer + 1 : 2 * layer + 2, :] = jnp.sum(db * normed, 0, keepdims=True)
        gain = gains_ref[2 * layer + 1 : 2 * layer + 2, :]
        grad[...] += norm_back(db * gain, normed, rstd)
        low[...] = grad[...].astype(LOW)
        fetch("k", (k_in.at[layer], mid))
        norm, _ = filter_norm_of(totals.at[layer])
        scale_row = spans / norm
        sums[0:1, :] = scale_row
        part[layer] = jnp.zeros(part.shape[1:], F32)
        fetched("mix", "front", "kh", "vh")

        def through(at):
            dmixed = dot_nt(low[...], weights[0, at, :])
            dq[:, at] = (dmixed * y[:, at] * sums[0:1, at]).astype(LOW)
            dy = dmixed * q[:, at]
            part[layer, 0:1, at] = jnp.sum(dy * y[:, at], 0, keepdims=True) * spans
            q[:, at] = dy

        columns(width, through)
        row_sums[layer].start()

    def mix_b(layer):
        def body(at):
            dh = dot(table[long], q[:, at].astype(LOW))
            dr, di = dh[:rows], dh[rows:]

            def against(turn):
                other_r = tiles[turn, 0, :, at].astype(F32)
                other_i = tiles[turn, 1, :, at].astype(F32)
                cross = di * other_i
                real = dr * other_r + jnp.where(lone, 0.0, cross)
                imag = jnp.where(lone, cross, di * other_r - dr * other_i)
                return dot(back[long, :, :rows], real.astype(LOW)) + dot(
                    back[long, :, rows:], imag.astype(LOW)
                )

            y[:, at] = against(1)
            dv[:, at] = (against(0) * sums[0:1, at] * valid).astype(LOW)

        columns(width, body)
        fetch("state", (state_in.at[layer], q))

    def sum_turn(layer):
        row_sums[layer].turn()

    def gain_turn(_):
        row_sums[layers].turn()

    def front_a(layer):
        fetched("a", "key")
        if layer > 0:
            fetch_mlp_tiles(layer - 1)
        stores.settle("outs")

        def body(at):
            outs[3, at, :] = dot_tn(mixed[:, at], low[...]).astype(LOW)
            outs[0, :, at] = dot_tn(b[...], dv[:, at]).astype(LOW)
            outs[1, :, at] = dot_tn(b[...], dq[:, at]).astype(LOW)

        columns(width, body)
        sums[...] = dot_nt(dv[...], weights[1]) + dot_nt(dq[...], weights[2])

    def front_b(layer):
        fetched("k")
        row_sums[layer].finish()
        norm, live = filter_norm_of(totals.at[layer])
        square = -total[layer, 0:1, :] / (norm * norm) / (2.0 * norm * live)
        dk[...] = ((y[...] * (spans / norm) + 2.0 * mid[...] * square) * valid).astype(LOW)

        def keys(at):
            outs[2, :, at] = dot_tn(b[...], dk[:, at]).astype(LOW)

        columns(width, keys)
        for j in range(4):
            stores.out("outs", outs.at[j], grads_ref.at[16 * layer + j])
        sums[...] += dot_nt(dk[...], weights[3])
        if layer > 0:
            fetch("b", (b_in.at[layer - 1], b))
            fetch_mlp_weights(layer - 1)
        fetched("state")
        da = sums[...]
        normed, rstd = normalize(q[...])
        part[layers, 2 * layer : 2 * layer + 1, :] = jnp.sum(da * normed, 0, keepdims=True)
        gain = gains_ref[2 * layer : 2 * layer + 1, :]
        grad[...] += norm_back(da * gain, normed, rstd)
        if layer == 0:
            stores.out("grad", grad, grad_out)
            row_sums[layers].start()

    def fetch_mlp_tiles(layer):
        fetch(
            "tiles", *[(ref.at[layer, 0], tiles.at[0, j]) for j, ref in enumerate((g_in, u_in, h_in))]
        )

    def fetch_mlp_weights(layer):
        fetch("weights", *[(w_ref.at[16 * layer + 4 * (j + 1)], weights.at[j]) for j in range(3)])
        waiting[("mlp", 0)] = waiting.pop("tiles") + waiting.pop("weights")

    compute = types.SimpleNamespace(
        mlp=mlp, mix_a=mix_a, mix_b=mix_b, front_a=front_a, front_b=front_b,
        sum_turn=sum_turn, gain_turn=gain_turn,
    )
    run_plan(backward_plan(layers, scatter.stages, n_fsdp), scatter, compute)
    row_sums[layers].finish()
    gain_total[...] = total[layers]
    scatter.drain()
    for one in row_sums:
        one.drain()
    stores.settle()


def backward(n_dp, n_fsdp, scalars, cotangent, weights, gains, tables, saved):
    width = weights.shape[-1]
    weights = weights.reshape(-1, width, width)
    blocks = weights.shape[0]
    layers = blocks // 16
    rows = cotangent.shape[0]
    stages = blocks // n_dp
    spots = n_dp // 2
    slots = 2 if n_dp == 8 else 1
    part_rows = width // n_fsdp
    row = (rows, width)
    late = max(16, part_rows // 6 // 16 * 16)
    spread_count = spots + 2 * (n_fsdp - 1)
    count = copy_count(n_dp, n_fsdp, stages, n_fsdp, 1, spread_count)
    count += (layers + 1) * (n_dp + n_fsdp - 2)
    any_space = pl.BlockSpec(memory_space=pl.ANY)
    scalar = pl.BlockSpec(memory_space=pltpu.SMEM)
    vmem = pl.BlockSpec(memory_space=pltpu.VMEM)
    return pl.pallas_call(
        functools.partial(backward_kernel, n_dp, n_fsdp, layers),
        name="backward",
        out_shape=[
            jax.ShapeDtypeStruct((stages, n_dp // 2, 2, part_rows, width), LOW),
            jax.ShapeDtypeStruct(row, F32),
            jax.ShapeDtypeStruct((8, width), F32),
            jax.ShapeDtypeStruct((blocks, width, width), LOW),
            jax.ShapeDtypeStruct((blocks // 2, width, width), LOW),
        ],
        in_specs=[scalar, scalar, any_space, any_space, vmem] + [any_space] * (2 + len(saved)),
        out_specs=[any_space, any_space, vmem, any_space, any_space],
        scratch_shapes=[pltpu.VMEM((slots, 2, n_dp // 4, width, width), LOW)]
        + plane_sum_shapes(n_dp, (slots, n_fsdp), part_rows, width)
        + [
            pltpu.VMEM((slots, n_fsdp - 1, part_rows - late, width), LOW),
            pltpu.VMEM((slots, n_fsdp - 1, 2, n_dp // 4, late, width), LOW),
            pltpu.VMEM((2, width, width), LOW),
            pltpu.VMEM(tables[0].shape, LOW),
            pltpu.VMEM(tables[1].shape, LOW),
            pltpu.VMEM((6, width, width), LOW),
            pltpu.VMEM((2, 3) + row, LOW),
            pltpu.VMEM((4, width, width), LOW),
        ]
        + [pltpu.VMEM(row, F32)] * 5
        + [pltpu.VMEM(row, LOW)] * 6
        + [
            pltpu.VMEM((layers, 8, width), F32),
            pltpu.VMEM((layers + 1, 8, width), F32),
            pltpu.VMEM((layers + 1, n_fsdp, 8, width), F32),
            pltpu.VMEM((layers + 1, n_dp, 8, width), F32),
            pltpu.VMEM((layers + 1, 8, width), F32),
            pltpu.VMEM((layers + 1, 8, width), F32),
            pltpu.SemaphoreType.DMA((count,)),
            pltpu.SemaphoreType.DMA((count,)),
            pltpu.SemaphoreType.DMA((stages * (2 * spots + 1) + layers * 64 + 16,)),
            pltpu.SemaphoreType.REGULAR((2, stages)),
        ],
        compiler_params=pltpu.CompilerParams(
            collective_id=1, has_side_effects=True, vmem_limit_bytes=VMEM_BYTES
        ),
    )(*scalars, cotangent, weights, gains, *tables, *saved)


def call(kernel, name, grid, scalars, args, specs, outs, out_specs, scratch=()):
    return pl.pallas_call(
        kernel,
        name=name,
        out_shape=outs,
        grid_spec=pltpu.PrefetchScalarGridSpec(
            num_scalar_prefetch=len(scalars),
            grid=(grid,),
            in_specs=specs,
            out_specs=out_specs,
            scratch_shapes=scratch,
        ),
        compiler_params=pltpu.CompilerParams(vmem_limit_bytes=VMEM_BYTES),
    )(*scalars, *args)


def adam_step(grad, first, second, weight, rate, decay):
    first_out = 0.5 * first + 0.5 * grad
    second_out = 0.5 * second + 0.5 * grad * grad
    fix = 1.0 / (1.0 - 0.5**STEP)
    weight_out = weight - rate * (
        first_out * fix / (jnp.sqrt(second_out * fix) + ADAM_EPS) + decay * weight
    )
    return (first_out, second_out, weight_out)


def adam_kernel(
    block, used, grad_ref, master_ref, first_ref, second_ref, first_out, second_out, master_out
):
    taken = used[pl.program_id(0)] == 1
    first, second, master = first_ref[...], second_ref[...], master_ref[...]
    new = adam_step(grad_ref[...].astype(F32), first, second, master, 0.03, 0.01)
    first_out[...] = jnp.where(taken, new[0], first)
    second_out[...] = jnp.where(taken, new[1], second)
    master_out[...] = jnp.where(taken, new[2], master)


def adam_blocks(block, used, grads, master, first, second):
    shape = (1,) + master.shape[1:]
    own = pl.BlockSpec(shape, lambda i, block, used: (i, 0, 0))
    picked = pl.BlockSpec(shape, lambda i, block, used: (block[i], 0, 0))
    return call(
        adam_kernel,
        "adam",
        master.shape[0],
        (block, used),
        (grads, master, first, second),
        [picked, own, own, own],
        [jax.ShapeDtypeStruct(master.shape, F32)] * 3,
        [own] * 3,
    )


def on_device(
    n_dp,
    n_fsdp,
    tokens,
    cotangent,
    row_counts,
    bucket_flags,
    owner_slots,
    master,
    first_moment,
    second_moment,
    gains,
    gain_first,
    gain_second,
):
    rows = tokens.shape[0]
    slot_cap = master.shape[0]
    layers = owner_slots.shape[0] // 16
    tables = transform_tables(rows)
    scalars = (bucket_flags, row_counts)
    weights, *saved, activations = forward(
        n_dp, n_fsdp, scalars, owner_slots, master, tokens, gains, tables
    )
    summed, grad, gain_sums, _, _ = backward(
        n_dp, n_fsdp, scalars, cotangent, weights, gains, tables, saved
    )
    gains_total = gain_sums[: 2 * layers]
    my_slots = lax.axis_index("dp") * slot_cap + jnp.arange(slot_cap, dtype=jnp.int32)
    hits = owner_slots[None, :] == my_slots[:, None]
    used = jnp.any(hits, 1).astype(jnp.int32)
    block = jnp.sum(jnp.where(hits, jnp.arange(owner_slots.shape[0], dtype=jnp.int32)[None, :], 0), 1)
    first_out, second_out, master_out = adam_blocks(
        block, used, summed.reshape(-1, *master.shape[1:]), master, first_moment, second_moment
    )
    gain_m, gain_v, gain_w = adam_step(gains_total, gain_first, gain_second, gains, 0.2, 0.0)
    return (activations, grad, first_out, second_out, master_out, gain_m, gain_v, gain_w)


def solution(mesh):
    rows = P(("dp", "fsdp"), None)
    blocks = P("dp", "fsdp", None)
    flat = P(("dp", "fsdp"))
    return jax.shard_map(
        functools.partial(on_device, mesh.shape["dp"], mesh.shape["fsdp"]),
        mesh=mesh,
        in_specs=(rows, rows, flat, flat, P(), blocks, blocks, blocks, P(), P(), P()),
        out_specs=(rows, rows, blocks, blocks, blocks, P(), P(), P()),
        check_vma=False,
    )
```

```python
import functools
import math
import types

import jax
import jax.numpy as jnp
import numpy as np
from jax import lax
from jax.experimental import pallas as pl
from jax.experimental.pallas import tpu as pltpu
from jax.sharding import PartitionSpec as P

STEP = 5
NORM_EPS = 1e-05
ADAM_EPS = 1e-08
LOW = jnp.bfloat16
F32 = jnp.float32
MESH = pl.DeviceIdType.MESH
VMEM_BYTES = 60 * 2**20


FORWARD_STEPS = (
    ("fill", 1), ("enter", 1), ("turn", 1), ("home", 1), ("column", 1), ("cell", 2), ("passing", 2),
    ("close", 2), ("late", 1), ("share", 1), ("done", 1), ("front_a", 1), ("front_b", 1), ("sum_turn", 1),
    ("front_c", 1), ("mix", 1), ("load", 1), ("mlp", 2),
)
FORWARD_ORDER = (
    0, 10, 100, 20, 110, 200, 120, 300, 400, 501, 600, 210, 700, 800, 601, 30, 503, 310, 701, 410, 502, 603,
    900, 602, 220, 610, 130, 703, 710, 512, 702, 810, 320, 230, 1000, 420, 612, 620, 513, 330, 720, 521, 511,
    1100, 522, 1200, 820, 430, 1300, 611, 712, 613, 1400, 630, 523, 622, 621, 1500, 711, 920, 910, 623, 713,
    730, 531, 721, 1010, 1600, 723, 1700, 830, 532, 722, 1701, 1702, 631, 1703, 533, 1020, 1110, 632, 731,
    1210, 633, 1410, 732, 1310, 930, 733, 1510, 1030, 1610, 1710, 1711, 1712, 1713,
)
BACKWARD_STEPS = (
    ("downs", 1), ("gates", 2), ("inputs", 2), ("mix_a", 1), ("mix_b", 1), ("sum_turn", 1), ("front_a", 1),
    ("front_b", 1), ("gain_turn", 1), ("offer", 2), ("join", 2), ("enter", 1), ("push", 2), ("turn", 2),
    ("home", 2), ("total", 1), ("passing", 1), ("close", 1), ("done", 1),
)
BACKWARD_ORDER = (
    10, 900, 110, 902, 901, 111, 1000, 903, 1001, 1002, 1003, 1100, 1202, 210, 211, 1201, 112, 212, 1203, 910,
    113, 213, 1301, 1010, 911, 310, 1302, 1401, 1200, 410, 1011, 510, 1402, 1303, 610, 1300, 710, 912, 913,
    1403, 1012, 1013, 1110, 1211, 0, 1400, 1213, 1500, 920, 100, 101, 921, 1311, 1020, 923, 200, 1210, 922,
    1021, 1600, 1022, 1023, 1120, 1313, 1222, 1212, 1413, 201, 102, 1221, 202, 1310, 103, 1700, 1312, 1411,
    1322, 203, 1321, 930, 1223, 300, 1410, 1412, 400, 1421, 500, 1220, 1800, 600, 700, 1323, 933, 1510, 1422,
    931, 932, 1030, 1320, 1031, 1032, 1033, 1130, 1232, 1420, 1423, 1231, 1233, 1331, 1332, 1230, 800, 1431,
    1333, 1432, 1520, 1433, 1330, 1620, 1610, 1430, 1530, 1710, 1630, 1720, 1820, 1810, 1730, 1830,
)


def span_tables(length):
    period = 2 * length
    freqs = np.arange(length)[:, None]
    places = np.arange(length)[None, :]
    angle = (freqs * places % period) * (2.0 * math.pi / period)
    cosine, sine = np.cos(angle), -np.sin(angle)
    sine[0] = np.cos(math.pi * np.arange(length))
    weight = np.where(np.arange(length) == 0, 1.0, 2.0)[None, :] / period
    return (cosine, sine, cosine.T * weight, sine.T * weight)


def transform_tables(rows):
    short = [np.kron(np.eye(4), table) for table in span_tables(rows // 4)]
    full = span_tables(rows)
    forward = np.stack([np.concatenate(t[:2], 0) for t in (short, full)])
    inverse = np.stack([np.concatenate(t[2:], 1) for t in (short, full)])
    return (jnp.asarray(forward, LOW), jnp.asarray(inverse, LOW))


class Place:
    def __init__(self, n_dp, n_fsdp):
        self.n_dp, self.depth = n_dp, n_fsdp
        self.up, self.across = 2, n_dp // 4
        self.d = lax.axis_index("dp")
        self.z = lax.axis_index("fsdp")
        self.core = lax.rem(self.d, 2)
        self.x = lax.rem(self.d // 2, self.across)
        self.y = self.d // (2 * self.across)

    def x_at(self, k):
        return lax.rem(self.x + k + self.across, self.across)

    def y_at(self, m):
        return lax.rem(self.y + m + self.up, self.up)

    def z_at(self, k):
        return lax.rem(self.z + k + self.depth, self.depth)

    def dp(self, y=None, x=None, core=None):
        y = self.y if y is None else y
        x = self.x if x is None else x
        core = self.core if core is None else core
        return (y * self.across + x) * 2 + core

    def greet(self):
        barrier = pltpu.get_barrier_semaphore()
        peers = [(self.dp(core=1 - self.core), self.z)]
        peers += [(self.dp(x=self.x_at(k)), self.z) for k in range(1, self.across)]
        peers += [(self.dp(y=self.y_at(m)), self.z) for m in range(1, self.up)]
        peers += [(self.d, self.z_at(k)) for k in range(1, self.depth)]
        for peer in peers:
            pl.semaphore_signal(barrier, inc=1, device_id=peer, device_id_type=MESH)
        pl.semaphore_wait(barrier, len(peers))

    def greet_all(self):
        barrier = pltpu.get_barrier_semaphore()
        peers = [(lax.rem(self.d + k, self.n_dp), self.z) for k in range(1, self.n_dp)]
        peers += [(self.d, self.z_at(k)) for k in range(1, self.depth)]
        for peer in peers:
            pl.semaphore_signal(barrier, inc=1, device_id=peer, device_id_type=MESH)
        pl.semaphore_wait(barrier, len(peers))


class Copies:
    def __init__(self, send, recv, local):
        self.send, self.recv, self.local = send, recv, local
        self.sent, self.moved = 0, 0

    def to(self, source, target, dp, z):
        index = self.sent
        self.sent += 1
        return pltpu.make_async_remote_copy(
            src_ref=source,
            dst_ref=target,
            send_sem=self.send.at[index],
            recv_sem=self.recv.at[index],
            device_id=(dp, z),
            device_id_type=MESH,
        )

    def here(self, source, target):
        index = self.moved
        self.moved += 1
        return pltpu.make_async_copy(source, target, self.local.at[index])


def add_into(total, terms, rows):
    step = next(size for size in (48, 32, 16) if rows % size == 0)

    def piece(i, carry):
        at = pl.ds(pl.multiple_of(i * step, 16), step)
        value = total[at, :].astype(F32)
        for term in terms:
            value = value + term[at, :].astype(F32)
        total[at, :] = value.astype(LOW)
        return carry

    lax.fori_loop(0, rows // step, piece, 0)


class PlaneSum:
    def __init__(self, place, copies, acc, window, count, from_x, from_y, last_y, last_x):
        self.place, self.copies, self.acc, self.window, self.count = place, copies, acc, window, count
        self.from_x, self.from_y, self.last_y, self.last_x = from_x, from_y, last_y, last_x
        half = acc.shape[-1] // 2
        self.first, self.second = pl.ds(0, half), pl.ds(half, half)
        self.rows = pl.ds(0, count)

    def start(self):
        p, rows = self.place, self.rows
        self.one = []
        for k in range(1, p.across):
            source = self.acc.at[:, p.x_at(k), self.window, self.first]
            target = self.from_x.at[k - 1, :, rows]
            self.one.append(self.copies.to(source, target, p.dp(x=p.x_at(k)), p.z))
        for m in range(1, p.up):
            source = self.acc.at[p.y_at(m), :, self.window, self.second]
            target = self.from_y.at[m - 1, :, rows]
            self.one.append(self.copies.to(source, target, p.dp(y=p.y_at(m)), p.z))
        for copy in self.one:
            copy.start()

    def turn(self):
        p, rows = self.place, self.rows
        for copy in self.one:
            copy.wait_recv()
        for y in range(p.up):
            terms = [self.from_x.at[k - 1, y, rows] for k in range(1, p.across)]
            add_into(self.acc.at[y, p.x, self.window, self.first], terms, self.count)
        for x in range(p.across):
            terms = [self.from_y.at[m - 1, x, rows] for m in range(1, p.up)]
            add_into(self.acc.at[p.y, x, self.window, self.second], terms, self.count)
        self.two = []
        for m in range(1, p.up):
            source = self.acc.at[p.y_at(m), p.x, self.window, self.first]
            target = self.last_y.at[m - 1, rows]
            self.two.append(self.copies.to(source, target, p.dp(y=p.y_at(m)), p.z))
        for k in range(1, p.across):
            source = self.acc.at[p.y, p.x_at(k), self.window, self.second]
            target = self.last_x.at[k - 1, rows]
            self.two.append(self.copies.to(source, target, p.dp(x=p.x_at(k)), p.z))
        for copy in self.two:
            copy.start()

    def finish(self):
        p, rows = self.place, self.rows
        for copy in self.two:
            copy.wait_recv()
        terms = [self.last_y.at[m - 1, rows] for m in range(1, p.up)]
        add_into(self.acc.at[p.y, p.x, self.window, self.first], terms, self.count)
        terms = [self.last_x.at[k - 1, rows] for k in range(1, p.across)]
        add_into(self.acc.at[p.y, p.x, self.window, self.second], terms, self.count)

    def drain(self):
        for copy in self.one + self.two:
            copy.wait_send()


class PlaneSpread:
    def __init__(self, place, copies, array, window, source=None):
        self.place, self.copies, self.array = place, copies, array
        self.window, self.source = window, source
        half = array.shape[-1] // 2
        self.halves = (pl.ds(0, half), pl.ds(half, half))
        self.sends = []

    def block(self, half=None, y=None, x=None):
        p = self.place
        y, x = p.y if y is None else y, p.x if x is None else x
        view = self.array.at[y * p.across + x, p.core, self.window]
        return view if half is None else view.at[:, self.halves[half]]

    def fire(self, ref, dp, source=None):
        copy = self.copies.to(ref if source is None else source, ref, dp, self.place.z)
        copy.start()
        self.sends.append(copy)
        return copy

    def start(self):
        p, own = self.place, self.block()
        self.by_x = [self.fire(own, p.dp(x=p.x_at(k)), self.source) for k in range(1, p.across)]
        self.by_y = [self.fire(own, p.dp(y=p.y_at(m)), self.source) for m in range(1, p.up)]

    def forward(self):
        p = self.place
        self.last = []
        for k in range(1, p.across):
            self.by_x[k - 1].wait_recv()
            for m in range(1, p.up):
                self.last.append(self.fire(self.block(0, x=p.x_at(-k)), p.dp(y=p.y_at(m))))
        for m in range(1, p.up):
            self.by_y[m - 1].wait_recv()
            for k in range(1, p.across):
                self.last.append(self.fire(self.block(1, y=p.y_at(-m)), p.dp(x=p.x_at(k))))

    def finish(self):
        for copy in self.last:
            copy.wait_recv()
        self.hand_over(self.window)

    def hand_over(self, window):
        p = self.place
        self.over = self.fire(self.array.at[:, p.core, window], p.dp(core=1 - p.core))

    def arrived(self):
        self.over.wait_recv()

    def drain(self):
        for copy in self.sends:
            copy.wait_send()


def plane_sum_shapes(n_dp, lead, rows, cols):
    up, across, half = 2, n_dp // 4, cols // 2
    return [
        pltpu.VMEM(lead + (across - 1, up, rows, half), LOW),
        pltpu.VMEM(lead + (up - 1, across, rows, half), LOW),
        pltpu.VMEM(lead + (up - 1, rows, half), LOW),
        pltpu.VMEM(lead + (across - 1, rows, half), LOW),
    ]


def copy_count(n_dp, n_fsdp, stages, sums, spreads, others):
    up, across = 2, n_dp // 4
    near = up - 1 + across - 1
    diagonal = (up - 1) * (across - 1)
    each_spread = near + 2 * diagonal + 1
    return stages * (sums * 2 * near + spreads * each_spread + others)


def run_plan(plan, *actors):
    for name, *where in plan:
        actor = next(a for a in actors if hasattr(a, name))
        getattr(actor, name)(*where)


def decode(steps, codes):
    plan = []
    for code in codes:
        name, count = steps[code // 100]
        plan.append((name, code // 10 % 10, code % 10)[: count + 1])
    return plan


def dot(left, right):
    return jnp.dot(left, right, preferred_element_type=F32)


def dot_nt(left, right):
    return lax.dot_general(left, right, (((1,), (1,)), ((), ())), preferred_element_type=F32)


def dot_tn(left, right):
    return lax.dot_general(left, right, (((0,), (0,)), ((), ())), preferred_element_type=F32)


def normalize(inputs):
    centred = inputs - jnp.mean(inputs, -1, keepdims=True)
    rstd = lax.rsqrt(jnp.mean(centred * centred, -1, keepdims=True) + NORM_EPS)
    return (centred * rstd, rstd)


def norm_back(grad, normed, rstd):
    return rstd * (
        grad
        - jnp.mean(grad, -1, keepdims=True)
        - normed * jnp.mean(grad * normed, -1, keepdims=True)
    )


def valid_rows(rows, count):
    return (lax.broadcasted_iota(jnp.int32, (rows, 1), 0) < count).astype(F32)


def lone_rows(rows, flag):
    span = jnp.where(flag == 1, rows, rows // 4)
    return lax.rem(lax.broadcasted_iota(jnp.int32, (rows, 1), 0), span) == 0


def span_scale(rows, flag):
    return jnp.where(flag == 1, rows**-0.5, (rows // 4) ** -0.5).astype(F32)


def filter_norm_of(total_ref):
    live = total_ref[1:2, :]
    return (jnp.sqrt(total_ref[0:1, :] / live + NORM_EPS), live)


def columns(width, body):
    for at in range(0, width, 256):
        body(pl.ds(at, 256))


class RowSum:
    def __init__(self, place, copies, part, by_z, by_d, mid, total):
        self.place, self.copies = place, copies
        self.part, self.by_z, self.by_d, self.mid, self.total = part, by_z, by_d, mid, total

    def start(self):
        p = self.place
        self.one = [
            self.copies.to(self.part, self.by_z.at[p.z], p.d, p.z_at(k)) for k in range(1, p.depth)
        ]
        for copy in self.one:
            copy.start()
        self.by_z[p.z] = self.part[...]

    def turn(self):
        p = self.place
        for copy in self.one:
            copy.wait_recv()
        total = self.by_z[0]
        for i in range(1, p.depth):
            total = total + self.by_z[i]
        self.mid[...] = total
        self.two = [
            self.copies.to(self.mid, self.by_d.at[p.d], lax.rem(p.d + k, p.n_dp), p.z)
            for k in range(1, p.n_dp)
        ]
        for copy in self.two:
            copy.start()
        self.by_d[p.d] = total

    def finish(self):
        for copy in self.two:
            copy.wait_recv()
        total = self.by_d[0]
        for i in range(1, self.place.n_dp):
            total = total + self.by_d[i]
        self.total[...] = total

    def drain(self):
        for copy in self.one + self.two:
            copy.wait_send()


class Gather:
    def __init__(self, place, copies, slots_ref, master_ref, out_ref, held, acc, *sum_refs):
        self.place, self.copies, self.slots_ref, self.master_ref = place, copies, slots_ref, master_ref
        self.out_ref, self.held, self.acc = out_ref, held, acc
        self.stages = stages = acc.shape[0]
        self.slot_cap, self.rows, _ = master_ref.shape
        self.piece_rows = 48 if self.rows % 48 == 0 else 16
        self.late_rows = max(16, self.rows // 6 // 16 * 16)
        early = self.early = self.rows - self.late_rows
        whole = pl.ds(0, self.rows)
        self.sums = [
            PlaneSum(place, copies, acc.at[s], whole, self.rows, *(ref.at[s] for ref in sum_refs))
            for s in range(stages)
        ]
        self.cells = [
            [
                PlaneSpread(
                    place, copies, out_ref.at[s], self.rows_of(place.z_at(-k), early if k else self.rows),
                    acc.at[s, place.y, place.x] if k == 0 else None,
                )
                for k in range(place.depth)
            ]
            for s in range(stages)
        ]
        self.over, self.along_z, self.kept = [None] * stages, [None] * stages, [None] * stages
        self.lates = [None] * stages
        self.shares = [[] for _ in range(stages)]

    def rows_of(self, z, count, first=0):
        return pl.ds(pl.multiple_of(z * self.rows + first, 16), count)

    def own(self, s, window):
        p = self.place
        return self.out_ref.at[s, p.y * p.across + p.x, p.core, window]

    def masked(self, s, y, x, core, at):
        slot = self.slots_ref[self.place.n_dp * s + self.place.dp(y, x, core)]
        low = slot - self.place.d * self.slot_cap
        mine = (low >= 0) & (low < self.slot_cap)
        index = jnp.clip(low, 0, self.slot_cap - 1)
        return jnp.where(mine, self.master_ref[index, at, :], 0.0).astype(LOW)

    def each_piece(self, body):
        p, rows = self.place, self.piece_rows
        pieces = self.rows // rows

        def one(i, carry):
            spot, piece = i // pieces, lax.rem(i, pieces)
            y, x = spot // p.across, lax.rem(spot, p.across)
            body(y, x, pl.ds(pl.multiple_of(piece * rows, 16), rows))
            return carry

        lax.fori_loop(0, p.up * p.across * pieces, one, 0)

    def fill(self, s):
        p = self.place

        def body(y, x, at):
            self.held[s, y, x, at, :] = self.masked(s, y, x, 1 - p.core, at)

        self.each_piece(body)
        self.over[s] = self.copies.to(
            self.held.at[s], self.acc.at[s], p.dp(core=1 - p.core), p.z
        )
        self.over[s].start()

    def enter(self, s):
        self.over[s].wait_recv()

        def join(y, x, at):
            mine = self.masked(s, y, x, self.place.core, at)
            self.acc[s, y, x, at, :] = self.acc[s, y, x, at, :] + mine

        self.each_piece(join)
        self.sums[s].start()

    def turn(self, s):
        self.sums[s].turn()

    def home(self, s):
        p = self.place
        self.sums[s].finish()
        target = self.own(s, self.rows_of(p.z, self.rows))
        self.kept[s] = self.copies.here(self.acc.at[s, p.y, p.x], target)
        self.kept[s].start()
        self.cells[s][0].start()

    def column(self, s):
        p = self.place
        source = self.acc.at[s, p.y, p.x, pl.ds(0, self.early), :]
        target = self.own(s, self.rows_of(p.z, self.early))
        self.along_z[s] = [
            self.copies.to(source, target, p.d, p.z_at(k)) for k in range(1, p.depth)
        ]
        for copy in self.along_z[s]:
            copy.start()

    def cell(self, s, k):
        self.along_z[s][k - 1].wait_recv()
        self.cells[s][k].start()

    def passing(self, s, k):
        self.cells[s][k].forward()

    def close(self, s, k):
        if k == 0:
            self.kept[s].wait()
        self.cells[s][k].finish()

    def late(self, s):
        p = self.place
        view = self.out_ref.at[s, :, p.core, self.rows_of(p.z, self.late_rows, self.early)]
        self.lates[s] = [self.copies.to(view, view, p.d, p.z_at(k)) for k in range(1, p.depth)]
        for copy in self.lates[s]:
            copy.start()

    def share(self, s):
        p = self.place
        for k in range(1, p.depth):
            self.lates[s][k - 1].wait_recv()
            rows = self.rows_of(p.z_at(-k), self.late_rows, self.early)
            view = self.out_ref.at[s, :, p.core, rows]
            self.shares[s].append(self.copies.to(view, view, p.dp(core=1 - p.core), p.z))
            self.shares[s][-1].start()

    def done(self, s):
        for cell in self.cells[s]:
            cell.arrived()
        for copy in self.shares[s]:
            copy.wait_recv()

    def drain(self):
        for s in range(self.stages):
            self.over[s].wait_send()
            self.sums[s].drain()
            for copy in self.along_z[s] + self.lates[s] + self.shares[s]:
                copy.wait_send()
            for cell in self.cells[s]:
                cell.drain()


class Stores:
    def __init__(self, copies):
        self.copies, self.open = copies, {}

    def out(self, name, source, target):
        copy = self.copies.here(source, target)
        copy.start()
        self.open.setdefault(name, []).append(copy)

    def settle(self, *names):
        for name in names or list(self.open):
            for copy in self.open.pop(name, []):
                copy.wait()


def forward_plan(layers, stages, depth):
    if (layers, stages, depth) == (2, 4, 4):
        return decode(FORWARD_STEPS, FORWARD_ORDER)
    plan = []
    for s in range(stages):
        plan += [(step, s) for step in ("fill", "enter", "turn", "home", "column")]
        for k in range(depth):
            plan += [("cell", s, k)] if k else []
            plan += [("passing", s, k), ("close", s, k)]
        plan += [(step, s) for step in ("late", "share", "done")]
        for layer in range(layers):
            if s == (layer + 1) * stages // layers - 1:
                steps = ("front_a", "front_b", "sum_turn", "front_c", "mix", "load")
                plan += [(step, layer) for step in steps]
                plan += [("mlp", layer, i) for i in range(4)]
    return plan


def forward_kernel(n_dp, n_fsdp, layers, *refs):
    (
        slots_ref, flag_ref, count_ref, master_in, tokens_in, gains_ref, table_in, back_in,
        w_ref, a_out, q_out, k_out, kh_out, vh_out, y_out, mixed_out, mid_out, b_out, g_out, u_out, h_out,
        total_out, state_out, act_out,
        master, held, acc, from_x, from_y, last_y, last_x,
        tok, state, table, back, wfront, wmlp, a, q, k, kh, vh, y, mixed, mid, b, g, u, h,
        part, by_z, by_d, mid_sum, total, send, recv, local,
    ) = refs
    place = Place(n_dp, n_fsdp)
    copies = Copies(send, recv, local)
    stores = Stores(copies)
    rows, width = state.shape
    load_master = copies.here(master_in, master)
    load_master.start()
    loads = [copies.here(*pair) for pair in ((tokens_in, tok), (table_in, table), (back_in, back))]
    for copy in loads:
        copy.start()
    place.greet_all()
    load_master.wait()
    gather = Gather(place, copies, slots_ref, master, w_ref, held, acc, from_x, from_y, last_y, last_x)
    sums = [
        RowSum(place, copies, *(ref.at[layer] for ref in (part, by_z, by_d, mid_sum, total)))
        for layer in range(layers)
    ]
    valid = valid_rows(rows, count_ref[0])
    long = flag_ref[0]
    lone = lone_rows(rows, long)
    spans = span_scale(rows, flag_ref[0])
    waiting = {}

    def fetch(name, blocks, targets):
        waiting[name] = [
            copies.here(w_ref.at[j // n_dp, j % n_dp // 2, j % 2], t)
            for j, t in zip(blocks, targets)
        ]
        for copy in waiting[name]:
            copy.start()

    def fetched(name):
        for copy in waiting.pop(name):
            copy.wait()

    def front_a(layer):
        fetch("front", [16 * layer + i for i in range(4)], [wfront.at[i] for i in range(4)])
        if layer == 0:
            for copy in loads:
                copy.wait()
            state[...] = tok[...].astype(F32)
        stores.settle("a", "k", "q", "kh", "vh", "y")
        stores.out("state", state, state_out.at[layer])
        normed, _ = normalize(state[...])
        a[...] = (normed * gains_ref[2 * layer : 2 * layer + 1, :]).astype(LOW)
        stores.out("a", a, a_out.at[layer])
        part[layer] = jnp.broadcast_to(jnp.sum(valid), part.shape[1:])
        fetched("front")

        def keys(at):
            value = dot(a[...], wfront[2, :, at]) * valid
            k[:, at] = value
            part[layer, 0:1, at] = jnp.sum(value * value, 0, keepdims=True)

        columns(width, keys)
        sums[layer].start()
        stores.out("k", k, k_out.at[layer])

    def front_b(layer):
        def spectra(at):
            q[:, at] = dot(a[...], wfront[1, :, at])
            values = (dot(a[...], wfront[0, :, at]) * valid).astype(LOW)
            kh[:, at] = dot(table[long], k[:, at].astype(LOW)).astype(LOW)
            vh[:, at] = dot(table[long], values).astype(LOW)

        columns(width, spectra)
        stores.out("q", q, q_out.at[layer])
        stores.out("kh", kh, kh_out.at[layer])
        stores.out("vh", vh, vh_out.at[layer])

    def sum_turn(layer):
        sums[layer].turn()

    def front_c(layer):
        def product(at):
            kr, ki = kh[:rows, at].astype(F32), kh[rows:, at].astype(F32)
            vr, vi = vh[:rows, at].astype(F32), vh[rows:, at].astype(F32)
            cross = ki * vi
            real = kr * vr - jnp.where(lone, 0.0, cross)
            imag = jnp.where(lone, cross, kr * vi + ki * vr)
            y[:, at] = dot(back[long, :, :rows], real.astype(LOW)) + dot(
                back[long, :, rows:], imag.astype(LOW)
            )

        columns(width, product)
        stores.out("y", y, y_out.at[layer])

    def fetch_mlp(layer, i):
        first = 16 * layer + i
        fetch(("mlp", i), [first + 4, first + 8, first + 12], [wmlp.at[i % 2, j] for j in range(3)])

    def load(layer):
        fetch_mlp(layer, 0)

    def mix(layer):
        stores.settle("mixed", "mid", "b", "state")
        sums[layer].finish()
        stores.out("total", total.at[layer], total_out.at[layer])
        norm, _ = filter_norm_of(total.at[layer])
        mixed[...] = (y[...] * (spans / norm) * q[...]).astype(LOW)
        stores.out("mixed", mixed, mixed_out.at[layer])
        state[...] += dot(mixed[...], wfront[3])
        mid[...] = state[...]
        stores.out("mid", mid, mid_out.at[layer])
        normed, _ = normalize(state[...])
        b[...] = (normed * gains_ref[2 * layer + 1 : 2 * layer + 2, :]).astype(LOW)
        stores.out("b", b, b_out.at[layer])

    def mlp(layer, i):
        turn = i % 2
        fetched(("mlp", i))
        if i < 3:
            fetch_mlp(layer, i + 1)
        stores.settle(("g", turn))

        def body(at, turn=turn):
            gate = dot(b[...], wmlp[turn, 0, :, at])
            up = dot(b[...], wmlp[turn, 1, :, at])
            g[turn, :, at] = gate.astype(LOW)
            u[turn, :, at] = up.astype(LOW)
            h[turn, :, at] = (gate * jax.nn.sigmoid(gate) * up).astype(LOW)

        columns(width, body)
        for held_ref, out in ((g, g_out), (u, u_out), (h, h_out)):
            stores.out(("g", turn), held_ref.at[turn], out.at[layer, i])
        state[...] += dot(h[turn], wmlp[turn, 2])
        if i == 3 and layer == layers - 1:
            tok[...] = state[...].astype(LOW)
            stores.out("act", tok, act_out)

    compute = types.SimpleNamespace(
        front_a=front_a, front_b=front_b, front_c=front_c, sum_turn=sum_turn, mix=mix, load=load, mlp=mlp
    )
    run_plan(forward_plan(layers, gather.stages, n_fsdp), gather, compute)
    gather.drain()
    for one in sums:
        one.drain()
    stores.settle()


def forward(n_dp, n_fsdp, scalars, owner_slots, master, tokens, gains, tables):
    blocks = owner_slots.shape[0]
    layers = blocks // 16
    part_rows, cols = master.shape[1:]
    rows, width = tokens.shape
    stages = blocks // n_dp
    row = (rows, width)
    spectrum = (2 * rows, width)
    saved = [
        (row, LOW), (row, F32), (row, F32), (spectrum, LOW), (spectrum, LOW), (row, F32), (row, LOW), (row, F32), (row, LOW),
        ((4,) + row, LOW), ((4,) + row, LOW), ((4,) + row, LOW), ((8, width), F32), (row, F32),
    ]
    count = copy_count(n_dp, n_fsdp, stages, 1, n_fsdp, 3 * n_fsdp) + layers * (n_dp + n_fsdp - 2)
    any_space = pl.BlockSpec(memory_space=pl.ANY)
    scalar = pl.BlockSpec(memory_space=pltpu.SMEM)
    vmem = pl.BlockSpec(memory_space=pltpu.VMEM)
    return pl.pallas_call(
        functools.partial(forward_kernel, n_dp, n_fsdp, layers),
        name="forward",
        out_shape=[jax.ShapeDtypeStruct((stages, n_dp // 2, 2, width, width), LOW)]
        + [jax.ShapeDtypeStruct((layers,) + shape, kind) for shape, kind in saved]
        + [jax.ShapeDtypeStruct(row, LOW)],
        in_specs=[scalar] * 3 + [any_space, any_space, vmem, any_space, any_space],
        out_specs=[any_space] * (2 + len(saved)),
        scratch_shapes=[
            pltpu.VMEM(master.shape, F32),
            pltpu.VMEM((stages, 2, n_dp // 4, part_rows, cols), LOW),
            pltpu.VMEM((stages, 2, n_dp // 4, part_rows, cols), LOW),
        ]
        + plane_sum_shapes(n_dp, (stages,), part_rows, cols)
        + [
            pltpu.VMEM(row, LOW),
            pltpu.VMEM(row, F32),
            pltpu.VMEM(tables[0].shape, LOW),
            pltpu.VMEM(tables[1].shape, LOW),
            pltpu.VMEM((4, width, width), LOW),
            pltpu.VMEM((2, 3, width, width), LOW),
        ]
        + [pltpu.VMEM(shape, kind) for shape, kind in saved[:9]]
        + [pltpu.VMEM((2,) + row, LOW)] * 3
        + [
            pltpu.VMEM((layers, 8, width), F32),
            pltpu.VMEM((layers, n_fsdp, 8, width), F32),
            pltpu.VMEM((layers, n_dp, 8, width), F32),
            pltpu.VMEM((layers, 8, width), F32),
            pltpu.VMEM((layers, 8, width), F32),
            pltpu.SemaphoreType.DMA((count,)),
            pltpu.SemaphoreType.DMA((count,)),
            pltpu.SemaphoreType.DMA((stages + 8 + layers * 48,)),
        ],
        compiler_params=pltpu.CompilerParams(
            collective_id=0, has_side_effects=True, vmem_limit_bytes=VMEM_BYTES
        ),
    )(owner_slots, *scalars, master, tokens, gains, *tables)


class Scatter:
    def __init__(self, place, copies, stores, order, grads, landed, out_ref, acc, aside, from_a, from_b, credits, *sum_refs):
        self.place, self.copies, self.stores, self.order = place, copies, stores, order
        self.grads, self.landed, self.out_ref = grads, landed, out_ref
        self.acc, self.aside, self.from_a, self.from_b = acc, aside, from_a, from_b
        self.credits = credits
        self.slots, self.size = acc.shape[0], acc.shape[-2]
        self.rows = self.size // place.depth
        self.late = from_b.shape[-2]
        self.early = self.rows - self.late
        self.spots = place.up * place.across
        self.stages = len(order)
        self.sums = [
            [
                PlaneSum(
                    place, copies, acc.at[n % self.slots],
                    self.window(place.z_at(k), 0, self.early if k else self.rows),
                    self.early if k else self.rows,
                    *(ref.at[n % self.slots, k] for ref in sum_refs),
                )
                for k in range(place.depth)
            ]
            for n in range(self.stages)
        ]
        whole = pl.ds(0, self.rows)
        self.spreads = [PlaneSpread(place, copies, out_ref.at[s], whole) for s in order]
        self.over = [{} for _ in order]
        self.along_a = [{} for _ in order]
        self.along_b = [[] for _ in order]

    def window(self, z, first, count):
        return pl.ds(pl.multiple_of(z * self.rows + first, 16), count)

    def near(self):
        p = self.place
        peers = [(p.dp(x=p.x_at(k)), p.z) for k in range(1, p.across)]
        return peers + [(p.dp(y=p.y_at(m)), p.z) for m in range(1, p.up)]

    def column(self):
        p = self.place
        return [(p.d, p.z_at(k)) for k in range(1, p.depth)]

    def free(self, n, kind, peers):
        if n + self.slots < self.stages:
            for peer in peers:
                pl.semaphore_signal(
                    self.credits.at[kind, n], inc=1, device_id=peer, device_id_type=MESH
                )

    def claim(self, n, kind, peers):
        if n >= self.slots:
            pl.semaphore_wait(self.credits.at[kind, n - self.slots], len(peers))

    def grad(self, n, spot, core):
        return self.grads.at[self.place.n_dp * self.order[n] + 2 * spot + core]

    def offer(self, n, spot):
        p = self.place
        self.stores.settle(*[("outs", i) for i in range(4)])
        self.over[n][spot] = self.copies.to(
            self.grad(n, spot, 1 - p.core),
            self.landed.at[n * self.spots + spot],
            p.dp(core=1 - p.core),
            p.z,
        )
        self.over[n][spot].start()

    def sent(self, n):
        for one in self.sums[n]:
            one.drain()
        for copy in list(self.along_a[n].values()) + self.along_b[n]:
            copy.wait_send()

    def join(self, n, spot):
        p, slot = self.place, n % self.slots
        if n >= self.slots and spot == 0:
            self.sent(n - self.slots)
        target = self.acc.at[slot, spot // p.across, spot % p.across]
        own = self.copies.here(self.grad(n, spot, p.core), target)
        own.start()
        self.over[n][spot].wait_recv()
        aside = self.aside
        other = self.copies.here(self.landed.at[n * self.spots + spot], aside)
        other.start()
        own.wait()
        other.wait()
        add_into(target, [aside], self.size)

    def enter(self, n):
        p, slot = self.place, n % self.slots
        self.claim(n, 0, self.near())
        self.claim(n, 1, self.column())
        for k in range(1, p.depth):
            source = self.acc.at[slot, :, :, self.window(p.z_at(k), self.early, self.late), :]
            self.along_b[n].append(
                self.copies.to(source, self.from_b.at[slot, k - 1], p.d, p.z_at(k))
            )
        for copy in self.along_b[n]:
            copy.start()

    def push(self, n, k):
        p, slot = self.place, n % self.slots
        if k == 0:
            for copy in self.along_b[n]:
                copy.wait_recv()
            window = self.window(p.z, self.early, self.late)
            for y in range(p.up):
                for x in range(p.across):
                    terms = [self.from_b.at[slot, i, y, x] for i in range(p.depth - 1)]
                    add_into(self.acc.at[slot, y, x, window, :], terms, self.late)
        self.sums[n][k].start()

    def turn(self, n, k):
        self.sums[n][k].turn()

    def home(self, n, k):
        p, slot = self.place, n % self.slots
        self.sums[n][k].finish()
        if k > 0:
            source = self.acc.at[slot, p.y, p.x, self.window(p.z_at(k), 0, self.early), :]
            self.along_a[n][k] = self.copies.to(
                source, self.from_a.at[slot, k - 1], p.d, p.z_at(k)
            )
            self.along_a[n][k].start()

    def total(self, n):
        p, slot = self.place, n % self.slots
        self.free(n, 0, self.near())
        for copy in self.along_a[n].values():
            copy.wait_recv()
        terms = [self.from_a.at[slot, k - 1] for k in range(1, p.depth)]
        add_into(self.acc.at[slot, p.y, p.x, self.window(p.z, 0, self.early), :], terms, self.early)
        self.free(n, 1, self.column())
        total = self.acc.at[slot, p.y, p.x, self.window(p.z, 0, self.rows), :]
        own = self.out_ref.at[self.order[n], p.y * p.across + p.x, p.core]
        kept = self.copies.here(total, own)
        kept.start()
        kept.wait()
        self.spreads[n].start()

    def passing(self, n):
        self.spreads[n].forward()

    def close(self, n):
        self.spreads[n].finish()

    def done(self, n):
        self.spreads[n].arrived()

    def drain(self):
        for n in range(self.stages):
            for copy in self.over[n].values():
                copy.wait_send()
            if n + self.slots >= self.stages:
                self.sent(n)
            self.spreads[n].drain()


def grad_positions(layers):
    pairs = [4 + 2 * i for i in range(4)] + [5 + 2 * i for i in range(4)]
    one = np.array([12, 13, 14, 15] + pairs + [0, 1, 2, 3], np.int32)
    return jnp.asarray(np.concatenate([one + 16 * layer for layer in range(layers)]))


def backward_plan(layers, stages, depth):
    if (layers, stages, depth) == (2, 4, 4):
        return decode(BACKWARD_STEPS, BACKWARD_ORDER)
    plan = []
    for layer in reversed(range(layers)):
        plan += [("downs", layer)]
        for i, step in ((0, "gates"), (1, "gates"), (0, "inputs"), (1, "inputs")):
            plan += [(step, layer, i)]
        plan += [(step, layer, i) for i in (2, 3) for step in ("gates", "inputs")]
        plan += [(step, layer) for step in ("mix_a", "mix_b", "sum_turn", "front_a", "front_b")]
    spots = 8 * layers // stages
    plan += [("gain_turn", 0)] + [("offer", n, i) for n in range(stages) for i in range(spots)]
    for n in range(stages):
        plan += [("join", n, i) for i in range(spots)] + [("enter", n)]
        for k in list(range(1, depth)) + [0]:
            plan += [(step, n, k) for step in ("push", "turn", "home")]
        plan += [(step, n) for step in ("total", "passing", "close", "done")]
    return plan


def backward_kernel(n_dp, n_fsdp, layers, *refs):
    (
        flag_ref, count_ref, cotangent, w_ref, gains_ref, table_in, back_in,
        a_in, q_in, k_in, kh_in, vh_in, y_in, mixed_in, mid_in, b_in, g_in, u_in, h_in, total_in, state_in,
        red_ref, grad_out, gain_total, grads_ref, landed_ref,
        acc, from_x, from_y, last_y, last_x, from_a, from_b, aside,
        table, back, weights, tiles, outs, grad, sums, mid, q, y, low, b, mixed, dv, dq, dk,
        totals, part, by_z, by_d, mid_sum, total, send, recv, local, credits,
    ) = refs
    place = Place(n_dp, n_fsdp)
    copies = Copies(send, recv, local)
    stores = Stores(copies)
    rows, width = grad.shape
    valid = valid_rows(rows, count_ref[0])
    long = flag_ref[0]
    lone = lone_rows(rows, long)
    spans = span_scale(rows, flag_ref[0])
    waiting = {}

    def fetch(name, *pairs):
        waiting[name] = [copies.here(*pair) for pair in pairs]
        for copy in waiting[name]:
            copy.start()

    def fetched(*names):
        for name in names:
            for copy in waiting.pop(name):
                copy.wait()

    def fetch_mlp(layer, i):
        first, turn = 16 * layer + i, i % 2
        fetch(
            ("mlp", i),
            *[(w_ref.at[first + 4 * (j + 1)], weights.at[3 * turn + j]) for j in range(3)],
            *[(ref.at[layer, i], tiles.at[turn, j]) for j, ref in enumerate((g_in, u_in))],
        )

    hidden = (tiles.at[0, 2], tiles.at[1, 2], dv, dq)

    def fetch_layer(layer):
        fetch("b", (b_in.at[layer], b))
        fetch("hidden", *[(h_in.at[layer, i], ref) for i, ref in enumerate(hidden)])
        fetch_mlp(layer, 0)
        fetch_mlp(layer, 1)

    def store_grad(layer, slot, position):
        target = grads_ref.at[16 * layer + position]
        stores.out(("outs", slot), outs.at[slot], target)

    fetch("cotangent", (cotangent, grad))
    fetch_layer(layers - 1)
    fetch("tables", (table_in, table), (back_in, back))
    fetch("totals", (total_in, totals))
    place.greet_all()
    each = 16 // n_dp
    order = [layer * each + i for layer in reversed(range(layers)) for i in range(each)]
    scatter = Scatter(
        place, copies, stores, order, grads_ref, landed_ref, red_ref, acc, aside, from_a, from_b, credits, from_x, from_y, last_y, last_x
    )
    row_sums = [
        RowSum(place, copies, *(ref.at[i] for ref in (part, by_z, by_d, mid_sum, total)))
        for i in range(layers + 1)
    ]
    part[layers] = jnp.zeros(part.shape[1:], F32)

    def begin(layer):
        if layer == layers - 1:
            fetched("cotangent")
            grad[...] = grad[...] * valid
        low[...] = grad[...].astype(LOW)
        sums[...] = jnp.zeros_like(sums)
        fetch("mid", (mid_in.at[layer], mid))
        fetch("mix", (q_in.at[layer], q), (y_in.at[layer], y), (mixed_in.at[layer], mixed))
        fetched("b")

    def downs(layer):
        begin(layer)
        fetched("hidden")
        for i in range(4):
            stores.settle(("outs", i))

            def body(at, i=i):
                outs[i, at, :] = dot_tn(hidden[i][:, at], low[...]).astype(LOW)

            columns(width, body)
            store_grad(layer, i, i)

    def gates(layer, i):
        turn, slot = i % 2, 2 * (i % 2)
        fetched(("mlp", i))
        stores.settle(("outs", slot), ("outs", slot + 1))

        def body(at):
            dhidden = dot_nt(low[...], weights[3 * turn + 2, at, :])
            gate = tiles[turn, 0, :, at].astype(F32)
            up = tiles[turn, 1, :, at].astype(F32)
            sig = jax.nn.sigmoid(gate)
            dup = (dhidden * gate * sig).astype(LOW)
            dgate = (dhidden * up * sig * (1.0 + gate * (1.0 - sig))).astype(LOW)
            tiles[turn, 0, :, at] = dgate
            tiles[turn, 1, :, at] = dup
            outs[slot, :, at] = dot_tn(b[...], dgate).astype(LOW)
            outs[slot + 1, :, at] = dot_tn(b[...], dup).astype(LOW)

        columns(width, body)
        store_grad(layer, slot, 4 + 2 * i)
        store_grad(layer, slot + 1, 5 + 2 * i)

    def inputs(layer, i):
        turn = i % 2
        gate_part = dot_nt(tiles[turn, 0], weights[3 * turn])
        sums[...] += gate_part + dot_nt(tiles[turn, 1], weights[3 * turn + 1])
        if i < 2:
            fetch_mlp(layer, i + 2)
        elif i == 2:
            places = [(16 * layer + 3, 0), (16 * layer, 1), (16 * layer + 1, 2)]
            fetch("front", *[(w_ref.at[j], weights.at[to]) for j, to in places])
            fetch("kh", *[(kh_in.at[layer, pl.ds(rows * j, rows)], tiles.at[0, j]) for j in range(2)])
        else:
            fetch("key", (w_ref.at[16 * layer + 2], weights.at[3]))
            fetch("vh", *[(vh_in.at[layer, pl.ds(rows * j, rows)], tiles.at[1, j]) for j in range(2)])
            fetch("a", (a_in.at[layer], b))

    def mix_a(layer):
        if layer == layers - 1:
            fetched("tables", "totals")
        fetched("mid")
        normed, rstd = normalize(mid[...])
        db = sums[...]
        part[layers, 2 * layer + 1 : 2 * layer + 2, :] = jnp.sum(db * normed, 0, keepdims=True)
        gain = gains_ref[2 * layer + 1 : 2 * layer + 2, :]
        grad[...] += norm_back(db * gain, normed, rstd)
        low[...] = grad[...].astype(LOW)
        fetch("k", (k_in.at[layer], mid))
        norm, _ = filter_norm_of(totals.at[layer])
        scale_row = spans / norm
        sums[0:1, :] = scale_row
        part[layer] = jnp.zeros(part.shape[1:], F32)
        fetched("mix", "front", "kh", "vh")

        def through(at):
            dmixed = dot_nt(low[...], weights[0, at, :])
            dq[:, at] = (dmixed * y[:, at] * sums[0:1, at]).astype(LOW)
            dy = dmixed * q[:, at]
            part[layer, 0:1, at] = jnp.sum(dy * y[:, at], 0, keepdims=True) * spans
            q[:, at] = dy

        columns(width, through)
        row_sums[layer].start()

    def mix_b(layer):
        def body(at):
            dh = dot(table[long], q[:, at].astype(LOW))
            dr, di = dh[:rows], dh[rows:]

            def against(turn):
                other_r = tiles[turn, 0, :, at].astype(F32)
                other_i = tiles[turn, 1, :, at].astype(F32)
                cross = di * other_i
                real = dr * other_r + jnp.where(lone, 0.0, cross)
                imag = jnp.where(lone, cross, di * other_r - dr * other_i)
                return dot(back[long, :, :rows], real.astype(LOW)) + dot(
                    back[long, :, rows:], imag.astype(LOW)
                )

            y[:, at] = against(1)
            dv[:, at] = (against(0) * sums[0:1, at] * valid).astype(LOW)

        columns(width, body)
        fetch("state", (state_in.at[layer], q))

    def sum_turn(layer):
        row_sums[layer].turn()

    def gain_turn(_):
        row_sums[layers].turn()

    def front_a(layer):
        fetched("a", "key")
        stores.settle(*[("outs", i) for i in range(4)])

        def body(at):
            outs[3, at, :] = dot_tn(mixed[:, at], low[...]).astype(LOW)
            outs[0, :, at] = dot_tn(b[...], dv[:, at]).astype(LOW)
            outs[1, :, at] = dot_tn(b[...], dq[:, at]).astype(LOW)

        columns(width, body)
        sums[...] = dot_nt(dv[...], weights[1]) + dot_nt(dq[...], weights[2])

    def front_b(layer):
        fetched("k")
        row_sums[layer].finish()
        norm, live = filter_norm_of(totals.at[layer])
        square = -total[layer, 0:1, :] / (norm * norm) / (2.0 * norm * live)
        dk[...] = ((y[...] * (spans / norm) + 2.0 * mid[...] * square) * valid).astype(LOW)

        def keys(at):
            outs[2, :, at] = dot_tn(b[...], dk[:, at]).astype(LOW)

        columns(width, keys)
        for j in range(4):
            store_grad(layer, j, 12 + j)
        sums[...] += dot_nt(dk[...], weights[3])
        if layer > 0:
            fetch_layer(layer - 1)
        fetched("state")
        da = sums[...]
        normed, rstd = normalize(q[...])
        part[layers, 2 * layer : 2 * layer + 1, :] = jnp.sum(da * normed, 0, keepdims=True)
        gain = gains_ref[2 * layer : 2 * layer + 1, :]
        grad[...] += norm_back(da * gain, normed, rstd)
        if layer == 0:
            stores.out("grad", grad, grad_out)
            row_sums[layers].start()

    compute = types.SimpleNamespace(
        downs=downs, gates=gates, inputs=inputs, mix_a=mix_a, mix_b=mix_b, front_a=front_a, front_b=front_b,
        sum_turn=sum_turn, gain_turn=gain_turn,
    )
    run_plan(backward_plan(layers, scatter.stages, n_fsdp), scatter, compute)
    row_sums[layers].finish()
    gain_total[...] = total[layers]
    scatter.drain()
    for one in row_sums:
        one.drain()
    stores.settle()


def backward(n_dp, n_fsdp, scalars, cotangent, weights, gains, tables, saved):
    width = weights.shape[-1]
    weights = weights.reshape(-1, width, width)
    blocks = weights.shape[0]
    layers = blocks // 16
    rows = cotangent.shape[0]
    stages = blocks // n_dp
    spots = n_dp // 2
    slots = 2 if n_dp == 8 else 1
    part_rows = width // n_fsdp
    row = (rows, width)
    late = max(16, part_rows // 6 // 16 * 16)
    spread_count = spots + 2 * (n_fsdp - 1)
    count = copy_count(n_dp, n_fsdp, stages, n_fsdp, 1, spread_count)
    count += (layers + 1) * (n_dp + n_fsdp - 2)
    any_space = pl.BlockSpec(memory_space=pl.ANY)
    scalar = pl.BlockSpec(memory_space=pltpu.SMEM)
    vmem = pl.BlockSpec(memory_space=pltpu.VMEM)
    return pl.pallas_call(
        functools.partial(backward_kernel, n_dp, n_fsdp, layers),
        name="backward",
        out_shape=[
            jax.ShapeDtypeStruct((stages, n_dp // 2, 2, part_rows, width), LOW),
            jax.ShapeDtypeStruct(row, F32),
            jax.ShapeDtypeStruct((8, width), F32),
            jax.ShapeDtypeStruct((blocks, width, width), LOW),
            jax.ShapeDtypeStruct((blocks // 2, width, width), LOW),
        ],
        in_specs=[scalar, scalar, any_space, any_space, vmem] + [any_space] * (2 + len(saved)),
        out_specs=[any_space, any_space, vmem, any_space, any_space],
        scratch_shapes=[pltpu.VMEM((slots, 2, n_dp // 4, width, width), LOW)]
        + plane_sum_shapes(n_dp, (slots, n_fsdp), part_rows, width)
        + [
            pltpu.VMEM((slots, n_fsdp - 1, part_rows - late, width), LOW),
            pltpu.VMEM((slots, n_fsdp - 1, 2, n_dp // 4, late, width), LOW),
            pltpu.VMEM((width, width), LOW),
            pltpu.VMEM(tables[0].shape, LOW),
            pltpu.VMEM(tables[1].shape, LOW),
            pltpu.VMEM((6, width, width), LOW),
            pltpu.VMEM((2, 3) + row, LOW),
            pltpu.VMEM((4, width, width), LOW),
        ]
        + [pltpu.VMEM(row, F32)] * 5
        + [pltpu.VMEM(row, LOW)] * 6
        + [
            pltpu.VMEM((layers, 8, width), F32),
            pltpu.VMEM((layers + 1, 8, width), F32),
            pltpu.VMEM((layers + 1, n_fsdp, 8, width), F32),
            pltpu.VMEM((layers + 1, n_dp, 8, width), F32),
            pltpu.VMEM((layers + 1, 8, width), F32),
            pltpu.VMEM((layers + 1, 8, width), F32),
            pltpu.SemaphoreType.DMA((count,)),
            pltpu.SemaphoreType.DMA((count,)),
            pltpu.SemaphoreType.DMA((stages * (2 * spots + 1) + layers * 64 + 16,)),
            pltpu.SemaphoreType.REGULAR((2, stages)),
        ],
        compiler_params=pltpu.CompilerParams(
            collective_id=1, has_side_effects=True, vmem_limit_bytes=VMEM_BYTES
        ),
    )(*scalars, cotangent, weights, gains, *tables, *saved)


def call(kernel, name, grid, scalars, args, specs, outs, out_specs, scratch=()):
    return pl.pallas_call(
        kernel,
        name=name,
        out_shape=outs,
        grid_spec=pltpu.PrefetchScalarGridSpec(
            num_scalar_prefetch=len(scalars),
            grid=(grid,),
            in_specs=specs,
            out_specs=out_specs,
            scratch_shapes=scratch,
        ),
        compiler_params=pltpu.CompilerParams(vmem_limit_bytes=VMEM_BYTES),
    )(*scalars, *args)


def adam_step(grad, first, second, weight, rate, decay):
    first_out = 0.5 * first + 0.5 * grad
    second_out = 0.5 * second + 0.5 * grad * grad
    fix = 1.0 / (1.0 - 0.5**STEP)
    weight_out = weight - rate * (
        first_out * fix / (jnp.sqrt(second_out * fix) + ADAM_EPS) + decay * weight
    )
    return (first_out, second_out, weight_out)


def adam_kernel(
    block, used, grad_ref, master_ref, first_ref, second_ref, first_out, second_out, master_out
):
    taken = used[pl.program_id(0)] == 1
    first, second, master = first_ref[...], second_ref[...], master_ref[...]
    new = adam_step(grad_ref[...].astype(F32), first, second, master, 0.03, 0.01)
    first_out[...] = jnp.where(taken, new[0], first)
    second_out[...] = jnp.where(taken, new[1], second)
    master_out[...] = jnp.where(taken, new[2], master)


def adam_blocks(block, used, grads, master, first, second):
    shape = (1,) + master.shape[1:]
    own = pl.BlockSpec(shape, lambda i, block, used: (i, 0, 0))
    picked = pl.BlockSpec(shape, lambda i, block, used: (block[i], 0, 0))
    return call(
        adam_kernel,
        "adam",
        master.shape[0],
        (block, used),
        (grads, master, first, second),
        [picked, own, own, own],
        [jax.ShapeDtypeStruct(master.shape, F32)] * 3,
        [own] * 3,
    )


def on_device(
    n_dp,
    n_fsdp,
    tokens,
    cotangent,
    row_counts,
    bucket_flags,
    owner_slots,
    master,
    first_moment,
    second_moment,
    gains,
    gain_first,
    gain_second,
):
    rows = tokens.shape[0]
    slot_cap = master.shape[0]
    layers = owner_slots.shape[0] // 16
    tables = transform_tables(rows)
    scalars = (bucket_flags, row_counts)
    weights, *saved, activations = forward(
        n_dp, n_fsdp, scalars, owner_slots, master, tokens, gains, tables
    )
    summed, grad, gain_sums, _, _ = backward(
        n_dp, n_fsdp, scalars, cotangent, weights, gains, tables, saved
    )
    gains_total = gain_sums[: 2 * layers]
    my_slots = lax.axis_index("dp") * slot_cap + jnp.arange(slot_cap, dtype=jnp.int32)
    hits = owner_slots[None, :] == my_slots[:, None]
    used = jnp.any(hits, 1).astype(jnp.int32)
    block = jnp.sum(jnp.where(hits, grad_positions(layers)[None, :], 0), 1)
    first_out, second_out, master_out = adam_blocks(
        block, used, summed.reshape(-1, *master.shape[1:]), master, first_moment, second_moment
    )
    gain_m, gain_v, gain_w = adam_step(gains_total, gain_first, gain_second, gains, 0.2, 0.0)
    return (activations, grad, first_out, second_out, master_out, gain_m, gain_v, gain_w)


def solution(mesh):
    rows = P(("dp", "fsdp"), None)
    blocks = P("dp", "fsdp", None)
    flat = P(("dp", "fsdp"))
    return jax.shard_map(
        functools.partial(on_device, mesh.shape["dp"], mesh.shape["fsdp"]),
        mesh=mesh,
        in_specs=(rows, rows, flat, flat, P(), blocks, blocks, blocks, P(), P(), P()),
        out_specs=(rows, rows, blocks, blocks, blocks, P(), P(), P()),
        check_vma=False,
    )
```

```python
import functools
import math
import types

import jax
import jax.numpy as jnp
import numpy as np
from jax import lax
from jax.experimental import pallas as pl
from jax.experimental.pallas import tpu as pltpu
from jax.sharding import PartitionSpec as P

STEP = 5
NORM_EPS = 1e-05
ADAM_EPS = 1e-08
LOW = jnp.bfloat16
F32 = jnp.float32
MESH = pl.DeviceIdType.MESH
VMEM_BYTES = 60 * 2**20


FORWARD_STEPS = (
    ("fill", 1), ("enter", 1), ("turn", 1), ("home", 1), ("column", 1), ("cell", 2), ("passing", 2),
    ("close", 2), ("late", 1), ("share", 1), ("done", 1), ("front_a", 1), ("front_b", 1), ("sum_turn", 1),
    ("front_c", 1), ("mix", 1), ("load", 1), ("mlp", 2),
)
FORWARD_ORDER = (
    0, 10, 20, 100, 110, 200, 210, 300, 400, 310, 600, 120, 502, 410, 700, 610, 220, 511, 320, 420, 800, 503,
    620, 513, 602, 30, 603, 130, 501, 710, 611, 703, 810, 720, 230, 820, 601, 512, 701, 330, 521, 702, 900,
    1000, 1100, 430, 612, 910, 522, 630, 622, 613, 711, 621, 1200, 712, 523, 1300, 713, 1400, 721, 531, 1010,
    722, 730, 1600, 920, 830, 623, 1500, 1700, 532, 1701, 631, 1702, 723, 1703, 533, 1020, 1110, 632, 1210,
    633, 731, 930, 1310, 732, 1410, 733, 1510, 1030, 1610, 1710, 1711, 1712, 1713,
)
BACKWARD_STEPS = (
    ("downs", 1), ("gates", 2), ("inputs", 2), ("mix_a", 1), ("mix_b", 1), ("sum_turn", 1), ("front_a", 1),
    ("front_b", 1), ("gain_turn", 1), ("offer", 2), ("join", 2), ("enter", 1), ("push", 2), ("turn", 2),
    ("home", 2), ("total", 1), ("passing", 1), ("close", 1), ("done", 1),
)
BACKWARD_ORDER = (
    10, 110, 900, 901, 902, 111, 903, 1000, 1001, 1002, 1003, 1100, 1202, 210, 1201, 211, 1203, 112, 212, 113,
    910, 1301, 213, 1302, 1010, 310, 1200, 1401, 410, 510, 1402, 610, 911, 1303, 710, 912, 913, 1300, 1011,
    1403, 1012, 1013, 1110, 1213, 1211, 0, 921, 1400, 1500, 920, 100, 1020, 1313, 1212, 101, 922, 1021, 923,
    1600, 1311, 1413, 1022, 1023, 1120, 1221, 1210, 200, 201, 102, 1312, 1222, 202, 103, 1223, 203, 1321, 300,
    1411, 1412, 1310, 930, 400, 1700, 931, 500, 1322, 600, 1220, 1421, 1410, 1800, 700, 1510, 1422, 933, 932,
    1030, 1031, 1320, 1032, 1033, 1130, 1231, 1323, 1232, 1331, 1233, 1420, 1423, 1332, 1431, 1230, 1333,
    1610, 1432, 1330, 1433, 1520, 1710, 1430, 1810, 1530, 1620, 1630, 800, 1720, 1730, 1820, 1830,
)


def span_tables(length):
    period = 2 * length
    freqs = np.arange(length)[:, None]
    places = np.arange(length)[None, :]
    angle = (freqs * places % period) * (2.0 * math.pi / period)
    cosine, sine = np.cos(angle), -np.sin(angle)
    sine[0] = np.cos(math.pi * np.arange(length))
    weight = np.where(np.arange(length) == 0, 1.0, 2.0)[None, :] / period
    return (cosine, sine, cosine.T * weight, sine.T * weight)


def transform_tables(rows):
    short = [np.kron(np.eye(4), table) for table in span_tables(rows // 4)]
    full = span_tables(rows)
    forward = np.stack([np.concatenate(t[:2], 0) for t in (short, full)])
    inverse = np.stack([np.concatenate(t[2:], 1) for t in (short, full)])
    return (jnp.asarray(forward, LOW), jnp.asarray(inverse, LOW))


class Place:
    def __init__(self, n_dp, n_fsdp):
        self.n_dp, self.depth = n_dp, n_fsdp
        self.up, self.across = 2, n_dp // 4
        self.d = lax.axis_index("dp")
        self.z = lax.axis_index("fsdp")
        self.core = lax.rem(self.d, 2)
        self.x = lax.rem(self.d // 2, self.across)
        self.y = self.d // (2 * self.across)

    def x_at(self, k):
        return lax.rem(self.x + k + self.across, self.across)

    def y_at(self, m):
        return lax.rem(self.y + m + self.up, self.up)

    def z_at(self, k):
        return lax.rem(self.z + k + self.depth, self.depth)

    def dp(self, y=None, x=None, core=None):
        y = self.y if y is None else y
        x = self.x if x is None else x
        core = self.core if core is None else core
        return (y * self.across + x) * 2 + core

    def greet(self):
        barrier = pltpu.get_barrier_semaphore()
        peers = [(self.dp(core=1 - self.core), self.z)]
        peers += [(self.dp(x=self.x_at(k)), self.z) for k in range(1, self.across)]
        peers += [(self.dp(y=self.y_at(m)), self.z) for m in range(1, self.up)]
        peers += [(self.d, self.z_at(k)) for k in range(1, self.depth)]
        for peer in peers:
            pl.semaphore_signal(barrier, inc=1, device_id=peer, device_id_type=MESH)
        pl.semaphore_wait(barrier, len(peers))

    def greet_all(self):
        barrier = pltpu.get_barrier_semaphore()
        peers = [(lax.rem(self.d + k, self.n_dp), self.z) for k in range(1, self.n_dp)]
        peers += [(self.d, self.z_at(k)) for k in range(1, self.depth)]
        for peer in peers:
            pl.semaphore_signal(barrier, inc=1, device_id=peer, device_id_type=MESH)
        pl.semaphore_wait(barrier, len(peers))


class Copies:
    def __init__(self, send, recv, local):
        self.send, self.recv, self.local = send, recv, local
        self.sent, self.moved = 0, 0

    def to(self, source, target, dp, z):
        index = self.sent
        self.sent += 1
        return pltpu.make_async_remote_copy(
            src_ref=source,
            dst_ref=target,
            send_sem=self.send.at[index],
            recv_sem=self.recv.at[index],
            device_id=(dp, z),
            device_id_type=MESH,
        )

    def here(self, source, target):
        index = self.moved
        self.moved += 1
        return pltpu.make_async_copy(source, target, self.local.at[index])


def add_into(total, terms, rows):
    step = next(size for size in (48, 32, 16) if rows % size == 0)

    def piece(i, carry):
        at = pl.ds(pl.multiple_of(i * step, 16), step)
        value = total[at, :].astype(F32)
        for term in terms:
            value = value + term[at, :].astype(F32)
        total[at, :] = value.astype(LOW)
        return carry

    lax.fori_loop(0, rows // step, piece, 0)


class PlaneSum:
    def __init__(self, place, copies, acc, window, count, from_x, from_y, last_y, last_x):
        self.place, self.copies, self.acc, self.window, self.count = place, copies, acc, window, count
        self.from_x, self.from_y, self.last_y, self.last_x = from_x, from_y, last_y, last_x
        half = acc.shape[-1] // 2
        self.first, self.second = pl.ds(0, half), pl.ds(half, half)
        self.rows = pl.ds(0, count)

    def start(self):
        p, rows = self.place, self.rows
        self.one = []
        for k in range(1, p.across):
            source = self.acc.at[:, p.x_at(k), self.window, self.first]
            target = self.from_x.at[k - 1, :, rows]
            self.one.append(self.copies.to(source, target, p.dp(x=p.x_at(k)), p.z))
        for m in range(1, p.up):
            source = self.acc.at[p.y_at(m), :, self.window, self.second]
            target = self.from_y.at[m - 1, :, rows]
            self.one.append(self.copies.to(source, target, p.dp(y=p.y_at(m)), p.z))
        for copy in self.one:
            copy.start()

    def turn(self):
        p, rows = self.place, self.rows
        for copy in self.one:
            copy.wait_recv()
        for y in range(p.up):
            terms = [self.from_x.at[k - 1, y, rows] for k in range(1, p.across)]
            add_into(self.acc.at[y, p.x, self.window, self.first], terms, self.count)
        for x in range(p.across):
            terms = [self.from_y.at[m - 1, x, rows] for m in range(1, p.up)]
            add_into(self.acc.at[p.y, x, self.window, self.second], terms, self.count)
        self.two = []
        for m in range(1, p.up):
            source = self.acc.at[p.y_at(m), p.x, self.window, self.first]
            target = self.last_y.at[m - 1, rows]
            self.two.append(self.copies.to(source, target, p.dp(y=p.y_at(m)), p.z))
        for k in range(1, p.across):
            source = self.acc.at[p.y, p.x_at(k), self.window, self.second]
            target = self.last_x.at[k - 1, rows]
            self.two.append(self.copies.to(source, target, p.dp(x=p.x_at(k)), p.z))
        for copy in self.two:
            copy.start()

    def finish(self):
        p, rows = self.place, self.rows
        for copy in self.two:
            copy.wait_recv()
        terms = [self.last_y.at[m - 1, rows] for m in range(1, p.up)]
        add_into(self.acc.at[p.y, p.x, self.window, self.first], terms, self.count)
        terms = [self.last_x.at[k - 1, rows] for k in range(1, p.across)]
        add_into(self.acc.at[p.y, p.x, self.window, self.second], terms, self.count)

    def drain(self):
        for copy in self.one + self.two:
            copy.wait_send()


class PlaneSpread:
    def __init__(self, place, copies, array, window, source=None):
        self.place, self.copies, self.array = place, copies, array
        self.window, self.source = window, source
        half = array.shape[-1] // 2
        self.halves = (pl.ds(0, half), pl.ds(half, half))
        self.sends = []

    def block(self, half=None, y=None, x=None):
        p = self.place
        y, x = p.y if y is None else y, p.x if x is None else x
        view = self.array.at[y * p.across + x, p.core, self.window]
        return view if half is None else view.at[:, self.halves[half]]

    def fire(self, ref, dp, source=None):
        copy = self.copies.to(ref if source is None else source, ref, dp, self.place.z)
        copy.start()
        self.sends.append(copy)
        return copy

    def start(self):
        p, own = self.place, self.block()
        self.by_x = [self.fire(own, p.dp(x=p.x_at(k)), self.source) for k in range(1, p.across)]
        self.by_y = [self.fire(own, p.dp(y=p.y_at(m)), self.source) for m in range(1, p.up)]

    def forward(self):
        p = self.place
        self.last = []
        for k in range(1, p.across):
            self.by_x[k - 1].wait_recv()
            for m in range(1, p.up):
                self.last.append(self.fire(self.block(0, x=p.x_at(-k)), p.dp(y=p.y_at(m))))
        for m in range(1, p.up):
            self.by_y[m - 1].wait_recv()
            for k in range(1, p.across):
                self.last.append(self.fire(self.block(1, y=p.y_at(-m)), p.dp(x=p.x_at(k))))

    def finish(self):
        for copy in self.last:
            copy.wait_recv()
        self.hand_over(self.window)

    def hand_over(self, window):
        p = self.place
        self.over = self.fire(self.array.at[:, p.core, window], p.dp(core=1 - p.core))

    def arrived(self):
        self.over.wait_recv()

    def drain(self):
        for copy in self.sends:
            copy.wait_send()


def plane_sum_shapes(n_dp, lead, rows, cols):
    up, across, half = 2, n_dp // 4, cols // 2
    return [
        pltpu.VMEM(lead + (across - 1, up, rows, half), LOW),
        pltpu.VMEM(lead + (up - 1, across, rows, half), LOW),
        pltpu.VMEM(lead + (up - 1, rows, half), LOW),
        pltpu.VMEM(lead + (across - 1, rows, half), LOW),
    ]


def copy_count(n_dp, n_fsdp, stages, sums, spreads, others):
    up, across = 2, n_dp // 4
    near = up - 1 + across - 1
    diagonal = (up - 1) * (across - 1)
    each_spread = near + 2 * diagonal + 1
    return stages * (sums * 2 * near + spreads * each_spread + others)


def run_plan(plan, *actors):
    for name, *where in plan:
        actor = next(a for a in actors if hasattr(a, name))
        getattr(actor, name)(*where)


def decode(steps, codes):
    plan = []
    for code in codes:
        name, count = steps[code // 100]
        plan.append((name, code // 10 % 10, code % 10)[: count + 1])
    return plan


def dot(left, right):
    return jnp.dot(left, right, preferred_element_type=F32)


def dot_nt(left, right):
    return lax.dot_general(left, right, (((1,), (1,)), ((), ())), preferred_element_type=F32)


def dot_tn(left, right):
    return lax.dot_general(left, right, (((0,), (0,)), ((), ())), preferred_element_type=F32)


def normalize(inputs):
    centred = inputs - jnp.mean(inputs, -1, keepdims=True)
    rstd = lax.rsqrt(jnp.mean(centred * centred, -1, keepdims=True) + NORM_EPS)
    return (centred * rstd, rstd)


def norm_back(grad, normed, rstd):
    return rstd * (
        grad
        - jnp.mean(grad, -1, keepdims=True)
        - normed * jnp.mean(grad * normed, -1, keepdims=True)
    )


def valid_rows(rows, count):
    return (lax.broadcasted_iota(jnp.int32, (rows, 1), 0) < count).astype(F32)


def lone_rows(rows, flag):
    span = jnp.where(flag == 1, rows, rows // 4)
    return lax.rem(lax.broadcasted_iota(jnp.int32, (rows, 1), 0), span) == 0


def span_scale(rows, flag):
    return jnp.where(flag == 1, rows**-0.5, (rows // 4) ** -0.5).astype(F32)


def filter_norm_of(total_ref):
    live = total_ref[1:2, :]
    return (jnp.sqrt(total_ref[0:1, :] / live + NORM_EPS), live)


def columns(width, body):
    for at in range(0, width, 256):
        body(pl.ds(at, 256))


class RowSum:
    def __init__(self, place, copies, part, by_z, by_d, mid, total):
        self.place, self.copies = place, copies
        self.part, self.by_z, self.by_d, self.mid, self.total = part, by_z, by_d, mid, total

    def start(self):
        p = self.place
        self.one = [
            self.copies.to(self.part, self.by_z.at[p.z], p.d, p.z_at(k)) for k in range(1, p.depth)
        ]
        for copy in self.one:
            copy.start()
        self.by_z[p.z] = self.part[...]

    def turn(self):
        p = self.place
        for copy in self.one:
            copy.wait_recv()
        total = self.by_z[0]
        for i in range(1, p.depth):
            total = total + self.by_z[i]
        self.mid[...] = total
        self.two = [
            self.copies.to(self.mid, self.by_d.at[p.d], lax.rem(p.d + k, p.n_dp), p.z)
            for k in range(1, p.n_dp)
        ]
        for copy in self.two:
            copy.start()
        self.by_d[p.d] = total

    def finish(self):
        for copy in self.two:
            copy.wait_recv()
        total = self.by_d[0]
        for i in range(1, self.place.n_dp):
            total = total + self.by_d[i]
        self.total[...] = total

    def drain(self):
        for copy in self.one + self.two:
            copy.wait_send()


class Gather:
    def __init__(self, place, copies, slots_ref, master_ref, out_ref, held, acc, *sum_refs):
        self.place, self.copies, self.slots_ref, self.master_ref = place, copies, slots_ref, master_ref
        self.out_ref, self.held, self.acc = out_ref, held, acc
        self.stages = stages = acc.shape[0]
        self.slot_cap, self.rows, _ = master_ref.shape
        self.piece_rows = 48 if self.rows % 48 == 0 else 16
        self.late_rows = max(16, self.rows // 6 // 16 * 16)
        early = self.early = self.rows - self.late_rows
        whole = pl.ds(0, self.rows)
        self.sums = [
            PlaneSum(place, copies, acc.at[s], whole, self.rows, *(ref.at[s] for ref in sum_refs))
            for s in range(stages)
        ]
        self.cells = [
            [
                PlaneSpread(
                    place, copies, out_ref.at[s], self.rows_of(place.z_at(-k), early if k else self.rows),
                    acc.at[s, place.y, place.x] if k == 0 else None,
                )
                for k in range(place.depth)
            ]
            for s in range(stages)
        ]
        self.over, self.along_z, self.kept = [None] * stages, [None] * stages, [None] * stages
        self.lates = [None] * stages
        self.shares = [[] for _ in range(stages)]

    def rows_of(self, z, count, first=0):
        return pl.ds(pl.multiple_of(z * self.rows + first, 16), count)

    def own(self, s, window):
        p = self.place
        return self.out_ref.at[s, p.y * p.across + p.x, p.core, window]

    def masked(self, s, y, x, core, at):
        slot = self.slots_ref[self.place.n_dp * s + self.place.dp(y, x, core)]
        low = slot - self.place.d * self.slot_cap
        mine = (low >= 0) & (low < self.slot_cap)
        index = jnp.clip(low, 0, self.slot_cap - 1)
        return jnp.where(mine, self.master_ref[index, at, :], 0.0).astype(LOW)

    def each_piece(self, body):
        p, rows = self.place, self.piece_rows
        pieces = self.rows // rows

        def one(i, carry):
            spot, piece = i // pieces, lax.rem(i, pieces)
            y, x = spot // p.across, lax.rem(spot, p.across)
            body(y, x, pl.ds(pl.multiple_of(piece * rows, 16), rows))
            return carry

        lax.fori_loop(0, p.up * p.across * pieces, one, 0)

    def fill(self, s):
        p = self.place

        def body(y, x, at):
            self.held[s, y, x, at, :] = self.masked(s, y, x, 1 - p.core, at)

        self.each_piece(body)
        self.over[s] = self.copies.to(
            self.held.at[s], self.acc.at[s], p.dp(core=1 - p.core), p.z
        )
        self.over[s].start()

    def enter(self, s):
        self.over[s].wait_recv()

        def join(y, x, at):
            mine = self.masked(s, y, x, self.place.core, at)
            self.acc[s, y, x, at, :] = self.acc[s, y, x, at, :] + mine

        self.each_piece(join)
        self.sums[s].start()

    def turn(self, s):
        self.sums[s].turn()

    def home(self, s):
        p = self.place
        self.sums[s].finish()
        target = self.own(s, self.rows_of(p.z, self.rows))
        self.kept[s] = self.copies.here(self.acc.at[s, p.y, p.x], target)
        self.kept[s].start()
        self.cells[s][0].start()

    def column(self, s):
        p = self.place
        source = self.acc.at[s, p.y, p.x, pl.ds(0, self.early), :]
        target = self.own(s, self.rows_of(p.z, self.early))
        self.along_z[s] = [
            self.copies.to(source, target, p.d, p.z_at(k)) for k in range(1, p.depth)
        ]
        for copy in self.along_z[s]:
            copy.start()

    def cell(self, s, k):
        self.along_z[s][k - 1].wait_recv()
        self.cells[s][k].start()

    def passing(self, s, k):
        self.cells[s][k].forward()

    def close(self, s, k):
        if k == 0:
            self.kept[s].wait()
        self.cells[s][k].finish()

    def late(self, s):
        p = self.place
        view = self.out_ref.at[s, :, p.core, self.rows_of(p.z, self.late_rows, self.early)]
        self.lates[s] = [self.copies.to(view, view, p.d, p.z_at(k)) for k in range(1, p.depth)]
        for copy in self.lates[s]:
            copy.start()

    def share(self, s):
        p = self.place
        for k in range(1, p.depth):
            self.lates[s][k - 1].wait_recv()
            rows = self.rows_of(p.z_at(-k), self.late_rows, self.early)
            view = self.out_ref.at[s, :, p.core, rows]
            self.shares[s].append(self.copies.to(view, view, p.dp(core=1 - p.core), p.z))
            self.shares[s][-1].start()

    def done(self, s):
        for cell in self.cells[s]:
            cell.arrived()
        for copy in self.shares[s]:
            copy.wait_recv()

    def drain(self):
        for s in range(self.stages):
            self.over[s].wait_send()
            self.sums[s].drain()
            for copy in self.along_z[s] + self.lates[s] + self.shares[s]:
                copy.wait_send()
            for cell in self.cells[s]:
                cell.drain()


class Stores:
    def __init__(self, copies):
        self.copies, self.open = copies, {}

    def out(self, name, source, target):
        copy = self.copies.here(source, target)
        copy.start()
        self.open.setdefault(name, []).append(copy)

    def settle(self, *names):
        for name in names or list(self.open):
            for copy in self.open.pop(name, []):
                copy.wait()


def forward_plan(layers, stages, depth):
    if (layers, stages, depth) == (2, 4, 4):
        return decode(FORWARD_STEPS, FORWARD_ORDER)
    plan = []
    for s in range(stages):
        plan += [(step, s) for step in ("fill", "enter", "turn", "home", "column")]
        for k in range(depth):
            plan += [("cell", s, k)] if k else []
            plan += [("passing", s, k), ("close", s, k)]
        plan += [(step, s) for step in ("late", "share", "done")]
        for layer in range(layers):
            if s == (layer + 1) * stages // layers - 1:
                steps = ("front_a", "front_b", "sum_turn", "front_c", "mix", "load")
                plan += [(step, layer) for step in steps]
                plan += [("mlp", layer, i) for i in range(4)]
    return plan


def forward_kernel(n_dp, n_fsdp, layers, *refs):
    (
        slots_ref, flag_ref, count_ref, master_in, tokens_in, gains_ref, table_in, back_in,
        w_ref, a_out, q_out, k_out, kh_out, vh_out, y_out, mixed_out, mid_out, b_out, g_out, u_out, h_out,
        total_out, state_out, act_out,
        master, held, acc, from_x, from_y, last_y, last_x,
        tok, state, table, back, wfront, wmlp, a, q, k, kh, vh, y, mixed, mid, b, g, u, h,
        part, by_z, by_d, mid_sum, total, send, recv, local,
    ) = refs
    place = Place(n_dp, n_fsdp)
    copies = Copies(send, recv, local)
    stores = Stores(copies)
    rows, width = state.shape
    load_master = copies.here(master_in, master)
    load_master.start()
    loads = [copies.here(*pair) for pair in ((tokens_in, tok), (table_in, table), (back_in, back))]
    for copy in loads:
        copy.start()
    place.greet_all()
    load_master.wait()
    gather = Gather(place, copies, slots_ref, master, w_ref, held, acc, from_x, from_y, last_y, last_x)
    sums = [
        RowSum(place, copies, *(ref.at[layer] for ref in (part, by_z, by_d, mid_sum, total)))
        for layer in range(layers)
    ]
    valid = valid_rows(rows, count_ref[0])
    long = flag_ref[0]
    lone = lone_rows(rows, long)
    spans = span_scale(rows, flag_ref[0])
    waiting = {}

    def fetch(name, blocks, targets):
        waiting[name] = [
            copies.here(w_ref.at[j // n_dp, j % n_dp // 2, j % 2], t)
            for j, t in zip(blocks, targets)
        ]
        for copy in waiting[name]:
            copy.start()

    def fetched(name):
        for copy in waiting.pop(name):
            copy.wait()

    def front_a(layer):
        fetch("front", [16 * layer + i for i in range(4)], [wfront.at[i] for i in range(4)])
        if layer == 0:
            for copy in loads:
                copy.wait()
            state[...] = tok[...].astype(F32)
        stores.settle("a", "k", "q", "kh", "vh", "y")
        stores.out("state", state, state_out.at[layer])
        normed, _ = normalize(state[...])
        a[...] = (normed * gains_ref[2 * layer : 2 * layer + 1, :]).astype(LOW)
        stores.out("a", a, a_out.at[layer])
        part[layer] = jnp.broadcast_to(jnp.sum(valid), part.shape[1:])
        fetched("front")

        def keys(at):
            value = dot(a[...], wfront[2, :, at]) * valid
            k[:, at] = value
            part[layer, 0:1, at] = jnp.sum(value * value, 0, keepdims=True)

        columns(width, keys)
        sums[layer].start()
        stores.out("k", k, k_out.at[layer])

    def front_b(layer):
        def spectra(at):
            q[:, at] = dot(a[...], wfront[1, :, at])
            values = (dot(a[...], wfront[0, :, at]) * valid).astype(LOW)
            kh[:, at] = dot(table[long], k[:, at].astype(LOW)).astype(LOW)
            vh[:, at] = dot(table[long], values).astype(LOW)

        columns(width, spectra)
        stores.out("q", q, q_out.at[layer])
        stores.out("kh", kh, kh_out.at[layer])
        stores.out("vh", vh, vh_out.at[layer])

    def sum_turn(layer):
        sums[layer].turn()

    def front_c(layer):
        def product(at):
            kr, ki = kh[:rows, at].astype(F32), kh[rows:, at].astype(F32)
            vr, vi = vh[:rows, at].astype(F32), vh[rows:, at].astype(F32)
            cross = ki * vi
            real = kr * vr - jnp.where(lone, 0.0, cross)
            imag = jnp.where(lone, cross, kr * vi + ki * vr)
            y[:, at] = dot(back[long, :, :rows], real.astype(LOW)) + dot(
                back[long, :, rows:], imag.astype(LOW)
            )

        columns(width, product)
        stores.out("y", y, y_out.at[layer])

    def fetch_mlp(layer, i):
        first = 16 * layer + i
        fetch(("mlp", i), [first + 4, first + 8, first + 12], [wmlp.at[i % 2, j] for j in range(3)])

    def load(layer):
        fetch_mlp(layer, 0)

    def mix(layer):
        stores.settle("mixed", "mid", "b", "state")
        sums[layer].finish()
        stores.out("total", total.at[layer], total_out.at[layer])
        norm, _ = filter_norm_of(total.at[layer])
        mixed[...] = (y[...] * (spans / norm) * q[...]).astype(LOW)
        stores.out("mixed", mixed, mixed_out.at[layer])
        state[...] += dot(mixed[...], wfront[3])
        mid[...] = state[...]
        stores.out("mid", mid, mid_out.at[layer])
        normed, _ = normalize(state[...])
        b[...] = (normed * gains_ref[2 * layer + 1 : 2 * layer + 2, :]).astype(LOW)
        stores.out("b", b, b_out.at[layer])

    def mlp(layer, i):
        turn = i % 2
        fetched(("mlp", i))
        if i < 3:
            fetch_mlp(layer, i + 1)
        stores.settle(("g", turn))

        def body(at, turn=turn):
            gate = dot(b[...], wmlp[turn, 0, :, at])
            up = dot(b[...], wmlp[turn, 1, :, at])
            g[turn, :, at] = gate.astype(LOW)
            u[turn, :, at] = up.astype(LOW)
            h[turn, :, at] = (gate * jax.nn.sigmoid(gate) * up).astype(LOW)

        columns(width, body)
        for held_ref, out in ((g, g_out), (u, u_out), (h, h_out)):
            stores.out(("g", turn), held_ref.at[turn], out.at[layer, i])
        state[...] += dot(h[turn], wmlp[turn, 2])
        if i == 3 and layer == layers - 1:
            tok[...] = state[...].astype(LOW)
            stores.out("act", tok, act_out)

    compute = types.SimpleNamespace(
        front_a=front_a, front_b=front_b, front_c=front_c, sum_turn=sum_turn, mix=mix, load=load, mlp=mlp
    )
    run_plan(forward_plan(layers, gather.stages, n_fsdp), gather, compute)
    gather.drain()
    for one in sums:
        one.drain()
    stores.settle()


def forward(n_dp, n_fsdp, scalars, owner_slots, master, tokens, gains, tables):
    blocks = owner_slots.shape[0]
    layers = blocks // 16
    part_rows, cols = master.shape[1:]
    rows, width = tokens.shape
    stages = blocks // n_dp
    row = (rows, width)
    spectrum = (2 * rows, width)
    saved = [
        (row, LOW), (row, F32), (row, F32), (spectrum, LOW), (spectrum, LOW), (row, F32), (row, LOW), (row, F32), (row, LOW),
        ((4,) + row, LOW), ((4,) + row, LOW), ((4,) + row, LOW), ((8, width), F32), (row, F32),
    ]
    count = copy_count(n_dp, n_fsdp, stages, 1, n_fsdp, 3 * n_fsdp) + layers * (n_dp + n_fsdp - 2)
    any_space = pl.BlockSpec(memory_space=pl.ANY)
    scalar = pl.BlockSpec(memory_space=pltpu.SMEM)
    vmem = pl.BlockSpec(memory_space=pltpu.VMEM)
    return pl.pallas_call(
        functools.partial(forward_kernel, n_dp, n_fsdp, layers),
        name="forward",
        out_shape=[jax.ShapeDtypeStruct((stages, n_dp // 2, 2, width, width), LOW)]
        + [jax.ShapeDtypeStruct((layers,) + shape, kind) for shape, kind in saved]
        + [jax.ShapeDtypeStruct(row, LOW)],
        in_specs=[scalar] * 3 + [any_space, any_space, vmem, any_space, any_space],
        out_specs=[any_space] * (2 + len(saved)),
        scratch_shapes=[
            pltpu.VMEM(master.shape, F32),
            pltpu.VMEM((stages, 2, n_dp // 4, part_rows, cols), LOW),
            pltpu.VMEM((stages, 2, n_dp // 4, part_rows, cols), LOW),
        ]
        + plane_sum_shapes(n_dp, (stages,), part_rows, cols)
        + [
            pltpu.VMEM(row, LOW),
            pltpu.VMEM(row, F32),
            pltpu.VMEM(tables[0].shape, LOW),
            pltpu.VMEM(tables[1].shape, LOW),
            pltpu.VMEM((4, width, width), LOW),
            pltpu.VMEM((2, 3, width, width), LOW),
        ]
        + [pltpu.VMEM(shape, kind) for shape, kind in saved[:9]]
        + [pltpu.VMEM((2,) + row, LOW)] * 3
        + [
            pltpu.VMEM((layers, 8, width), F32),
            pltpu.VMEM((layers, n_fsdp, 8, width), F32),
            pltpu.VMEM((layers, n_dp, 8, width), F32),
            pltpu.VMEM((layers, 8, width), F32),
            pltpu.VMEM((layers, 8, width), F32),
            pltpu.SemaphoreType.DMA((count,)),
            pltpu.SemaphoreType.DMA((count,)),
            pltpu.SemaphoreType.DMA((stages + 8 + layers * 48,)),
        ],
        compiler_params=pltpu.CompilerParams(
            collective_id=0, has_side_effects=True, vmem_limit_bytes=VMEM_BYTES
        ),
    )(owner_slots, *scalars, master, tokens, gains, *tables)


class Scatter:
    def __init__(self, place, copies, stores, order, grads, landed, out_ref, acc, aside, from_a, from_b, credits, *sum_refs):
        self.place, self.copies, self.stores, self.order = place, copies, stores, order
        self.grads, self.landed, self.out_ref = grads, landed, out_ref
        self.acc, self.aside, self.from_a, self.from_b = acc, aside, from_a, from_b
        self.credits = credits
        self.slots, self.size = acc.shape[0], acc.shape[-2]
        self.rows = self.size // place.depth
        self.late = from_b.shape[-2]
        self.early = self.rows - self.late
        self.spots = place.up * place.across
        self.stages = len(order)
        self.sums = [
            [
                PlaneSum(
                    place, copies, acc.at[n % self.slots],
                    self.window(place.z_at(k), 0, self.early if k else self.rows),
                    self.early if k else self.rows,
                    *(ref.at[n % self.slots, k] for ref in sum_refs),
                )
                for k in range(place.depth)
            ]
            for n in range(self.stages)
        ]
        whole = pl.ds(0, self.rows)
        self.spreads = [PlaneSpread(place, copies, out_ref.at[s], whole) for s in order]
        self.over = [{} for _ in order]
        self.along_a = [{} for _ in order]
        self.along_b = [[] for _ in order]

    def window(self, z, first, count):
        return pl.ds(pl.multiple_of(z * self.rows + first, 16), count)

    def near(self):
        p = self.place
        peers = [(p.dp(x=p.x_at(k)), p.z) for k in range(1, p.across)]
        return peers + [(p.dp(y=p.y_at(m)), p.z) for m in range(1, p.up)]

    def column(self):
        p = self.place
        return [(p.d, p.z_at(k)) for k in range(1, p.depth)]

    def free(self, n, kind, peers):
        if n + self.slots < self.stages:
            for peer in peers:
                pl.semaphore_signal(
                    self.credits.at[kind, n], inc=1, device_id=peer, device_id_type=MESH
                )

    def claim(self, n, kind, peers):
        if n >= self.slots:
            pl.semaphore_wait(self.credits.at[kind, n - self.slots], len(peers))

    def grad(self, n, spot, core):
        return self.grads.at[self.place.n_dp * self.order[n] + 2 * spot + core]

    def offer(self, n, spot):
        p = self.place
        self.stores.settle(*[("outs", i) for i in range(4)])
        self.over[n][spot] = self.copies.to(
            self.grad(n, spot, 1 - p.core),
            self.landed.at[n * self.spots + spot],
            p.dp(core=1 - p.core),
            p.z,
        )
        self.over[n][spot].start()

    def sent(self, n):
        for one in self.sums[n]:
            one.drain()
        for copy in list(self.along_a[n].values()) + self.along_b[n]:
            copy.wait_send()

    def join(self, n, spot):
        p, slot = self.place, n % self.slots
        if n >= self.slots and spot == 0:
            self.sent(n - self.slots)
        target = self.acc.at[slot, spot // p.across, spot % p.across]
        own = self.copies.here(self.grad(n, spot, p.core), target)
        own.start()
        self.over[n][spot].wait_recv()
        aside = self.aside
        other = self.copies.here(self.landed.at[n * self.spots + spot], aside)
        other.start()
        own.wait()
        other.wait()
        add_into(target, [aside], self.size)

    def enter(self, n):
        p, slot = self.place, n % self.slots
        self.claim(n, 0, self.near())
        self.claim(n, 1, self.column())
        for k in range(1, p.depth):
            source = self.acc.at[slot, :, :, self.window(p.z_at(k), self.early, self.late), :]
            self.along_b[n].append(
                self.copies.to(source, self.from_b.at[slot, k - 1], p.d, p.z_at(k))
            )
        for copy in self.along_b[n]:
            copy.start()

    def push(self, n, k):
        p, slot = self.place, n % self.slots
        if k == 0:
            for copy in self.along_b[n]:
                copy.wait_recv()
            window = self.window(p.z, self.early, self.late)
            for y in range(p.up):
                for x in range(p.across):
                    terms = [self.from_b.at[slot, i, y, x] for i in range(p.depth - 1)]
                    add_into(self.acc.at[slot, y, x, window, :], terms, self.late)
        self.sums[n][k].start()

    def turn(self, n, k):
        self.sums[n][k].turn()

    def home(self, n, k):
        p, slot = self.place, n % self.slots
        self.sums[n][k].finish()
        if k > 0:
            source = self.acc.at[slot, p.y, p.x, self.window(p.z_at(k), 0, self.early), :]
            self.along_a[n][k] = self.copies.to(
                source, self.from_a.at[slot, k - 1], p.d, p.z_at(k)
            )
            self.along_a[n][k].start()

    def total(self, n):
        p, slot = self.place, n % self.slots
        self.free(n, 0, self.near())
        for copy in self.along_a[n].values():
            copy.wait_recv()
        terms = [self.from_a.at[slot, k - 1] for k in range(1, p.depth)]
        add_into(self.acc.at[slot, p.y, p.x, self.window(p.z, 0, self.early), :], terms, self.early)
        self.free(n, 1, self.column())
        total = self.acc.at[slot, p.y, p.x, self.window(p.z, 0, self.rows), :]
        own = self.out_ref.at[self.order[n], p.y * p.across + p.x, p.core]
        kept = self.copies.here(total, own)
        kept.start()
        kept.wait()
        self.spreads[n].start()

    def passing(self, n):
        self.spreads[n].forward()

    def close(self, n):
        self.spreads[n].finish()

    def done(self, n):
        self.spreads[n].arrived()

    def drain(self):
        for n in range(self.stages):
            for copy in self.over[n].values():
                copy.wait_send()
            if n + self.slots >= self.stages:
                self.sent(n)
            self.spreads[n].drain()


def grad_positions(layers):
    pairs = [4 + 2 * i for i in range(4)] + [5 + 2 * i for i in range(4)]
    one = np.array([12, 13, 14, 15] + pairs + [0, 1, 2, 3], np.int32)
    return jnp.asarray(np.concatenate([one + 16 * layer for layer in range(layers)]))


def backward_plan(layers, stages, depth):
    if (layers, stages, depth) == (2, 4, 4):
        return decode(BACKWARD_STEPS, BACKWARD_ORDER)
    plan = []
    for layer in reversed(range(layers)):
        plan += [("downs", layer)]
        for i, step in ((0, "gates"), (1, "gates"), (0, "inputs"), (1, "inputs")):
            plan += [(step, layer, i)]
        plan += [(step, layer, i) for i in (2, 3) for step in ("gates", "inputs")]
        plan += [(step, layer) for step in ("mix_a", "mix_b", "sum_turn", "front_a", "front_b")]
    spots = 8 * layers // stages
    plan += [("gain_turn", 0)] + [("offer", n, i) for n in range(stages) for i in range(spots)]
    for n in range(stages):
        plan += [("join", n, i) for i in range(spots)] + [("enter", n)]
        for k in list(range(1, depth)) + [0]:
            plan += [(step, n, k) for step in ("push", "turn", "home")]
        plan += [(step, n) for step in ("total", "passing", "close", "done")]
    return plan


def backward_kernel(n_dp, n_fsdp, layers, *refs):
    (
        flag_ref, count_ref, cotangent, w_ref, gains_ref, table_in, back_in,
        a_in, q_in, k_in, kh_in, vh_in, y_in, mixed_in, mid_in, b_in, g_in, u_in, h_in, total_in, state_in,
        red_ref, grad_out, gain_total, grads_ref, landed_ref,
        acc, from_x, from_y, last_y, last_x, from_a, from_b, aside,
        table, back, weights, tiles, outs, grad, sums, mid, q, y, low, b, mixed, dv, dq, dk,
        totals, part, by_z, by_d, mid_sum, total, send, recv, local, credits,
    ) = refs
    place = Place(n_dp, n_fsdp)
    copies = Copies(send, recv, local)
    stores = Stores(copies)
    rows, width = grad.shape
    valid = valid_rows(rows, count_ref[0])
    long = flag_ref[0]
    lone = lone_rows(rows, long)
    spans = span_scale(rows, flag_ref[0])
    waiting = {}

    def fetch(name, *pairs):
        waiting[name] = [copies.here(*pair) for pair in pairs]
        for copy in waiting[name]:
            copy.start()

    def fetched(*names):
        for name in names:
            for copy in waiting.pop(name):
                copy.wait()

    def fetch_mlp(layer, i):
        first, turn = 16 * layer + i, i % 2
        fetch(
            ("mlp", i),
            *[(w_ref.at[first + 4 * (j + 1)], weights.at[3 * turn + j]) for j in range(3)],
            *[(ref.at[layer, i], tiles.at[turn, j]) for j, ref in enumerate((g_in, u_in))],
        )

    hidden = (tiles.at[0, 2], tiles.at[1, 2], dv, dq)

    def fetch_layer(layer):
        fetch("b", (b_in.at[layer], b))
        fetch("hidden", *[(h_in.at[layer, i], ref) for i, ref in enumerate(hidden)])
        fetch_mlp(layer, 0)
        fetch_mlp(layer, 1)

    def store_grad(layer, slot, position):
        target = grads_ref.at[16 * layer + position]
        stores.out(("outs", slot), outs.at[slot], target)

    fetch("cotangent", (cotangent, grad))
    fetch_layer(layers - 1)
    fetch("tables", (table_in, table), (back_in, back))
    fetch("totals", (total_in, totals))
    place.greet_all()
    each = 16 // n_dp
    order = [layer * each + i for layer in reversed(range(layers)) for i in range(each)]
    scatter = Scatter(
        place, copies, stores, order, grads_ref, landed_ref, red_ref, acc, aside, from_a, from_b, credits, from_x, from_y, last_y, last_x
    )
    row_sums = [
        RowSum(place, copies, *(ref.at[i] for ref in (part, by_z, by_d, mid_sum, total)))
        for i in range(layers + 1)
    ]
    part[layers] = jnp.zeros(part.shape[1:], F32)

    def begin(layer):
        if layer == layers - 1:
            fetched("cotangent")
            grad[...] = grad[...] * valid
        low[...] = grad[...].astype(LOW)
        sums[...] = jnp.zeros_like(sums)
        fetch("mid", (mid_in.at[layer], mid))
        fetch("mix", (q_in.at[layer], q), (y_in.at[layer], y), (mixed_in.at[layer], mixed))
        fetched("b")

    def downs(layer):
        begin(layer)
        fetched("hidden")
        for i in range(4):
            stores.settle(("outs", i))

            def body(at, i=i):
                outs[i, at, :] = dot_tn(hidden[i][:, at], low[...]).astype(LOW)

            columns(width, body)
            store_grad(layer, i, i)

    def gates(layer, i):
        turn, slot = i % 2, 2 * (i % 2)
        fetched(("mlp", i))
        stores.settle(("outs", slot), ("outs", slot + 1))

        def body(at):
            dhidden = dot_nt(low[...], weights[3 * turn + 2, at, :])
            gate = tiles[turn, 0, :, at].astype(F32)
            up = tiles[turn, 1, :, at].astype(F32)
            sig = jax.nn.sigmoid(gate)
            dup = (dhidden * gate * sig).astype(LOW)
            dgate = (dhidden * up * sig * (1.0 + gate * (1.0 - sig))).astype(LOW)
            tiles[turn, 0, :, at] = dgate
            tiles[turn, 1, :, at] = dup
            outs[slot, :, at] = dot_tn(b[...], dgate).astype(LOW)
            outs[slot + 1, :, at] = dot_tn(b[...], dup).astype(LOW)

        columns(width, body)
        store_grad(layer, slot, 4 + 2 * i)
        store_grad(layer, slot + 1, 5 + 2 * i)

    def inputs(layer, i):
        turn = i % 2
        gate_part = dot_nt(tiles[turn, 0], weights[3 * turn])
        sums[...] += gate_part + dot_nt(tiles[turn, 1], weights[3 * turn + 1])
        if i < 2:
            fetch_mlp(layer, i + 2)
        elif i == 2:
            places = [(16 * layer + 3, 0), (16 * layer, 1), (16 * layer + 1, 2)]
            fetch("front", *[(w_ref.at[j], weights.at[to]) for j, to in places])
            fetch("kh", *[(kh_in.at[layer, pl.ds(rows * j, rows)], tiles.at[0, j]) for j in range(2)])
        else:
            fetch("key", (w_ref.at[16 * layer + 2], weights.at[3]))
            fetch("vh", *[(vh_in.at[layer, pl.ds(rows * j, rows)], tiles.at[1, j]) for j in range(2)])
            fetch("a", (a_in.at[layer], b))

    def mix_a(layer):
        if layer == layers - 1:
            fetched("tables", "totals")
        fetched("mid")
        normed, rstd = normalize(mid[...])
        db = sums[...]
        part[layers, 2 * layer + 1 : 2 * layer + 2, :] = jnp.sum(db * normed, 0, keepdims=True)
        gain = gains_ref[2 * layer + 1 : 2 * layer + 2, :]
        grad[...] += norm_back(db * gain, normed, rstd)
        low[...] = grad[...].astype(LOW)
        fetch("k", (k_in.at[layer], mid))
        norm, _ = filter_norm_of(totals.at[layer])
        scale_row = spans / norm
        sums[0:1, :] = scale_row
        part[layer] = jnp.zeros(part.shape[1:], F32)
        fetched("mix", "front", "kh", "vh")

        def through(at):
            dmixed = dot_nt(low[...], weights[0, at, :])
            dq[:, at] = (dmixed * y[:, at] * sums[0:1, at]).astype(LOW)
            dy = dmixed * q[:, at]
            part[layer, 0:1, at] = jnp.sum(dy * y[:, at], 0, keepdims=True) * spans
            q[:, at] = dy

        columns(width, through)
        row_sums[layer].start()

    def mix_b(layer):
        def body(at):
            dh = dot(table[long], q[:, at].astype(LOW))
            dr, di = dh[:rows], dh[rows:]

            def against(turn):
                other_r = tiles[turn, 0, :, at].astype(F32)
                other_i = tiles[turn, 1, :, at].astype(F32)
                cross = di * other_i
                real = dr * other_r + jnp.where(lone, 0.0, cross)
                imag = jnp.where(lone, cross, di * other_r - dr * other_i)
                return dot(back[long, :, :rows], real.astype(LOW)) + dot(
                    back[long, :, rows:], imag.astype(LOW)
                )

            y[:, at] = against(1)
            dv[:, at] = (against(0) * sums[0:1, at] * valid).astype(LOW)

        columns(width, body)
        fetch("state", (state_in.at[layer], q))

    def sum_turn(layer):
        row_sums[layer].turn()

    def gain_turn(_):
        row_sums[layers].turn()

    def front_a(layer):
        fetched("a", "key")
        stores.settle(*[("outs", i) for i in range(4)])

        def body(at):
            outs[3, at, :] = dot_tn(mixed[:, at], low[...]).astype(LOW)
            outs[0, :, at] = dot_tn(b[...], dv[:, at]).astype(LOW)
            outs[1, :, at] = dot_tn(b[...], dq[:, at]).astype(LOW)

        columns(width, body)
        sums[...] = dot_nt(dv[...], weights[1]) + dot_nt(dq[...], weights[2])

    def front_b(layer):
        fetched("k")
        row_sums[layer].finish()
        norm, live = filter_norm_of(totals.at[layer])
        square = -total[layer, 0:1, :] / (norm * norm) / (2.0 * norm * live)
        dk[...] = ((y[...] * (spans / norm) + 2.0 * mid[...] * square) * valid).astype(LOW)

        def keys(at):
            outs[2, :, at] = dot_tn(b[...], dk[:, at]).astype(LOW)

        columns(width, keys)
        for j in range(4):
            store_grad(layer, j, 12 + j)
        sums[...] += dot_nt(dk[...], weights[3])
        if layer > 0:
            fetch_layer(layer - 1)
        fetched("state")
        da = sums[...]
        normed, rstd = normalize(q[...])
        part[layers, 2 * layer : 2 * layer + 1, :] = jnp.sum(da * normed, 0, keepdims=True)
        gain = gains_ref[2 * layer : 2 * layer + 1, :]
        grad[...] += norm_back(da * gain, normed, rstd)
        if layer == 0:
            stores.out("grad", grad, grad_out)
            row_sums[layers].start()

    compute = types.SimpleNamespace(
        downs=downs, gates=gates, inputs=inputs, mix_a=mix_a, mix_b=mix_b, front_a=front_a, front_b=front_b,
        sum_turn=sum_turn, gain_turn=gain_turn,
    )
    run_plan(backward_plan(layers, scatter.stages, n_fsdp), scatter, compute)
    row_sums[layers].finish()
    gain_total[...] = total[layers]
    scatter.drain()
    for one in row_sums:
        one.drain()
    stores.settle()


def backward(n_dp, n_fsdp, scalars, cotangent, weights, gains, tables, saved):
    width = weights.shape[-1]
    weights = weights.reshape(-1, width, width)
    blocks = weights.shape[0]
    layers = blocks // 16
    rows = cotangent.shape[0]
    stages = blocks // n_dp
    spots = n_dp // 2
    slots = 2 if n_dp == 8 else 1
    part_rows = width // n_fsdp
    row = (rows, width)
    late = max(16, part_rows // 6 // 16 * 16)
    spread_count = spots + 2 * (n_fsdp - 1)
    count = copy_count(n_dp, n_fsdp, stages, n_fsdp, 1, spread_count)
    count += (layers + 1) * (n_dp + n_fsdp - 2)
    any_space = pl.BlockSpec(memory_space=pl.ANY)
    scalar = pl.BlockSpec(memory_space=pltpu.SMEM)
    vmem = pl.BlockSpec(memory_space=pltpu.VMEM)
    return pl.pallas_call(
        functools.partial(backward_kernel, n_dp, n_fsdp, layers),
        name="backward",
        out_shape=[
            jax.ShapeDtypeStruct((stages, n_dp // 2, 2, part_rows, width), LOW),
            jax.ShapeDtypeStruct(row, F32),
            jax.ShapeDtypeStruct((8, width), F32),
            jax.ShapeDtypeStruct((blocks, width, width), LOW),
            jax.ShapeDtypeStruct((blocks // 2, width, width), LOW),
        ],
        in_specs=[scalar, scalar, any_space, any_space, vmem] + [any_space] * (2 + len(saved)),
        out_specs=[any_space, any_space, vmem, any_space, any_space],
        scratch_shapes=[pltpu.VMEM((slots, 2, n_dp // 4, width, width), LOW)]
        + plane_sum_shapes(n_dp, (slots, n_fsdp), part_rows, width)
        + [
            pltpu.VMEM((slots, n_fsdp - 1, part_rows - late, width), LOW),
            pltpu.VMEM((slots, n_fsdp - 1, 2, n_dp // 4, late, width), LOW),
            pltpu.VMEM((width, width), LOW),
            pltpu.VMEM(tables[0].shape, LOW),
            pltpu.VMEM(tables[1].shape, LOW),
            pltpu.VMEM((6, width, width), LOW),
            pltpu.VMEM((2, 3) + row, LOW),
            pltpu.VMEM((4, width, width), LOW),
        ]
        + [pltpu.VMEM(row, F32)] * 5
        + [pltpu.VMEM(row, LOW)] * 6
        + [
            pltpu.VMEM((layers, 8, width), F32),
            pltpu.VMEM((layers + 1, 8, width), F32),
            pltpu.VMEM((layers + 1, n_fsdp, 8, width), F32),
            pltpu.VMEM((layers + 1, n_dp, 8, width), F32),
            pltpu.VMEM((layers + 1, 8, width), F32),
            pltpu.VMEM((layers + 1, 8, width), F32),
            pltpu.SemaphoreType.DMA((count,)),
            pltpu.SemaphoreType.DMA((count,)),
            pltpu.SemaphoreType.DMA((stages * (2 * spots + 1) + layers * 64 + 16,)),
            pltpu.SemaphoreType.REGULAR((2, stages)),
        ],
        compiler_params=pltpu.CompilerParams(
            collective_id=1, has_side_effects=True, vmem_limit_bytes=VMEM_BYTES
        ),
    )(*scalars, cotangent, weights, gains, *tables, *saved)


def call(kernel, name, grid, scalars, args, specs, outs, out_specs, scratch=()):
    return pl.pallas_call(
        kernel,
        name=name,
        out_shape=outs,
        grid_spec=pltpu.PrefetchScalarGridSpec(
            num_scalar_prefetch=len(scalars),
            grid=(grid,),
            in_specs=specs,
            out_specs=out_specs,
            scratch_shapes=scratch,
        ),
        compiler_params=pltpu.CompilerParams(vmem_limit_bytes=VMEM_BYTES),
    )(*scalars, *args)


def adam_step(grad, first, second, weight, rate, decay):
    first_out = 0.5 * first + 0.5 * grad
    second_out = 0.5 * second + 0.5 * grad * grad
    fix = 1.0 / (1.0 - 0.5**STEP)
    weight_out = weight - rate * (
        first_out * fix / (jnp.sqrt(second_out * fix) + ADAM_EPS) + decay * weight
    )
    return (first_out, second_out, weight_out)


def adam_kernel(
    block, used, grad_ref, master_ref, first_ref, second_ref, first_out, second_out, master_out
):
    taken = used[pl.program_id(0)] == 1
    first, second, master = first_ref[...], second_ref[...], master_ref[...]
    new = adam_step(grad_ref[...].astype(F32), first, second, master, 0.03, 0.01)
    first_out[...] = jnp.where(taken, new[0], first)
    second_out[...] = jnp.where(taken, new[1], second)
    master_out[...] = jnp.where(taken, new[2], master)


def adam_blocks(block, used, grads, master, first, second):
    shape = (1,) + master.shape[1:]
    own = pl.BlockSpec(shape, lambda i, block, used: (i, 0, 0))
    picked = pl.BlockSpec(shape, lambda i, block, used: (block[i], 0, 0))
    return call(
        adam_kernel,
        "adam",
        master.shape[0],
        (block, used),
        (grads, master, first, second),
        [picked, own, own, own],
        [jax.ShapeDtypeStruct(master.shape, F32)] * 3,
        [own] * 3,
    )


def on_device(
    n_dp,
    n_fsdp,
    tokens,
    cotangent,
    row_counts,
    bucket_flags,
    owner_slots,
    master,
    first_moment,
    second_moment,
    gains,
    gain_first,
    gain_second,
):
    rows = tokens.shape[0]
    slot_cap = master.shape[0]
    layers = owner_slots.shape[0] // 16
    tables = transform_tables(rows)
    scalars = (bucket_flags, row_counts)
    weights, *saved, activations = forward(
        n_dp, n_fsdp, scalars, owner_slots, master, tokens, gains, tables
    )
    summed, grad, gain_sums, _, _ = backward(
        n_dp, n_fsdp, scalars, cotangent, weights, gains, tables, saved
    )
    gains_total = gain_sums[: 2 * layers]
    my_slots = lax.axis_index("dp") * slot_cap + jnp.arange(slot_cap, dtype=jnp.int32)
    hits = owner_slots[None, :] == my_slots[:, None]
    used = jnp.any(hits, 1).astype(jnp.int32)
    block = jnp.sum(jnp.where(hits, grad_positions(layers)[None, :], 0), 1)
    first_out, second_out, master_out = adam_blocks(
        block, used, summed.reshape(-1, *master.shape[1:]), master, first_moment, second_moment
    )
    gain_m, gain_v, gain_w = adam_step(gains_total, gain_first, gain_second, gains, 0.2, 0.0)
    return (activations, grad, first_out, second_out, master_out, gain_m, gain_v, gain_w)


def solution(mesh):
    rows = P(("dp", "fsdp"), None)
    blocks = P("dp", "fsdp", None)
    flat = P(("dp", "fsdp"))
    return jax.shard_map(
        functools.partial(on_device, mesh.shape["dp"], mesh.shape["fsdp"]),
        mesh=mesh,
        in_specs=(rows, rows, flat, flat, P(), blocks, blocks, blocks, P(), P(), P()),
        out_specs=(rows, rows, blocks, blocks, blocks, P(), P(), P()),
        check_vma=False,
    )
```
